32 devices in a mesh: dp: 2 (over x), context: 16 (over z, y, core).
Axes of the slice: x: 2, y: 2, z: 4, core: 2. Of those that a mesh axis runs over, the one named last changes fastest.
Arguments:
- queries: bfloat16 [2, 2048, 2048], P('dp', 'context'), may hold values from -6 to 6
- key_rows: bfloat16 [2, 2048, 2048], P('dp', 'context'), may hold values from -6 to 6
- value_rows: bfloat16 [2, 2048, 2048], P('dp', 'context'), may hold values from -6 to 6
- out_grad: bfloat16 [2, 2048, 2048], P('dp', 'context'), may hold values from -6 to 6
- feature_maps: bfloat16 [16, 128, 128], replicated, may hold values from -0.5 to 0.5
Outputs:
- query_grad: bfloat16 [2, 2048, 2048], P('dp', 'context')
- key_grad: bfloat16 [2, 2048, 2048], P('dp', 'context')
- value_grad: bfloat16 [2, 2048, 2048], P('dp', 'context')
- maps_grad: float32 [2048, 128], P(('dp', 'context'))
The draws below stay inside these ranges and needn't reach their ends.
All inputs are finite; a program needn't handle non-finite values.
Results may differ from the reference program's by a relative error of at most 0.0085.
Values sent between devices are 32-bit elements; how exact they have to be, the bound alone decides.
No kernel may reach another device: no remote copies, remote signals or barrier semaphores. Data moves between devices by JAX's collectives and lax.ppermute only.
A program may use at most 64 MiB of HBM per device.

```python
import math
import jax
import jax.numpy as jnp
from jax import lax

H = 16
DH = 128
TOK_DEV = 128
LENGTH = 2048
BATCH = 2


def block_scale(key, dims, cuts, low, high):
    level, own = 1.0, jax.random.fold_in(key, 6)
    for position, parts in cuts:
        draws = jnp.exp(jax.random.uniform(jax.random.fold_in(own, position), (parts,), jnp.float32, low / len(cuts), high / len(cuts)))
        level = level * jnp.repeat(draws, dims[position] // parts).reshape([-1 if axis == position else 1 for axis in range(len(dims))])
    return level


def scatter_about(own_key, extent, scale, most, split=(), held_as=jnp.bfloat16):
    factor_of = block_scale(own_key, extent, split, -0.22, 0.18) if split else 1.0
    drawn = jax.random.normal(own_key, extent, jnp.float32) * scale * factor_of
    return jnp.minimum(jnp.maximum(drawn, -most), most).astype(held_as)


def setup_inputs(seed: int = 0) -> dict:
    splits = jax.random.split(jax.random.key(seed), 6)
    return {
        "queries": scatter_about(splits[0], (BATCH, LENGTH, H * DH), 1.0, 6.0, ((0, 2), (1, 16))),
        "key_rows": scatter_about(splits[1], (BATCH, LENGTH, H * DH), 1.0, 6.0, ((0, 2), (1, 16))),
        "value_rows": scatter_about(splits[2], (BATCH, LENGTH, H * DH), 1.0, 6.0, ((0, 2), (1, 16))),
        "out_grad": scatter_about(splits[3], (BATCH, LENGTH, H * DH), 1.0, 6.0, ((0, 2), (1, 16))),
        "feature_maps": scatter_about(splits[4], (H, DH, DH), DH ** -0.5, 0.5),
    }


HIGHEST = lax.Precision.HIGHEST

def one_sequence(queries, key_rows, value_rows, out_grad, feature_maps):
    blocks = LENGTH // TOK_DEV
    factor = 1.0 / math.sqrt(DH * LENGTH)

    def split_heads(rows):
        return rows.reshape(blocks, TOK_DEV, H, DH).astype(jnp.float32)
    maps_wide = feature_maps.astype(jnp.float32)
    query_heads = split_heads(queries)
    key_heads = split_heads(key_rows)
    value_heads = split_heads(value_rows)
    grad_heads = split_heads(out_grad)
    feat_query = jnp.einsum('nthd,hde->nhte', query_heads, maps_wide).astype(jnp.bfloat16).astype(jnp.float32)
    feat_key = jnp.einsum('nthd,hde->nhte', key_heads, maps_wide).astype(jnp.bfloat16).astype(jnp.float32)
    kv_blocks = jnp.einsum('nhsd,nshe->nhde', feat_key, value_heads)
    ga_blocks = jnp.einsum('nhtd,nthe->nhde', feat_query, grad_heads)

    def forward(running, block_term):
        return (running + block_term, running)
    empty_state = jnp.zeros((H, DH, DH), jnp.float32)
    _, prefix = lax.scan(forward, empty_state, kv_blocks)
    _, suffix = lax.scan(forward, empty_state, ga_blocks, reverse=True)
    causal = jnp.arange(TOK_DEV)[:, None] >= jnp.arange(TOK_DEV)[None, :]
    score_ab = jnp.where(causal, jnp.einsum('nhtd,nhsd->nhts', feat_query, feat_key), 0.0)
    score_ab = score_ab.astype(jnp.bfloat16).astype(jnp.float32)
    score_gv = jnp.where(causal, jnp.einsum('nthe,nshe->nhts', grad_heads, value_heads), 0.0)
    score_gv = score_gv.astype(jnp.bfloat16).astype(jnp.float32)
    feat_qgrad = factor * (jnp.einsum('nhts,nhsd->nhtd', score_gv, feat_key) + jnp.einsum('nthe,nhde->nhtd', grad_heads, prefix, precision=HIGHEST))
    feat_qgrad = feat_qgrad.astype(jnp.bfloat16).astype(jnp.float32)
    feat_kgrad = factor * (jnp.einsum('nhts,nhtd->nhsd', score_gv, feat_query) + jnp.einsum('nshe,nhde->nhsd', value_heads, suffix, precision=HIGHEST))
    feat_kgrad = feat_kgrad.astype(jnp.bfloat16).astype(jnp.float32)
    value_grad = factor * (jnp.einsum('nhts,nthe->nshe', score_ab, grad_heads) + jnp.einsum('nhsd,nhde->nshe', feat_key, suffix, precision=HIGHEST))
    query_grad = jnp.einsum('nhte,hde->nthd', feat_qgrad, maps_wide)
    key_grad = jnp.einsum('nhse,hde->nshd', feat_kgrad, maps_wide)
    maps_term = jnp.einsum('nthd,nhte->hde', query_heads, feat_qgrad) + jnp.einsum('nshd,nhse->hde', key_heads, feat_kgrad)
    return (query_grad.reshape(LENGTH, H * DH).astype(jnp.bfloat16), key_grad.reshape(LENGTH, H * DH).astype(jnp.bfloat16), value_grad.reshape(LENGTH, H * DH).astype(jnp.bfloat16), maps_term)

def reference(queries, key_rows, value_rows, out_grad, feature_maps):

    def per_sequence(inputs):
        return one_sequence(inputs[0], inputs[1], inputs[2], inputs[3], feature_maps)
    query_grad, key_grad, value_grad, maps_terms = lax.map(per_sequence, (queries, key_rows, value_rows, out_grad))
    maps_grad = lax.optimization_barrier(jnp.sum(maps_terms, axis=0)) * (1.0 / math.sqrt(BATCH * LENGTH))
    return (query_grad, key_grad, value_grad, maps_grad.reshape(H * DH, DH))
```

```python
import math

import jax
import jax.numpy as jnp
from jax import lax
from jax.sharding import PartitionSpec as P


def swap_core(state, ranks):
    return lax.ppermute(state, "context", [(i, i ^ 1) for i in range(ranks)])


def swap_chip(state, ranks):
    return lax.ppermute(state, "context", [(i, i ^ 2) for i in range(ranks)])


def shift_groups(state, ranks, hop):
    steps = []
    for i in range(ranks):
        target = i + 4 * hop * (1 if i % 2 else -1)
        if 0 <= target < ranks:
            steps.append((i, target))
    return lax.ppermute(state, "context", steps)


def exchange_states(kv_local, grad_local):
    ranks = lax.axis_size("context")
    index = lax.axis_index("context")
    core, chip = index % 2, (index // 2) % 2
    groups = ranks // 4
    odd = core == 1
    heads = kv_local.shape[0]
    half = heads // 2
    sent = jnp.where(odd, grad_local, kv_local)
    kept = jnp.where(odd, kv_local, grad_local)
    from_core = swap_core(sent, ranks)
    total = kept + from_core
    mine = lax.dynamic_slice_in_dim(total, chip * half, half, 0)
    other = lax.dynamic_slice_in_dim(total, (1 - chip) * half, half, 0)
    from_chip = swap_chip(other, ranks)
    group = mine + from_chip
    last = chip == core
    before = jnp.zeros_like(group)
    window = group
    hop = 1
    while hop < groups:
        arrived = shift_groups(window, ranks, hop)
        before = before + arrived
        window = window + arrived
        hop *= 2
    own_half = before + jnp.where(last, from_chip, 0.0)
    mate_half = before + jnp.where(last, 0.0, mine)
    got_half = swap_chip(mate_half, ranks)
    first = chip == 0
    whole = jnp.concatenate(
        [jnp.where(first, own_half, got_half), jnp.where(first, got_half, own_half)], axis=0
    )
    crossed = swap_core(whole, ranks)
    finished = whole + from_core
    prefix = jnp.where(odd, finished, crossed)
    suffix = jnp.where(odd, crossed, finished)
    return prefix, suffix


def scatter_sum(terms):
    ranks = lax.axis_size("context")
    copies = lax.axis_size("dp")
    index = lax.axis_index("context")
    replica = lax.axis_index("dp")
    core, chip, group = index % 2, (index // 2) % 2, index // 4
    groups = ranks // 4
    width = terms.shape[-1]
    parts = terms.reshape(copies * groups * 2, 2, -1, width)
    sent = lax.dynamic_index_in_dim(parts, 1 - core, 1, keepdims=False)
    kept = lax.dynamic_index_in_dim(parts, core, 1, keepdims=False)
    total = (kept + swap_core(sent, ranks)).reshape(copies, groups, 2, -1, width)

    def plane_part(target_replica, target_chip):
        some = lax.dynamic_index_in_dim(total, target_replica, 0, keepdims=False)
        return lax.dynamic_index_in_dim(some, target_chip, 1, keepdims=False)

    plane = plane_part(replica, chip)
    for turn in range(copies):
        for flip in range(2):
            if turn == 0 and flip == 0:
                continue
            steps = [
                (r * ranks + i, ((r + turn) % copies) * ranks + (i ^ (2 * flip)))
                for r in range(copies)
                for i in range(ranks)
            ]
            sent = plane_part((replica + turn) % copies, (chip + flip) % 2)
            plane = plane + lax.ppermute(sent, ("dp", "context"), steps)
    result = lax.dynamic_index_in_dim(plane, group, 0, keepdims=False)
    for turn in range(1, groups):
        steps = [(i, (i + 4 * turn) % ranks) for i in range(ranks)]
        sent = lax.dynamic_index_in_dim(plane, (group + turn) % groups, 0, keepdims=False)
        result = result + lax.ppermute(sent, "context", steps)
    return result


def split_state(state):
    upper = state.astype(jnp.bfloat16)
    lower = (state - upper.astype(jnp.float32)).astype(jnp.bfloat16)
    return (upper, lower)


def state_product(form, rows, parts):
    return jnp.einsum(form, rows, parts[0], preferred_element_type=jnp.float32) + jnp.einsum(
        form, rows, parts[1], preferred_element_type=jnp.float32
    )


def per_device(queries, key_rows, value_rows, out_grad, feature_maps):
    tokens = queries.shape[1]
    head_count = feature_maps.shape[0]
    head_width = feature_maps.shape[1]
    ranks = lax.axis_size("context")
    length = tokens * ranks
    factor = 1.0 / math.sqrt(head_width * length)
    norm_factor = 1.0 / math.sqrt(lax.axis_size("dp") * length)
    query_heads = queries.reshape(tokens, head_count, head_width)
    key_heads = key_rows.reshape(tokens, head_count, head_width)
    value_heads = value_rows.reshape(tokens, head_count, head_width)
    grad_heads = out_grad.reshape(tokens, head_count, head_width)
    feat_query = jnp.einsum(
        "thd,hde->hte", query_heads, feature_maps, preferred_element_type=jnp.float32
    ).astype(jnp.bfloat16)
    feat_key = jnp.einsum(
        "thd,hde->hte", key_heads, feature_maps, preferred_element_type=jnp.float32
    ).astype(jnp.bfloat16)
    kv_local = jnp.einsum("hsd,she->hde", feat_key, value_heads, preferred_element_type=jnp.float32)
    grad_local = jnp.einsum(
        "htd,the->hde", feat_query, grad_heads, preferred_element_type=jnp.float32
    )
    state_rows = head_count * head_width
    before_mine, after_mine = exchange_states(kv_local, grad_local)
    prefix_parts = split_state(before_mine.reshape(head_count, head_width, head_width))
    suffix_parts = split_state(after_mine.reshape(head_count, head_width, head_width))
    causal = jnp.arange(tokens)[:, None] >= jnp.arange(tokens)[None, :]
    score_ab = jnp.where(
        causal,
        jnp.einsum("htd,hsd->hts", feat_query, feat_key, preferred_element_type=jnp.float32),
        0.0,
    ).astype(jnp.bfloat16)
    score_gv = jnp.where(
        causal,
        jnp.einsum("the,she->hts", grad_heads, value_heads, preferred_element_type=jnp.float32),
        0.0,
    ).astype(jnp.bfloat16)
    feat_qgrad = factor * (
        jnp.einsum("hts,hsd->htd", score_gv, feat_key, preferred_element_type=jnp.float32)
        + state_product("the,hde->htd", grad_heads, prefix_parts)
    )
    feat_qgrad = feat_qgrad.astype(jnp.bfloat16)
    query_grad = jnp.einsum(
        "hte,hde->thd", feat_qgrad, feature_maps, preferred_element_type=jnp.float32
    )
    query_grad = query_grad.astype(jnp.bfloat16).reshape(1, tokens, head_count * head_width)
    query_term = jnp.einsum(
        "thd,hte->hde", query_heads, feat_qgrad, preferred_element_type=jnp.float32
    )
    feat_kgrad = factor * (
        jnp.einsum("hts,htd->hsd", score_gv, feat_query, preferred_element_type=jnp.float32)
        + state_product("she,hde->hsd", value_heads, suffix_parts)
    )
    feat_kgrad = feat_kgrad.astype(jnp.bfloat16)
    value_grad = factor * (
        jnp.einsum("hts,the->she", score_ab, grad_heads, preferred_element_type=jnp.float32)
        + state_product("hsd,hde->she", feat_key, suffix_parts)
    )
    value_grad = value_grad.astype(jnp.bfloat16).reshape(1, tokens, head_count * head_width)
    key_grad = jnp.einsum(
        "hse,hde->shd", feat_kgrad, feature_maps, preferred_element_type=jnp.float32
    )
    key_grad = key_grad.astype(jnp.bfloat16).reshape(1, tokens, head_count * head_width)
    key_term = jnp.einsum("shd,hse->hde", key_heads, feat_kgrad, preferred_element_type=jnp.float32)
    both_terms = (query_term + key_term).reshape(state_rows, head_width)
    maps_grad = scatter_sum(both_terms) * norm_factor
    return (query_grad, key_grad, value_grad, maps_grad)


def solution(mesh):
    in_specs = (
        P("dp", "context", None),
        P("dp", "context", None),
        P("dp", "context", None),
        P("dp", "context", None),
        P(),
    )
    out_specs = (
        P("dp", "context", None),
        P("dp", "context", None),
        P("dp", "context", None),
        P(("dp", "context"), None),
    )
    return jax.shard_map(
        per_device, mesh=mesh, in_specs=in_specs, out_specs=out_specs, check_vma=False
    )
```

```python
import functools
import math

import jax
import jax.numpy as jnp
from jax import lax
from jax.experimental import pallas as pl
from jax.experimental.pallas import tpu as pltpu
from jax.sharding import PartitionSpec as P

F32 = jnp.float32
BF16 = jnp.bfloat16
VMEM_LIMIT = 32 * 1024 * 1024


class Plan:
    def __init__(self, heads, width, tokens, ranks, copies):
        self.heads, self.width, self.tokens = heads, width, tokens
        self.ranks, self.copies = ranks, copies
        self.groups = ranks // 4
        per_copy = heads // copies if heads % copies == 0 else 0
        self.chunks = 2 if per_copy and per_copy % 2 == 0 and self.groups % 2 == 0 else 1
        self.in_chunk = heads // self.chunks
        self.half = self.in_chunk // 2
        self.run = per_copy // self.chunks if self.chunks > 1 else self.in_chunk
        self.stride = per_copy if self.chunks > 1 else 0
        self.factor = 1.0 / math.sqrt(width * tokens * ranks)
        self.norm = 1.0 / math.sqrt(copies * tokens * ranks)

    def head(self, chunk, place):
        return (place // self.run) * self.stride + chunk * self.run + place % self.run


def device_place():
    index = lax.axis_index("context")
    return index % 2, (index // 2) % 2, index // 4


def columns(ref, head, width):
    start = head * width
    if not isinstance(start, int):
        start = pl.multiple_of(start, width)
    return ref[:, pl.ds(start, width)]


def dot(left, right, left_dim=1, right_dim=0):
    return lax.dot_general(
        left, right, (((left_dim,), (right_dim,)), ((), ())), preferred_element_type=F32
    )


def state_dot(rows, state, state_dim):
    upper = state.astype(BF16)
    lower = (state - upper.astype(F32)).astype(BF16)
    return dot(rows, upper, 1, state_dim) + dot(rows, lower, 1, state_dim)


def by_core(core, zero, one):
    pl.when(core == 0)(zero)
    pl.when(core == 1)(one)


def call(body, operands, shapes, flops):
    moved = sum(x.size * x.dtype.itemsize for x in list(operands) + list(shapes))
    return pl.pallas_call(
        body,
        out_shape=shapes,
        in_specs=[pl.BlockSpec(memory_space=pltpu.VMEM)] * len(operands),
        out_specs=[pl.BlockSpec(memory_space=pltpu.VMEM)] * len(shapes),
        compiler_params=pltpu.CompilerParams(vmem_limit_bytes=VMEM_LIMIT),
        cost_estimate=pl.CostEstimate(flops=flops, bytes_accessed=moved, transcendentals=0),
    )(*operands)


def matmuls(plan, count):
    return 2 * count * plan.tokens * plan.width * plan.width


def states_kernel(plan, own, q_ref, k_ref, v_ref, g_ref, maps_ref, *out_refs):
    core, chip, _ = device_place()

    def fill(rows_ref, with_ref):
        for chunk in range(plan.chunks):
            for part in range(2):
                first = jnp.where(chip == part, 0, plan.half)
                for i in range(plan.half):
                    head = plan.head(chunk, first + i)
                    feat = dot(columns(rows_ref, head, plan.width), maps_ref[head]).astype(BF16)
                    out_refs[2 * chunk + part][i] = dot(
                        feat, columns(with_ref, head, plan.width), 0, 0
                    )

    keys = lambda: fill(k_ref, v_ref)
    queries = lambda: fill(q_ref, g_ref)
    if own:
        by_core(core, queries, keys)
    else:
        by_core(core, keys, queries)


def states(plan, own, rows, maps):
    shape = jax.ShapeDtypeStruct((plan.half, plan.width, plan.width), F32)
    outs = call(
        functools.partial(states_kernel, plan, own),
        (*rows, maps),
        [shape] * (2 * plan.chunks),
        matmuls(plan, 2 * plan.heads),
    )
    return [outs[2 * chunk : 2 * chunk + 2] for chunk in range(plan.chunks)]


def inner_kernel(plan, q_ref, k_ref, v_ref, g_ref, maps_ref, *out_refs):
    tokens, width = plan.tokens, plan.width
    row = lax.broadcasted_iota(jnp.int32, (tokens, tokens), 0)
    column = lax.broadcasted_iota(jnp.int32, (tokens, tokens), 1)
    causal = row >= column
    for chunk in range(plan.chunks):
        feat_ref, da_ref, db_ref, dv_ref = out_refs[4 * chunk : 4 * chunk + 4]
        for place in range(plan.in_chunk):
            head = plan.head(chunk, place)
            grads, values = columns(g_ref, head, width), columns(v_ref, head, width)
            feat_query = dot(columns(q_ref, head, width), maps_ref[head]).astype(BF16)
            feat_key = dot(columns(k_ref, head, width), maps_ref[head]).astype(BF16)
            score_gv = jnp.where(causal, dot(grads, values, 1, 1), 0.0).astype(BF16)
            score_ab = jnp.where(causal, dot(feat_query, feat_key, 1, 1), 0.0).astype(BF16)
            feat_ref[place] = feat_key
            da_ref[place] = dot(score_gv, feat_key)
            db_ref[place] = dot(score_gv, feat_query, 0, 0)
            dv_ref[place] = dot(score_ab, grads, 0, 0)


def inner(plan, rows, maps):
    wide = jax.ShapeDtypeStruct((plan.in_chunk, plan.tokens, plan.width), F32)
    narrow = jax.ShapeDtypeStruct((plan.in_chunk, plan.tokens, plan.width), BF16)
    outs = call(
        functools.partial(inner_kernel, plan),
        (*rows, maps),
        [narrow, wide, wide, wide] * plan.chunks,
        matmuls(plan, 7 * plan.heads),
    )
    return [outs[4 * chunk : 4 * chunk + 4] for chunk in range(plan.chunks)]


def query_side(plan, head, place, state, q_ref, g_ref, da_ref):
    total = da_ref[place] + state_dot(columns(g_ref, head, plan.width), state, 1)
    grad = (plan.factor * total).astype(BF16)
    return grad, dot(columns(q_ref, head, plan.width), grad, 0, 0)


def key_side(plan, head, place, state, k_ref, v_ref, feat_ref, db_ref, dv_ref):
    total = db_ref[place] + state_dot(columns(v_ref, head, plan.width), state, 1)
    grad = (plan.factor * total).astype(BF16)
    values = plan.factor * (dv_ref[place] + state_dot(feat_ref[place], state, 0))
    return grad, dot(columns(k_ref, head, plan.width), grad, 0, 0), values.astype(BF16)


def outer_kernel(plan, own, chunk, *refs):
    core, chip, _ = device_place()
    q_ref, k_ref, v_ref, g_ref, feat_ref, da_ref, db_ref, dv_ref, keep_ref, give_ref = refs[:10]
    extra, (grad_ref, term_ref, value_ref) = refs[10:-3], refs[-3:]

    def each(use):
        for part, state_ref in enumerate((keep_ref, give_ref)):
            first = jnp.where(chip == part, 0, plan.half)
            for i in range(plan.half):
                place = first + i
                state = state_ref[i]
                if own:
                    state = state + extra[part][i]
                use(plan.head(chunk, place), place, state)

    def put(place, grad, term):
        grad_ref[place] = grad
        term_ref[place] = term if own else term + extra[0][place]

    def use_queries(head, place, state):
        put(place, *query_side(plan, head, place, state, q_ref, g_ref, da_ref))

    def use_keys(head, place, state):
        grad, term, values = key_side(
            plan, head, place, state, k_ref, v_ref, feat_ref, db_ref, dv_ref
        )
        put(place, grad, term)
        value_ref[place] = values

    queries, keys = lambda: each(use_queries), lambda: each(use_keys)
    if own:
        by_core(core, keys, queries)
    else:
        by_core(core, queries, keys)


def outer(plan, own, chunk, rows, stash, keep, give, extra):
    shape = (plan.in_chunk, plan.tokens, plan.width)
    square = (plan.in_chunk, plan.width, plan.width)
    return call(
        functools.partial(outer_kernel, plan, own, chunk),
        (*rows, *stash, keep, give, *extra),
        [
            jax.ShapeDtypeStruct(shape, BF16),
            jax.ShapeDtypeStruct(square, F32),
            jax.ShapeDtypeStruct(shape, BF16),
        ],
        matmuls(plan, 5 * plan.in_chunk),
    )


def rows_kernel(plan, maps_ref, *refs):
    core, _, _ = device_place()
    qg_ref, kg_ref, vg_ref = refs[-3:]

    def fill(order):
        for chunk in range(plan.chunks):
            own_grad, own_value, far_grad, far_value = refs[4 * chunk : 4 * chunk + 4]
            da_ref, db_ref, dv_ref = (
                (own_grad, far_grad, far_value) if order else (far_grad, own_grad, own_value)
            )
            for place in range(plan.in_chunk):
                head = plan.head(chunk, place)
                at = pl.ds(head * plan.width, plan.width)
                qg_ref[:, at] = dot(da_ref[place], maps_ref[head], 1, 1).astype(BF16)
                kg_ref[:, at] = dot(db_ref[place], maps_ref[head], 1, 1).astype(BF16)
                vg_ref[:, at] = dv_ref[place]

    by_core(core, lambda: fill(0), lambda: fill(1))


def output_rows(plan, maps, pieces):
    shape = jax.ShapeDtypeStruct((plan.tokens, plan.heads * plan.width), BF16)
    return call(
        functools.partial(rows_kernel, plan),
        (maps, *pieces),
        [shape] * 3,
        matmuls(plan, 2 * plan.heads),
    )


def swap_core(plan, state):
    return lax.ppermute(state, "context", [(i, i ^ 1) for i in range(plan.ranks)])


def swap_chip(plan, state):
    return lax.ppermute(state, "context", [(i, i ^ 2) for i in range(plan.ranks)])


def chain_hop(plan, state, hop):
    steps = []
    for low in range(4):
        source = hop if low % 2 else plan.groups - 1 - hop
        target = source + (1 if low % 2 else -1)
        steps.append((4 * source + low, 4 * target + low))
    return lax.ppermute(state, "context", steps)


def plane_sums(plan, terms):
    core, chip, _ = device_place()
    replica = lax.axis_index("dp")
    ranks, copies, width = plan.ranks, plan.copies, plan.width
    height = plan.heads * width // (copies * ranks)
    parts = terms.reshape(-1, 2, height, width)
    sent = lax.dynamic_index_in_dim(parts, 1 - core, 1, keepdims=False)
    kept = lax.dynamic_index_in_dim(parts, core, 1, keepdims=False)
    total = (kept + swap_core(plan, sent)).reshape(copies, -1, 2, height, width)

    def plane_part(target_replica, target_chip):
        some = lax.dynamic_index_in_dim(total, target_replica, 0, keepdims=False)
        return lax.dynamic_index_in_dim(some, target_chip, 1, keepdims=False)

    plane = plane_part(replica, chip)
    for turn in range(copies):
        for flip in range(2):
            if turn == 0 and flip == 0:
                continue
            steps = [
                (r * ranks + i, ((r + turn) % copies) * ranks + (i ^ (2 * flip)))
                for r in range(copies)
                for i in range(ranks)
            ]
            sent = plane_part((replica + turn) % copies, (chip + flip) % 2)
            plane = plane + lax.ppermute(sent, ("dp", "context"), steps)
    return plane


def group_sum(plan, plane):
    _, _, group = device_place()
    result = lax.dynamic_index_in_dim(plane, group, 0, keepdims=False)
    for turn in range(1, plan.groups):
        steps = [(i, (i + 4 * turn) % plan.ranks) for i in range(plan.ranks)]
        sent = lax.dynamic_index_in_dim(plane, (group + turn) % plan.groups, 0, keepdims=False)
        result = result + lax.ppermute(sent, "context", steps)
    return result


def per_device(queries, key_rows, value_rows, out_grad, feature_maps):
    tokens = queries.shape[1]
    heads, width, _ = feature_maps.shape
    plan = Plan(heads, width, tokens, lax.axis_size("context"), lax.axis_size("dp"))
    rows = [x.reshape(tokens, heads * width) for x in (queries, key_rows, value_rows, out_grad)]
    core, chip, _ = device_place()
    last = chip == core
    chunks = range(plan.chunks)

    sent = states(plan, False, rows, feature_maps)
    from_core = [[swap_core(plan, x) for x in sent[chunk]] for chunk in chunks]
    mine = states(plan, True, rows, feature_maps)
    stash = inner(plan, rows, feature_maps)

    kept, from_chip, group = [], [], []
    for chunk in chunks:
        given = mine[chunk][1] + from_core[chunk][1]
        if chunk:
            given, from_chip[-1] = lax.optimization_barrier((given, from_chip[-1]))
        kept.append(mine[chunk][0] + from_core[chunk][0])
        from_chip.append(swap_chip(plan, given))
        group.append(kept[chunk] + from_chip[chunk])

    before = [jnp.zeros_like(x) for x in group]
    for stage in range(plan.groups - 1 + plan.chunks - 1):
        for chunk in chunks:
            hop = stage - chunk
            if 0 <= hop < plan.groups - 1:
                before[chunk] = before[chunk] + chain_hop(plan, before[chunk] + group[chunk], hop)

    planes, pieces = [], []
    for chunk in chunks:
        keep = before[chunk] + jnp.where(last, from_chip[chunk], 0.0)
        give = swap_chip(plan, before[chunk] + jnp.where(last, 0.0, kept[chunk]))
        far_keep, far_give = swap_core(plan, keep), swap_core(plan, give)
        grad, term, value = outer(
            plan, True, chunk, rows, stash[chunk], keep, give, from_core[chunk]
        )
        far_grad, term, far_value = outer(
            plan, False, chunk, rows, stash[chunk], far_keep, far_give, [term]
        )
        pieces += [grad, value, far_grad, far_value]
        planes.append(plane_sums(plan, term))
    query_grad, key_grad, value_grad = output_rows(plan, feature_maps, pieces)
    maps_grad = group_sum(plan, jnp.concatenate(planes, axis=0)) * plan.norm
    return (query_grad[None], key_grad[None], value_grad[None], maps_grad)


def solution(mesh):
    in_specs = (
        P("dp", "context", None),
        P("dp", "context", None),
        P("dp", "context", None),
        P("dp", "context", None),
        P(),
    )
    out_specs = (
        P("dp", "context", None),
        P("dp", "context", None),
        P("dp", "context", None),
        P(("dp", "context"), None),
    )
    return jax.shard_map(
        per_device, mesh=mesh, in_specs=in_specs, out_specs=out_specs, check_vma=False
    )
```

```python
import functools
import math

import jax
import jax.numpy as jnp
from jax import lax
from jax.experimental import pallas as pl
from jax.experimental.pallas import tpu as pltpu
from jax.sharding import PartitionSpec as P

F32 = jnp.float32
BF16 = jnp.bfloat16
VMEM_LIMIT = 8 * 1024 * 1024
LOAD_LIMIT = 50 * 1024 * 1024
LOAD_ROWS = 32


class Plan:
    def __init__(self, heads, width, tokens, ranks, copies):
        self.heads, self.width, self.tokens = heads, width, tokens
        self.ranks, self.copies = ranks, copies
        self.groups = ranks // 4
        per_copy = heads // copies if heads % copies == 0 else 0
        self.chunks = 2 if per_copy and per_copy % 2 == 0 and self.groups % 2 == 0 else 1
        self.in_chunk = heads // self.chunks
        self.quarter = self.in_chunk // 4
        self.run = per_copy // self.chunks if self.chunks > 1 else self.in_chunk
        self.stride = per_copy if self.chunks > 1 else 0
        self.factor = 1.0 / math.sqrt(width * tokens * ranks)
        self.norm = 1.0 / math.sqrt(copies * tokens * ranks)

    def head(self, chunk, place):
        return (place // self.run) * self.stride + chunk * self.run + place % self.run


def device_place():
    index = lax.axis_index("context")
    return index % 2, (index // 2) % 2, index // 4


def columns(ref, head, width):
    start = head * width
    if not isinstance(start, int):
        start = pl.multiple_of(start, width)
    return ref[:, pl.ds(start, width)]


def dot(left, right, left_dim=1, right_dim=0):
    return lax.dot_general(
        left, right, (((left_dim,), (right_dim,)), ((), ())), preferred_element_type=F32
    )


def state_dot(rows, parts, state_dim):
    return dot(rows, parts[0], 1, state_dim) + dot(rows, parts[1], 1, state_dim)


def split_state(state):
    upper = state.astype(BF16)
    return upper, (state - upper.astype(F32)).astype(BF16)


def call(body, operands, shapes, flops, in_specs=None, scratch=(), limit=VMEM_LIMIT):
    moved = sum(x.size * x.dtype.itemsize for x in list(operands) + list(shapes))
    whole = pl.BlockSpec(memory_space=pltpu.VMEM)
    return pl.pallas_call(
        body,
        out_shape=shapes,
        in_specs=in_specs or [whole] * len(operands),
        out_specs=[whole] * len(shapes),
        scratch_shapes=list(scratch),
        compiler_params=pltpu.CompilerParams(vmem_limit_bytes=limit),
        cost_estimate=pl.CostEstimate(flops=flops, bytes_accessed=moved, transcendentals=0),
    )(*operands)


def matmuls(plan, count):
    return 2 * count * plan.tokens * plan.width * plan.width


def near_places(plan, chip_turn, core_turn):
    core, chip, _ = device_place()
    core = core if core_turn == 0 else 1 - core
    chip = chip if chip_turn == 0 else 1 - chip
    first = (2 * chip + core) * plan.quarter
    return [first + i for i in range(plan.quarter)]


def fill_states(plan, core_turn, q_ref, k_ref, v_ref, g_ref, maps_ref, out_refs):
    width = plan.width
    for chunk in range(plan.chunks):
        for chip_turn in range(2):
            for i, place in enumerate(near_places(plan, chip_turn, core_turn)):
                head = plan.head(chunk, place)
                feat_key = dot(columns(k_ref, head, width), maps_ref[head]).astype(BF16)
                feat_query = dot(columns(q_ref, head, width), maps_ref[head]).astype(BF16)
                out_refs[chunk][chip_turn, 0, i] = dot(feat_key, columns(v_ref, head, width), 0, 0)
                out_refs[chunk][chip_turn, 1, i] = dot(
                    feat_query, columns(g_ref, head, width), 0, 0
                )


def load_kernel(plan, *refs):
    sources, loaded = refs[:5], refs[5:10]
    out_refs, sems = refs[10:-1], refs[-1]
    copies = []
    for source, target in zip(sources, loaded):
        step = LOAD_ROWS if source.shape[0] % LOAD_ROWS == 0 else source.shape[0]
        if len(source.shape) == 3:
            step = max(1, source.shape[0] // 4)
        for start in range(0, source.shape[0], step):
            at = pl.ds(start, step)
            copies.append(
                pltpu.make_async_copy(source.at[at], target.at[at], sems.at[len(copies)])
            )
    for copy in copies:
        copy.start()
    for copy in copies:
        copy.wait()
    fill_states(plan, 1, *loaded, out_refs)


def load_and_send_states(plan, rows, maps):
    shape = (2, 2, plan.quarter, plan.width, plan.width)
    loads = [jax.ShapeDtypeStruct(x.shape, x.dtype) for x in (*rows, maps)]
    outs = call(
        functools.partial(load_kernel, plan),
        (*rows, maps),
        loads + [jax.ShapeDtypeStruct(shape, F32)] * plan.chunks,
        matmuls(plan, 2 * plan.heads),
        in_specs=[pl.BlockSpec(memory_space=pltpu.HBM)] * 5,
        scratch=[pltpu.SemaphoreType.DMA((64,))],
        limit=LOAD_LIMIT,
    )
    return outs[:4], outs[4], outs[5:]


def kept_states(plan, rows, maps):
    shape = (2, 2, plan.quarter, plan.width, plan.width)
    return call(
        lambda *refs: fill_states(plan, 0, *refs[:5], refs[5:]),
        (*rows, maps),
        [jax.ShapeDtypeStruct(shape, F32)] * plan.chunks,
        matmuls(plan, 2 * plan.heads),
    )


def inner_kernel(plan, q_ref, k_ref, v_ref, g_ref, maps_ref, *out_refs):
    tokens, width = plan.tokens, plan.width
    row = lax.broadcasted_iota(jnp.int32, (tokens, tokens), 0)
    column = lax.broadcasted_iota(jnp.int32, (tokens, tokens), 1)
    causal = row >= column
    for chunk in range(plan.chunks):
        feat_ref, da_ref, db_ref, dv_ref = out_refs[4 * chunk : 4 * chunk + 4]
        for first in range(0, plan.in_chunk, 4):
            places = range(first, min(first + 4, plan.in_chunk))
            heads = [plan.head(chunk, place) for place in places]
            grads = [columns(g_ref, head, width) for head in heads]
            scores_gv = [
                jnp.where(causal, dot(grad, columns(v_ref, head, width), 1, 1), 0.0).astype(BF16)
                for grad, head in zip(grads, heads)
            ]
            feats_query = [
                dot(columns(q_ref, head, width), maps_ref[head]).astype(BF16) for head in heads
            ]
            feats_key = [
                dot(columns(k_ref, head, width), maps_ref[head]).astype(BF16) for head in heads
            ]
            scores_ab = [
                jnp.where(causal, dot(left, right, 1, 1), 0.0).astype(BF16)
                for left, right in zip(feats_query, feats_key)
            ]
            for n, place in enumerate(places):
                feat_ref[place] = feats_key[n]
                da_ref[place] = dot(scores_gv[n], feats_key[n])
                db_ref[place] = dot(scores_gv[n], feats_query[n], 0, 0)
                dv_ref[place] = dot(scores_ab[n], grads[n], 0, 0)


def inner(plan, rows, maps):
    wide = jax.ShapeDtypeStruct((plan.in_chunk, plan.tokens, plan.width), F32)
    narrow = jax.ShapeDtypeStruct((plan.in_chunk, plan.tokens, plan.width), BF16)
    outs = call(
        functools.partial(inner_kernel, plan),
        (*rows, maps),
        [narrow, wide, wide, wide] * plan.chunks,
        matmuls(plan, 7 * plan.heads),
    )
    return [outs[4 * chunk : 4 * chunk + 4] for chunk in range(plan.chunks)]


def outer_kernel(plan, core_turn, chunk, *refs):
    width = plan.width
    core, _, _ = device_place()
    q_ref, k_ref, v_ref, g_ref, feat_ref, da_ref, db_ref, dv_ref = refs[:8]
    state_refs, extra_ref = refs[8:10], refs[10]
    da_out, db_out, dv_out, term_out = refs[11:]
    jobs = []
    for chip_turn in range(2):
        for i, place in enumerate(near_places(plan, chip_turn, core_turn)):
            jobs.append((chip_turn, i, place, plan.head(chunk, place)))
    parts = []
    for chip_turn, i, _, _ in jobs:
        prefix, suffix = state_refs[chip_turn][0, i], state_refs[chip_turn][1, i]
        if core_turn == 0:
            prefix = prefix + jnp.where(core == 1, extra_ref[chip_turn, 0, i], 0.0)
            suffix = suffix + jnp.where(core == 0, extra_ref[chip_turn, 1, i], 0.0)
        parts.append((split_state(prefix), split_state(suffix)))
    from_queries = [
        state_dot(columns(g_ref, job[3], width), part[0], 1) for job, part in zip(jobs, parts)
    ]
    from_keys = [
        state_dot(columns(v_ref, job[3], width), part[1], 1) for job, part in zip(jobs, parts)
    ]
    from_values = [state_dot(feat_ref[job[2]], part[1], 0) for job, part in zip(jobs, parts)]
    grads_a = [
        (plan.factor * (da_ref[job[2]] + far)).astype(BF16)
        for job, far in zip(jobs, from_queries)
    ]
    grads_b = [
        (plan.factor * (db_ref[job[2]] + far)).astype(BF16) for job, far in zip(jobs, from_keys)
    ]
    terms = [
        dot(columns(q_ref, job[3], width), grad_a, 0, 0)
        + dot(columns(k_ref, job[3], width), grad_b, 0, 0)
        for job, grad_a, grad_b in zip(jobs, grads_a, grads_b)
    ]
    for n, (chip_turn, i, place, _) in enumerate(jobs):
        da_out[chip_turn, i] = grads_a[n]
        db_out[chip_turn, i] = grads_b[n]
        dv_out[chip_turn, i] = (plan.factor * (dv_ref[place] + from_values[n])).astype(BF16)
        if core_turn == 0:
            term_out[chip_turn, i] = terms[n]
        else:
            term_out[place] = terms[n]
    if core_turn:
        for chip_turn in range(2):
            for i, place in enumerate(near_places(plan, chip_turn, 0)):
                term_out[place] = extra_ref[chip_turn, i]


def outer(plan, core_turn, chunk, rows, stash, states, extra):
    shape = jax.ShapeDtypeStruct((2, plan.quarter, plan.tokens, plan.width), BF16)
    square = (plan.width, plan.width)
    lead = (plan.in_chunk,) if core_turn else (2, plan.quarter)
    outs = call(
        functools.partial(outer_kernel, plan, core_turn, chunk),
        (*rows, *stash, *states, extra),
        [shape] * 3 + [jax.ShapeDtypeStruct(lead + square, F32)],
        matmuls(plan, 4 * plan.in_chunk),
    )
    return outs[:3], outs[3]


def rows_kernel(plan, maps_ref, *refs):
    qg_ref, kg_ref, vg_ref = refs[-3:]
    for chunk in range(plan.chunks):
        for core_turn in range(2):
            first = 6 * chunk + 3 * core_turn
            da_ref, db_ref, dv_ref = refs[first : first + 3]
            for chip_turn in range(2):
                for i, place in enumerate(near_places(plan, chip_turn, core_turn)):
                    head = plan.head(chunk, place)
                    at = pl.ds(pl.multiple_of(head * plan.width, plan.width), plan.width)
                    qg_ref[:, at] = dot(da_ref[chip_turn, i], maps_ref[head], 1, 1).astype(BF16)
                    kg_ref[:, at] = dot(db_ref[chip_turn, i], maps_ref[head], 1, 1).astype(BF16)
                    vg_ref[:, at] = dv_ref[chip_turn, i]


def output_rows(plan, maps, pieces):
    shape = jax.ShapeDtypeStruct((plan.tokens, plan.heads * plan.width), BF16)
    return call(
        functools.partial(rows_kernel, plan),
        (maps, *pieces),
        [shape] * 3,
        matmuls(plan, 2 * plan.heads),
    )


def swap_core(plan, state):
    return lax.ppermute(state, "context", [(i, i ^ 1) for i in range(plan.ranks)])


def swap_chip(plan, state):
    return lax.ppermute(state, "context", [(i, i ^ 2) for i in range(plan.ranks)])


def chain_hop(plan, before, group_state, hop):
    _, _, group = device_place()
    mirror = plan.groups - 1 - hop
    upwards = [(4 * hop + low, 4 * hop + 4 + low) for low in range(4)]
    downwards = [(4 * mirror + low, 4 * mirror - 4 + low) for low in range(4)]
    ready = before + group_state
    if plan.groups % 2:
        up = lax.ppermute(ready[0], "context", upwards)
        down = lax.ppermute(ready[1], "context", downwards)
        return before + jnp.stack([up, down])
    steps = sorted(set(upwards + downwards + [(b, a) for a, b in upwards + downwards]))
    got = lax.ppermute(jnp.where(group == hop, ready[0], ready[1]), "context", steps)
    side = jnp.arange(2).reshape(2, 1, 1, 1)
    wanted = jnp.where(side == 0, group == hop + 1, group == mirror - 1)
    return before + jnp.where(wanted, got[None], 0.0)


def plane_sums(plan, terms):
    core, chip, _ = device_place()
    replica = lax.axis_index("dp")
    ranks, copies, width = plan.ranks, plan.copies, plan.width
    height = plan.heads * width // (copies * ranks)
    parts = terms.reshape(-1, 2, height, width)
    sent = lax.dynamic_index_in_dim(parts, 1 - core, 1, keepdims=False)
    kept = lax.dynamic_index_in_dim(parts, core, 1, keepdims=False)
    total = (kept + swap_core(plan, sent)).reshape(copies, -1, 2, height, width)

    def plane_part(target_replica, target_chip):
        some = lax.dynamic_index_in_dim(total, target_replica, 0, keepdims=False)
        return lax.dynamic_index_in_dim(some, target_chip, 1, keepdims=False)

    plane = plane_part(replica, chip)
    for turn in range(copies):
        for flip in range(2):
            if turn == 0 and flip == 0:
                continue
            steps = [
                (r * ranks + i, ((r + turn) % copies) * ranks + (i ^ (2 * flip)))
                for r in range(copies)
                for i in range(ranks)
            ]
            sent = plane_part((replica + turn) % copies, (chip + flip) % 2)
            plane = plane + lax.ppermute(sent, ("dp", "context"), steps)
    return plane


def group_sum(plan, plane):
    _, _, group = device_place()
    result = lax.dynamic_index_in_dim(plane, group, 0, keepdims=False)
    for turn in range(1, plan.groups):
        steps = [(i, (i + 4 * turn) % plan.ranks) for i in range(plan.ranks)]
        sent = lax.dynamic_index_in_dim(plane, (group + turn) % plan.groups, 0, keepdims=False)
        result = result + lax.ppermute(sent, "context", steps)
    return result


def per_device(queries, key_rows, value_rows, out_grad, feature_maps):
    tokens = queries.shape[1]
    heads, width, _ = feature_maps.shape
    plan = Plan(heads, width, tokens, lax.axis_size("context"), lax.axis_size("dp"))
    rows = [x.reshape(tokens, heads * width) for x in (queries, key_rows, value_rows, out_grad)]
    core, chip, _ = device_place()
    side = jnp.arange(2).reshape(2, 1, 1, 1)
    chunks = range(plan.chunks)

    rows, maps, sent = load_and_send_states(plan, rows, feature_maps)
    from_core = [swap_core(plan, sent[chunk]) for chunk in chunks]
    kept = kept_states(plan, rows, maps)
    stash = inner(plan, rows, maps)

    total, from_chip, group_state = [], [], []
    for chunk in chunks:
        given = kept[chunk][1] + from_core[chunk][1]
        if chunk:
            given, from_chip[-1], stash = lax.optimization_barrier((given, from_chip[-1], stash))
        total.append(kept[chunk][0] + from_core[chunk][0])
        from_chip.append(swap_chip(plan, given))
        group_state.append(total[chunk] + from_chip[chunk])

    before = [jnp.zeros_like(x) for x in group_state]
    for stage in range(plan.groups - 1 + plan.chunks - 1):
        for chunk in chunks:
            hop = stage - chunk
            if 0 <= hop < plan.groups - 1:
                before[chunk] = chain_hop(plan, before[chunk], group_state[chunk], hop)

    planes, pieces = [], []
    for chunk in chunks:
        mate = before[chunk] + jnp.where(side == chip, total[chunk], 0.0)
        states = [
            before[chunk] + jnp.where(side != chip, from_chip[chunk], 0.0),
            swap_chip(plan, mate),
        ]
        crossed = [
            swap_core(plan, state + jnp.where(side == core, kept[chunk][turn], 0.0))
            for turn, state in enumerate(states)
        ]
        own, term = outer(plan, 0, chunk, rows, stash[chunk], states, from_core[chunk])
        far, term = outer(plan, 1, chunk, rows, stash[chunk], crossed, term)
        pieces += [*own, *far]
        planes.append(plane_sums(plan, term))
    query_grad, key_grad, value_grad = output_rows(plan, maps, pieces)
    maps_grad = group_sum(plan, jnp.concatenate(planes, axis=0)) * plan.norm
    return (query_grad[None], key_grad[None], value_grad[None], maps_grad)


def solution(mesh):
    in_specs = (
        P("dp", "context", None),
        P("dp", "context", None),
        P("dp", "context", None),
        P("dp", "context", None),
        P(),
    )
    out_specs = (
        P("dp", "context", None),
        P("dp", "context", None),
        P("dp", "context", None),
        P(("dp", "context"), None),
    )
    return jax.shard_map(
        per_device, mesh=mesh, in_specs=in_specs, out_specs=out_specs, check_vma=False
    )
```

```python
import functools
import math

import jax
import jax.numpy as jnp
from jax import lax
from jax.experimental import pallas as pl
from jax.experimental.pallas import tpu as pltpu
from jax.sharding import PartitionSpec as P

F32 = jnp.float32
BF16 = jnp.bfloat16
VMEM_LIMIT = 57 * 1024 * 1024


class Plan:
    def __init__(self, heads, width, tokens, ranks, copies):
        self.heads, self.width, self.tokens = heads, width, tokens
        self.ranks, self.copies = ranks, copies
        self.groups = ranks // 4
        per_copy = heads // copies if heads % copies == 0 else 0
        self.chunks = 2 if per_copy and per_copy % 2 == 0 and self.groups % 2 == 0 else 1
        self.in_chunk = heads // self.chunks
        self.quarter = self.in_chunk // 4
        self.run = per_copy // self.chunks if self.chunks > 1 else self.in_chunk
        self.stride = per_copy if self.chunks > 1 else 0
        self.factor = 1.0 / math.sqrt(width * tokens * ranks)
        self.norm = 1.0 / math.sqrt(copies * tokens * ranks)

    def head(self, chunk, place):
        return (place // self.run) * self.stride + chunk * self.run + place % self.run


def device_place():
    index = lax.axis_index("context")
    return index % 2, (index // 2) % 2, index // 4


def dot(left, right, left_dim=1, right_dim=0):
    return lax.dot_general(
        left, right, (((left_dim,), (right_dim,)), ((), ())), preferred_element_type=F32
    )


def split(value):
    upper = value.astype(BF16)
    return upper, (value - upper.astype(F32)).astype(BF16)


def call(body, operands, shapes, flops, scratch, copies, aliases=None):
    moved = sum(x.size * x.dtype.itemsize for x in list(operands) + list(shapes))
    anywhere = pl.BlockSpec(memory_space=pl.ANY)
    return pl.pallas_call(
        body,
        out_shape=shapes,
        in_specs=[anywhere] * len(operands),
        out_specs=[anywhere] * len(shapes),
        scratch_shapes=list(scratch) + [pltpu.SemaphoreType.DMA((copies,))],
        input_output_aliases=aliases or {},
        compiler_params=pltpu.CompilerParams(vmem_limit_bytes=VMEM_LIMIT),
        cost_estimate=pl.CostEstimate(flops=flops, bytes_accessed=moved, transcendentals=0),
    )(*operands)


class Copies:
    def __init__(self, sems):
        self.sems, self.used = sems, 0

    def start(self, source, target):
        copy = pltpu.make_async_copy(source, target, self.sems.at[self.used])
        self.used += 1
        copy.start()
        return copy


def wait(copies):
    for copy in copies:
        copy.wait()


def matmuls(plan, count):
    return 2 * count * plan.tokens * plan.width * plan.width


def quarter_place(plan, chip_turn, core_turn):
    core, chip, _ = device_place()
    core = core if core_turn == 0 else 1 - core
    chip = chip if chip_turn == 0 else 1 - chip
    return (2 * chip + core) * plan.quarter


def quarter_heads(plan, chunk, chip_turn, core_turn):
    first = quarter_place(plan, chip_turn, core_turn)
    if plan.run % plan.quarter == 0:
        base = plan.head(chunk, first)
        return [base + i for i in range(plan.quarter)]
    return [plan.head(chunk, first + i) for i in range(plan.quarter)]


def head_columns(ref, head, width):
    start = head * width
    if not isinstance(start, int):
        start = pl.multiple_of(start, width)
    return ref.at[:, pl.ds(start, width)]


def load_heads(plan, copies, row_refs, maps_ref, heads, row_bufs, maps_buf):
    started = []
    for n, head in enumerate(heads):
        mine = [copies.start(maps_ref.at[head], maps_buf.at[n])]
        for ref, buf in zip(row_refs, row_bufs):
            mine.append(copies.start(head_columns(ref, head, plan.width), buf.at[n]))
        started.append(mine)
    return started


def row_scratch(plan, count):
    rows = [pltpu.VMEM((count, plan.tokens, plan.width), BF16)] * 4
    return rows + [pltpu.VMEM((count, plan.width, plan.width), BF16)]


def states_kernel(plan, core_turn, *refs):
    row_refs, maps_ref = refs[:4], refs[4]
    out_refs = refs[5 : 5 + plan.chunks]
    row_bufs, maps_buf = refs[5 + plan.chunks : 9 + plan.chunks], refs[9 + plan.chunks]
    out_buf, sems = refs[-2:]
    copies = Copies(sems)
    heads = []
    for chunk in range(plan.chunks):
        for chip_turn in range(2):
            heads += quarter_heads(plan, chunk, chip_turn, core_turn)
    started = load_heads(plan, copies, row_refs, maps_ref, heads, row_bufs, maps_buf)
    q_buf, k_buf, v_buf, g_buf = row_bufs
    written = []
    n = 0
    for chunk in range(plan.chunks):
        for chip_turn in range(2):
            places = range(n, n + plan.quarter)
            n += plan.quarter
            for place in places:
                wait(started[place])
            feats = [
                (
                    dot(k_buf[place], maps_buf[place]).astype(BF16),
                    dot(q_buf[place], maps_buf[place]).astype(BF16),
                )
                for place in places
            ]
            for i, place in enumerate(places):
                feat_key, feat_query = feats[i]
                out_buf[chunk, chip_turn, 0, i] = dot(feat_key, v_buf[place], 0, 0)
                out_buf[chunk, chip_turn, 1, i] = dot(feat_query, g_buf[place], 0, 0)
        written.append(copies.start(out_buf.at[chunk], out_refs[chunk]))
    wait(written)


def block_states(plan, core_turn, rows, maps):
    shape = (2, 2, plan.quarter, plan.width, plan.width)
    count = plan.heads // 2
    return call(
        functools.partial(states_kernel, plan, core_turn),
        (*rows, maps),
        [jax.ShapeDtypeStruct(shape, F32)] * plan.chunks,
        matmuls(plan, 2 * plan.heads),
        row_scratch(plan, count) + [pltpu.VMEM((plan.chunks,) + shape, F32)],
        5 * count + plan.chunks,
    )


def causal_mask(tokens):
    row = lax.broadcasted_iota(jnp.int32, (tokens, tokens), 0)
    column = lax.broadcasted_iota(jnp.int32, (tokens, tokens), 1)
    return row >= column


def inner_kernel(plan, chunk, *refs):
    row_refs, maps_ref, base_ref, pair_ref = refs[:4], refs[4], refs[5], refs[6]
    row_bufs, maps_buf = refs[7:11], refs[11]
    base_buf, pair_buf, sems = refs[12:]
    copies = Copies(sems)
    heads = [plan.head(chunk, place) for place in range(plan.in_chunk)]
    started = load_heads(plan, copies, row_refs, maps_ref, heads, row_bufs, maps_buf)
    q_buf, k_buf, v_buf, g_buf = row_bufs
    causal = causal_mask(plan.tokens)
    step = 2
    for first in range(0, plan.in_chunk, step):
        places = range(first, min(first + step, plan.in_chunk))
        for place in places:
            wait(started[place])
        scores = [
            jnp.where(causal, dot(g_buf[place], v_buf[place], 1, 1), 0.0).astype(BF16)
            for place in places
        ]
        feats_query = [dot(q_buf[place], maps_buf[place]).astype(BF16) for place in places]
        feats_key = [dot(k_buf[place], maps_buf[place]).astype(BF16) for place in places]
        for place in places:
            pair_buf[0, place], pair_buf[1, place] = split(dot(q_buf[place], g_buf[place], 0, 0))
            pair_buf[2, place], pair_buf[3, place] = split(dot(k_buf[place], v_buf[place], 0, 0))
        grads_a = [dot(score, feat).astype(F32) for score, feat in zip(scores, feats_key)]
        grads_b = [dot(score, feat, 0, 0) for score, feat in zip(scores, feats_query)]
        for n, place in enumerate(places):
            upper_a, lower_a = split(grads_a[n])
            upper_b, lower_b = split(grads_b[n])
            base_buf[place] = (
                dot(q_buf[place], upper_a, 0, 0)
                + dot(q_buf[place], lower_a, 0, 0)
                + dot(k_buf[place], upper_b, 0, 0)
                + dot(k_buf[place], lower_b, 0, 0)
            )
    wait([copies.start(base_buf, base_ref), copies.start(pair_buf, pair_ref)])


def inner(plan, chunk, rows, maps):
    square = (plan.in_chunk, plan.width, plan.width)
    return call(
        functools.partial(inner_kernel, plan, chunk),
        (*rows, maps),
        [jax.ShapeDtypeStruct(square, F32), jax.ShapeDtypeStruct((4,) + square, BF16)],
        matmuls(plan, 11 * plan.in_chunk),
        row_scratch(plan, plan.in_chunk)
        + [pltpu.VMEM(square, F32), pltpu.VMEM((4,) + square, BF16)],
        5 * plan.in_chunk + 2,
    )


def final_states(plan, state_bufs, extra_buf):
    core, _, _ = device_place()
    for core_turn in range(2):
        for chip_turn in range(2):
            for i in range(plan.quarter):
                state = state_bufs[2 * core_turn + chip_turn]
                prefix, suffix = state[0, i], state[1, i]
                if core_turn == 0:
                    prefix = prefix + jnp.where(core == 1, extra_buf[chip_turn, 0, i], 0.0)
                    suffix = suffix + jnp.where(core == 0, extra_buf[chip_turn, 1, i], 0.0)
                yield core_turn, chip_turn, i, prefix, suffix


def state_scratch(plan):
    shape = (2, plan.quarter, plan.width, plan.width)
    return [pltpu.VMEM(shape, F32)] * 4 + [pltpu.VMEM((2,) + shape, F32)]


def term_kernel(plan, *refs):
    sources, out_ref = refs[:7], refs[7]
    bufs, out_buf, sems = refs[8:15], refs[15], refs[16]
    copies = Copies(sems)
    wait([copies.start(source, buf) for source, buf in zip(sources, bufs)])
    base_buf, pair_buf = bufs[5:]
    for core_turn, chip_turn, i, prefix, suffix in final_states(plan, bufs[:4], bufs[4]):
        place = quarter_place(plan, chip_turn, core_turn) + i
        total = base_buf[place]
        for n, state in enumerate((prefix, suffix)):
            upper, lower = split(state)
            left_upper, left_lower = pair_buf[2 * n, place], pair_buf[2 * n + 1, place]
            total = total + (
                dot(left_upper, upper, 1, 1)
                + dot(left_upper, lower, 1, 1)
                + dot(left_lower, upper, 1, 1)
            )
        out_buf[place] = plan.factor * total
    wait([copies.start(out_buf, out_ref)])


def maps_term(plan, states, extra, base, pair):
    square = (plan.in_chunk, plan.width, plan.width)
    return call(
        functools.partial(term_kernel, plan),
        (*states, extra, base, pair),
        [jax.ShapeDtypeStruct(square, F32)],
        matmuls(plan, 6 * plan.in_chunk),
        state_scratch(plan)
        + [pltpu.VMEM(square, F32), pltpu.VMEM((4,) + square, BF16), pltpu.VMEM(square, F32)],
        8,
    )[0]


def rows_kernel(plan, chunk, *refs):
    count = plan.in_chunk
    row_refs, maps_ref, sources = refs[:4], refs[4], refs[5:10]
    refs = refs[10 + (3 if chunk else 0) :]
    out_refs, row_bufs, maps_buf = refs[:3], refs[3:7], refs[7]
    bufs, out_bufs, sems = refs[8:13], refs[13:16], refs[16]
    copies = Copies(sems)
    heads = []
    for core_turn in range(2):
        for chip_turn in range(2):
            heads += quarter_heads(plan, chunk, chip_turn, core_turn)
    state_copies = [copies.start(source, buf) for source, buf in zip(sources, bufs)]
    started = load_heads(plan, copies, row_refs, maps_ref, heads, row_bufs, maps_buf)
    q_buf, k_buf, v_buf, g_buf = row_bufs
    causal = causal_mask(plan.tokens)
    wait(state_copies)
    written = []
    for n, item in enumerate(final_states(plan, bufs[:4], bufs[4])):
        prefix, suffix = split(item[3]), split(item[4])
        wait(started[n])
        query, key, value, grad, matrix = (
            q_buf[n], k_buf[n], v_buf[n], g_buf[n], maps_buf[n]
        )
        score_gv = jnp.where(causal, dot(grad, value, 1, 1), 0.0).astype(BF16)
        feat_query, feat_key = dot(query, matrix).astype(BF16), dot(key, matrix).astype(BF16)
        score_ab = jnp.where(causal, dot(feat_query, feat_key, 1, 1), 0.0).astype(BF16)
        far_a = dot(grad, prefix[0], 1, 1) + dot(grad, prefix[1], 1, 1)
        far_b = dot(value, suffix[0], 1, 1) + dot(value, suffix[1], 1, 1)
        far_v = dot(feat_key, suffix[0]) + dot(feat_key, suffix[1])
        grad_a = (plan.factor * (dot(score_gv, feat_key) + far_a)).astype(BF16)
        grad_b = (plan.factor * (dot(score_gv, feat_query, 0, 0) + far_b)).astype(BF16)
        out_bufs[0][n] = dot(grad_a, matrix, 1, 1).astype(BF16)
        out_bufs[1][n] = dot(grad_b, matrix, 1, 1).astype(BF16)
        out_bufs[2][n] = (plan.factor * (dot(score_ab, grad, 0, 0) + far_v)).astype(BF16)
        for buf, ref in zip(out_bufs, out_refs):
            written.append(copies.start(buf.at[n], head_columns(ref, heads[n], plan.width)))
    wait(written)


def output_rows(plan, chunk, rows, maps, states, extra, done):
    shape = jax.ShapeDtypeStruct((plan.tokens, plan.heads * plan.width), BF16)
    count = plan.in_chunk
    narrow = [pltpu.VMEM((count, plan.tokens, plan.width), BF16)] * 3
    return call(
        functools.partial(rows_kernel, plan, chunk),
        (*rows, maps, *states, extra, *done),
        [shape] * 3,
        matmuls(plan, 15 * count),
        row_scratch(plan, count) + state_scratch(plan) + narrow,
        8 * count + 5,
        {10: 0, 11: 1, 12: 2} if done else None,
    )


def swap_core(plan, state):
    return lax.ppermute(state, "context", [(i, i ^ 1) for i in range(plan.ranks)])


def swap_chip(plan, state):
    return lax.ppermute(state, "context", [(i, i ^ 2) for i in range(plan.ranks)])


def chain_swap(plan, state, hop):
    mirror = plan.groups - 1 - hop
    steps = [(i, i ^ 1) for i in range(plan.ranks)]
    for low in range(4):
        for left in (hop, mirror - 1):
            a, b = 4 * left + low, 4 * left + 4 + low
            steps[a], steps[b] = (a, b), (b, a)
    return lax.ppermute(state, "context", steps)


def chain_split(plan, state, hop):
    mirror = plan.groups - 1 - hop
    up = [(4 * hop + low, 4 * hop + 4 + low) for low in range(4)]
    down = [(4 * mirror + low, 4 * mirror - 4 + low) for low in range(4)]
    return lax.ppermute(state[0], "context", up), lax.ppermute(state[1], "context", down)


def plane_sums(plan, terms):
    core, chip, _ = device_place()
    replica = lax.axis_index("dp")
    ranks, copies, width = plan.ranks, plan.copies, plan.width
    height = plan.heads * width // (copies * ranks)
    parts = terms.reshape(-1, 2, height, width)
    sent = lax.dynamic_index_in_dim(parts, 1 - core, 1, keepdims=False)
    kept = lax.dynamic_index_in_dim(parts, core, 1, keepdims=False)
    total = (kept + swap_core(plan, sent)).reshape(copies, -1, 2, height, width)

    def plane_part(target_replica, target_chip):
        some = lax.dynamic_index_in_dim(total, target_replica, 0, keepdims=False)
        return lax.dynamic_index_in_dim(some, target_chip, 1, keepdims=False)

    plane = plane_part(replica, chip)
    for turn in range(copies):
        for flip in range(2):
            if turn == 0 and flip == 0:
                continue
            steps = [
                (r * ranks + i, ((r + turn) % copies) * ranks + (i ^ (2 * flip)))
                for r in range(copies)
                for i in range(ranks)
            ]
            sent = plane_part((replica + turn) % copies, (chip + flip) % 2)
            plane = plane + lax.ppermute(sent, ("dp", "context"), steps)
    return plane


def group_sum(plan, plane):
    _, _, group = device_place()
    result = lax.dynamic_index_in_dim(plane, group, 0, keepdims=False)
    for turn in range(1, plan.groups):
        steps = [(i, (i + 4 * turn) % plan.ranks) for i in range(plan.ranks)]
        sent = lax.dynamic_index_in_dim(plane, (group + turn) % plan.groups, 0, keepdims=False)
        result = result + lax.ppermute(sent, "context", steps)
    return result


def scan_groups(plan, group_state):
    _, _, group = device_place()
    chunks, hops = range(plan.chunks), plan.groups - 1
    before = [jnp.zeros_like(x) for x in group_state]
    if plan.groups % 2:
        for chunk in chunks:
            for hop in range(hops):
                up, down = chain_split(plan, before[chunk] + group_state[chunk], hop)
                before[chunk] = before[chunk] + jnp.stack([up, down])
        return before
    got = [[] for _ in chunks]
    for stage in range(hops + plan.chunks - 1):
        for chunk in chunks:
            hop = stage - chunk
            if not 0 <= hop < hops:
                continue
            send = jnp.where(group == hop, group_state[chunk][0], group_state[chunk][1])
            if hop:
                send = send + got[chunk][-1]
            if chunk:
                send, got[0][hop] = lax.optimization_barrier((send, got[0][hop]))
            got[chunk].append(chain_swap(plan, send, hop))
    for chunk in chunks:
        prefix, suffix = before[chunk]
        for hop in range(hops):
            prefix = jnp.where(group == hop + 1, got[chunk][hop], prefix)
            suffix = jnp.where(group == hops - 1 - hop, got[chunk][hop], suffix)
        before[chunk] = jnp.stack([prefix, suffix])
    return before


def per_device(queries, key_rows, value_rows, out_grad, maps):
    tokens = queries.shape[1]
    heads, width, _ = maps.shape
    plan = Plan(heads, width, tokens, lax.axis_size("context"), lax.axis_size("dp"))
    rows = [x.reshape(tokens, heads * width) for x in (queries, key_rows, value_rows, out_grad)]
    core, chip, _ = device_place()
    side = jnp.arange(2).reshape(2, 1, 1, 1)
    chunks = range(plan.chunks)

    sent = block_states(plan, 1, rows, maps)
    from_core = [swap_core(plan, sent[chunk]) for chunk in chunks]
    kept = block_states(plan, 0, rows, maps)
    terms = [inner(plan, chunk, rows, maps) for chunk in chunks]

    total, from_chip, group_state = [], [], []
    for chunk in chunks:
        given = kept[chunk][1] + from_core[chunk][1]
        if chunk:
            given, from_chip[-1], terms[0] = lax.optimization_barrier(
                (given, from_chip[-1], terms[0])
            )
        total.append(kept[chunk][0] + from_core[chunk][0])
        from_chip.append(swap_chip(plan, given))
        group_state.append(total[chunk] + from_chip[chunk])
    before = scan_groups(plan, group_state)

    planes, done = [], ()
    for chunk in chunks:
        mate = before[chunk] + jnp.where(side == chip, total[chunk], 0.0)
        states = [
            before[chunk] + jnp.where(side != chip, from_chip[chunk], 0.0),
            swap_chip(plan, mate),
        ]
        states += [
            swap_core(plan, state + jnp.where(side == core, kept[chunk][turn], 0.0))
            for turn, state in enumerate(states)
        ]
        term = maps_term(plan, states, from_core[chunk], *terms[chunk])
        done = output_rows(plan, chunk, rows, maps, states, from_core[chunk], done)
        planes.append(plane_sums(plan, term))
    query_grad, key_grad, value_grad = done
    maps_grad = group_sum(plan, jnp.concatenate(planes, axis=0)) * plan.norm
    return (query_grad[None], key_grad[None], value_grad[None], maps_grad)


def solution(mesh):
    in_specs = (
        P("dp", "context", None),
        P("dp", "context", None),
        P("dp", "context", None),
        P("dp", "context", None),
        P(),
    )
    out_specs = (
        P("dp", "context", None),
        P("dp", "context", None),
        P("dp", "context", None),
        P(("dp", "context"), None),
    )
    return jax.shard_map(
        per_device, mesh=mesh, in_specs=in_specs, out_specs=out_specs, check_vma=False
    )
```

```python
import functools
import math

import jax
import jax.numpy as jnp
from jax import lax
from jax.experimental import pallas as pl
from jax.experimental.pallas import tpu as pltpu
from jax.sharding import PartitionSpec as P

F32 = jnp.float32
BF16 = jnp.bfloat16
VMEM_LIMIT = 57 * 1024 * 1024


class Plan:
    def __init__(self, heads, width, tokens, ranks, copies):
        self.heads, self.width, self.tokens = heads, width, tokens
        self.ranks, self.copies = ranks, copies
        self.groups = ranks // 4
        per_copy = heads // copies if heads % copies == 0 else 0
        self.chunks = 2 if per_copy and per_copy % 2 == 0 and self.groups % 2 == 0 else 1
        self.in_chunk = heads // self.chunks
        self.quarter = self.in_chunk // 4
        self.run = per_copy // self.chunks if self.chunks > 1 else self.in_chunk
        self.stride = per_copy if self.chunks > 1 else 0
        self.height = heads * width // (copies * ranks)
        self.factor = 1.0 / math.sqrt(width * tokens * ranks)
        self.norm = 1.0 / math.sqrt(copies * tokens * ranks)

    def head(self, chunk, place):
        return (place // self.run) * self.stride + chunk * self.run + place % self.run


def device_place():
    index = lax.axis_index("context")
    return index % 2, (index // 2) % 2, index // 4


def dot(left, right, left_dim=1, right_dim=0):
    return lax.dot_general(
        left, right, (((left_dim,), (right_dim,)), ((), ())), preferred_element_type=F32
    )


def call(body, operands, shapes, flops, scratch, copies, aliases=None):
    moved = sum(x.size * x.dtype.itemsize for x in list(operands) + list(shapes))
    anywhere = pl.BlockSpec(memory_space=pl.ANY)
    return pl.pallas_call(
        body,
        out_shape=shapes,
        in_specs=[anywhere] * len(operands),
        out_specs=[anywhere] * len(shapes),
        scratch_shapes=list(scratch) + [pltpu.SemaphoreType.DMA((copies,))],
        input_output_aliases=aliases or {},
        compiler_params=pltpu.CompilerParams(vmem_limit_bytes=VMEM_LIMIT),
        cost_estimate=pl.CostEstimate(flops=flops, bytes_accessed=moved, transcendentals=0),
    )(*operands)


class Copies:
    def __init__(self, sems):
        self.sems, self.used = sems, 0

    def start(self, source, target):
        copy = pltpu.make_async_copy(source, target, self.sems.at[self.used])
        self.used += 1
        copy.start()
        return copy


def wait(copies):
    for copy in copies:
        copy.wait()


def matmuls(plan, count):
    return 2 * count * plan.tokens * plan.width * plan.width


def load_chunk(plan, copies, chunk, offset, row_refs, maps_ref, row_bufs, maps_buf):
    width, started = plan.width, []
    for first in range(0, plan.in_chunk, plan.run):
        head = plan.head(chunk, first)
        source, target = pl.ds(head, plan.run), pl.ds(offset + first, plan.run)
        started.append(copies.start(maps_ref.at[source], maps_buf.at[target]))
        source = pl.ds(head * width, plan.run * width)
        target = pl.ds((offset + first) * width, plan.run * width)
        for ref, buf in zip(row_refs, row_bufs):
            started.append(copies.start(ref.at[:, source], buf.at[:, target]))
    return started


def chunk_copies(plan):
    return 5 * (plan.in_chunk // plan.run)


def row_scratch(plan, count):
    rows = [pltpu.VMEM((plan.tokens, count * plan.width), BF16)] * 4
    return rows + [pltpu.VMEM((count, plan.width, plan.width), BF16)]


def head_of(buf, place, width):
    return buf[:, place * width : (place + 1) * width]


def quarter_of(plan, place):
    core, chip, _ = device_place()
    low = place // plan.quarter
    core_turn = 1 - core if low % 2 else core
    chip_turn = 1 - chip if low // 2 else chip
    return core_turn, chip_turn, place % plan.quarter


def states_kernel(plan, *refs):
    row_refs, maps_ref = refs[:4], refs[4]
    out_refs = refs[5 : 5 + 2 * plan.chunks]
    row_bufs, maps_buf, out_buf, sems = refs[-7:-3], refs[-3], refs[-2], refs[-1]
    copies, width = Copies(sems), plan.width
    started = [
        load_chunk(plan, copies, chunk, chunk * plan.in_chunk, row_refs, maps_ref, row_bufs, maps_buf)
        for chunk in range(plan.chunks)
    ]
    q_buf, k_buf, v_buf, g_buf = row_bufs
    written = []
    for chunk in range(plan.chunks):
        wait(started[chunk])
        for first in range(0, plan.in_chunk, 4):
            places = range(first, first + 4)
            at = [chunk * plan.in_chunk + place for place in places]
            feats_key = [dot(head_of(k_buf, n, width), maps_buf[n]).astype(BF16) for n in at]
            feats_query = [dot(head_of(q_buf, n, width), maps_buf[n]).astype(BF16) for n in at]
            key_states = [
                dot(feat, head_of(v_buf, n, width), 0, 0) for feat, n in zip(feats_key, at)
            ]
            query_states = [
                dot(feat, head_of(g_buf, n, width), 0, 0) for feat, n in zip(feats_query, at)
            ]
            for place, key_state, query_state in zip(places, key_states, query_states):
                core_turn, chip_turn, i = quarter_of(plan, place)
                out_buf[core_turn, chunk, chip_turn, 0, i] = key_state
                out_buf[core_turn, chunk, chip_turn, 1, i] = query_state
        for turn in range(2):
            written.append(copies.start(out_buf.at[1 - turn, chunk], out_refs[2 * chunk + turn]))
    wait(written)


def block_states(plan, rows, maps):
    shape = (2, 2, plan.quarter, plan.width, plan.width)
    outs = call(
        functools.partial(states_kernel, plan),
        (*rows, maps),
        [jax.ShapeDtypeStruct(shape, F32)] * (2 * plan.chunks),
        matmuls(plan, 4 * plan.heads),
        row_scratch(plan, plan.heads) + [pltpu.VMEM((2, plan.chunks) + shape, F32)],
        plan.chunks * (chunk_copies(plan) + 2),
    )
    return outs[0::2], outs[1::2]


def causal_mask(tokens):
    row = lax.broadcasted_iota(jnp.int32, (tokens, tokens), 0)
    column = lax.broadcasted_iota(jnp.int32, (tokens, tokens), 1)
    return row >= column


def inner_kernel(plan, *refs):
    row_refs, maps_ref = refs[:4], refs[4]
    out_refs = refs[5 : 5 + 2 * plan.chunks]
    row_bufs, maps_buf = refs[-8:-4], refs[-4]
    base_buf, pair_buf, sems = refs[-3:]
    copies, width = Copies(sems), plan.width
    started = [
        load_chunk(plan, copies, chunk, chunk * plan.in_chunk, row_refs, maps_ref, row_bufs, maps_buf)
        for chunk in range(plan.chunks)
    ]
    causal = causal_mask(plan.tokens)
    written = []
    for chunk in range(plan.chunks):
        wait(started[chunk])
        for first in range(0, plan.in_chunk, 4):
            places = range(first, first + 4)
            at = [chunk * plan.in_chunk + place for place in places]
            queries, keys, values, grads = [
                [head_of(buf, n, width) for n in at] for buf in row_bufs
            ]
            scores = [
                jnp.where(causal, dot(grad, value, 1, 1), 0.0).astype(BF16)
                for grad, value in zip(grads, values)
            ]
            feats_query = [dot(x, maps_buf[n]).astype(BF16) for x, n in zip(queries, at)]
            feats_key = [dot(x, maps_buf[n]).astype(BF16) for x, n in zip(keys, at)]
            grads_a = [dot(s, feat).astype(BF16) for s, feat in zip(scores, feats_key)]
            grads_b = [dot(s, feat, 0, 0).astype(BF16) for s, feat in zip(scores, feats_query)]
            for n, place in enumerate(places):
                pair_buf[chunk, 0, place] = dot(queries[n], grads[n], 0, 0).astype(BF16)
                pair_buf[chunk, 1, place] = dot(keys[n], values[n], 0, 0).astype(BF16)
                base_buf[chunk, place] = dot(queries[n], grads_a[n], 0, 0) + dot(
                    keys[n], grads_b[n], 0, 0
                )
        written.append(copies.start(base_buf.at[chunk], out_refs[2 * chunk]))
        written.append(copies.start(pair_buf.at[chunk], out_refs[2 * chunk + 1]))
    wait(written)


def inner(plan, rows, maps):
    square = (plan.in_chunk, plan.width, plan.width)
    outs = call(
        functools.partial(inner_kernel, plan),
        (*rows, maps),
        [jax.ShapeDtypeStruct(square, F32), jax.ShapeDtypeStruct((2,) + square, BF16)]
        * plan.chunks,
        matmuls(plan, 9 * plan.heads),
        row_scratch(plan, plan.heads)
        + [
            pltpu.VMEM((plan.chunks,) + square, F32),
            pltpu.VMEM((plan.chunks, 2) + square, BF16),
        ],
        plan.chunks * (chunk_copies(plan) + 2),
    )
    return [outs[2 * chunk : 2 * chunk + 2] for chunk in range(plan.chunks)]


def load_states(copies, sources, state_buf, extra_buf):
    started = [
        copies.start(source, state_buf.at[n // 2, n % 2]) for n, source in enumerate(sources[:4])
    ]
    return started + [copies.start(sources[4], extra_buf)]


def finish_states(plan, state_buf, extra_buf):
    core, _, _ = device_place()
    for chip_turn in range(2):
        for side in range(2):
            wanted = core == 1 - side
            state_buf[0, chip_turn, side] += jnp.where(wanted, extra_buf[chip_turn, side], 0.0)


def state_scratch(plan):
    shape = (2, 2, plan.quarter, plan.width, plan.width)
    return [pltpu.VMEM((2,) + shape, F32), pltpu.VMEM(shape, F32)]


def term_kernel(plan, *refs):
    sources, base_ref, pair_ref = refs[:5], refs[5], refs[6]
    out_refs = refs[7:-6]
    state_buf, extra_buf, base_buf, pair_buf, out_buf, sems = refs[-6:]
    copies = Copies(sems)
    core, _, _ = device_place()
    wait(
        load_states(copies, sources, state_buf, extra_buf)
        + [copies.start(base_ref, base_buf), copies.start(pair_ref, pair_buf)]
    )
    finish_states(plan, state_buf, extra_buf)
    for first in range(0, plan.in_chunk, 4):
        places = range(first, first + 4)
        where = [quarter_of(plan, place) for place in places]
        products = [
            dot(pair_buf[side, place], state_buf[c, y, side, i].astype(BF16), 1, 1)
            for place, (c, y, i) in zip(places, where)
            for side in range(2)
        ]
        for n, place in enumerate(places):
            out_buf[place] = plan.factor * (
                base_buf[place] + products[2 * n] + products[2 * n + 1]
            )
    if len(out_refs) == 1:
        wait([copies.start(out_buf, out_refs[0])])
    else:
        half = plan.width // 2
        written = []
        for ref, turn in zip(out_refs, (1 - core, core)):
            rows = pl.ds(pl.multiple_of(turn * half, half), half)
            written.append(copies.start(out_buf.at[:, rows], ref))
        wait(written)


def maps_term(plan, states, extra, base, pair):
    width = plan.width
    square = (plan.in_chunk, width, width)
    in_halves = 2 * plan.height == width and plan.height % 8 == 0
    shapes = [(plan.in_chunk, width // 2, width)] * 2 if in_halves else [square]
    outs = call(
        functools.partial(term_kernel, plan),
        (*states, extra, base, pair),
        [jax.ShapeDtypeStruct(shape, F32) for shape in shapes],
        matmuls(plan, 2 * plan.in_chunk),
        state_scratch(plan)
        + [pltpu.VMEM(square, F32), pltpu.VMEM((2,) + square, BF16), pltpu.VMEM(square, F32)],
        9,
    )
    if in_halves:
        return outs
    core, _, _ = device_place()
    parts = outs[0].reshape(-1, 2, plan.height, width)
    return [
        lax.dynamic_index_in_dim(parts, turn, 1, keepdims=False) for turn in (1 - core, core)
    ]


def rows_kernel(plan, chunk, *refs):
    row_refs, maps_ref, sources = refs[:4], refs[4], refs[5:10]
    refs = refs[10 + (3 if chunk else 0) :]
    out_refs, row_bufs, maps_buf = refs[:3], refs[3:7], refs[7]
    state_buf, extra_buf, out_bufs, sems = refs[8], refs[9], refs[10:13], refs[13]
    copies, width = Copies(sems), plan.width
    started = load_states(copies, sources, state_buf, extra_buf)
    started += load_chunk(plan, copies, chunk, 0, row_refs, maps_ref, row_bufs, maps_buf)
    causal = causal_mask(plan.tokens)
    wait(started)
    finish_states(plan, state_buf, extra_buf)
    for first in range(0, plan.in_chunk, 4):
        places = range(first, first + 4)
        queries, keys, values, grads = [
            [head_of(buf, place, width) for place in places] for buf in row_bufs
        ]
        where = [quarter_of(plan, place) for place in places]
        prefixes = [state_buf[c, y, 0, i].astype(BF16) for c, y, i in where]
        suffixes = [state_buf[c, y, 1, i].astype(BF16) for c, y, i in where]
        matrices = [maps_buf[place] for place in places]
        scores_gv = [
            jnp.where(causal, dot(grad, value, 1, 1), 0.0).astype(BF16)
            for grad, value in zip(grads, values)
        ]
        feats_query = [dot(x, matrix).astype(BF16) for x, matrix in zip(queries, matrices)]
        feats_key = [dot(x, matrix).astype(BF16) for x, matrix in zip(keys, matrices)]
        scores_ab = [
            jnp.where(causal, dot(left, right, 1, 1), 0.0).astype(BF16)
            for left, right in zip(feats_query, feats_key)
        ]
        grads_a = [
            (plan.factor * (dot(score, feat) + dot(grad, prefix, 1, 1))).astype(BF16)
            for score, feat, grad, prefix in zip(scores_gv, feats_key, grads, prefixes)
        ]
        grads_b = [
            (plan.factor * (dot(score, feat, 0, 0) + dot(value, suffix, 1, 1))).astype(BF16)
            for score, feat, value, suffix in zip(scores_gv, feats_query, values, suffixes)
        ]
        for n, place in enumerate(places):
            at = slice(place * width, (place + 1) * width)
            out_bufs[0][:, at] = dot(grads_a[n], matrices[n], 1, 1).astype(BF16)
            out_bufs[1][:, at] = dot(grads_b[n], matrices[n], 1, 1).astype(BF16)
            value_grad = dot(scores_ab[n], grads[n], 0, 0) + dot(feats_key[n], suffixes[n])
            out_bufs[2][:, at] = (plan.factor * value_grad).astype(BF16)
    written = []
    for first in range(0, plan.in_chunk, plan.run):
        source = pl.ds(first * width, plan.run * width)
        target = pl.ds(plan.head(chunk, first) * width, plan.run * width)
        for buf, ref in zip(out_bufs, out_refs):
            written.append(copies.start(buf.at[:, source], ref.at[:, target]))
    wait(written)


def output_rows(plan, chunk, rows, maps, states, extra, done):
    shape = jax.ShapeDtypeStruct((plan.tokens, plan.heads * plan.width), BF16)
    narrow = [pltpu.VMEM((plan.tokens, plan.in_chunk * plan.width), BF16)] * 3
    return call(
        functools.partial(rows_kernel, plan, chunk),
        (*rows, maps, *states, extra, *done),
        [shape] * 3,
        matmuls(plan, 12 * plan.in_chunk),
        row_scratch(plan, plan.in_chunk) + state_scratch(plan) + narrow,
        2 * chunk_copies(plan) + 5,
        {10: 0, 11: 1, 12: 2} if done else None,
    )


def swap_core(plan, state):
    return lax.ppermute(state, "context", [(i, i ^ 1) for i in range(plan.ranks)])


def swap_chip(plan, state):
    return lax.ppermute(state, "context", [(i, i ^ 2) for i in range(plan.ranks)])


def chain_swap(plan, state, hop):
    mirror = plan.groups - 1 - hop
    steps = [(i, i ^ 1) for i in range(plan.ranks)]
    for low in range(4):
        for left in (hop, mirror - 1):
            a, b = 4 * left + low, 4 * left + 4 + low
            steps[a], steps[b] = (a, b), (b, a)
    return lax.ppermute(state, "context", steps)


def chain_split(plan, state, hop):
    mirror = plan.groups - 1 - hop
    up = [(4 * hop + low, 4 * hop + 4 + low) for low in range(4)]
    down = [(4 * mirror + low, 4 * mirror - 4 + low) for low in range(4)]
    return lax.ppermute(state[0], "context", up), lax.ppermute(state[1], "context", down)


def plane_sums(plan, halves):
    _, chip, _ = device_place()
    replica = lax.axis_index("dp")
    ranks, copies, width = plan.ranks, plan.copies, plan.width
    totals = [half.reshape(copies, -1, 2, plan.height, width) for half in halves]

    def plane_part(target_replica, target_chip):
        parts = []
        for total in totals:
            some = lax.dynamic_index_in_dim(total, target_replica, 0, keepdims=False)
            parts.append(lax.dynamic_index_in_dim(some, target_chip, 1, keepdims=False))
        return jnp.concatenate(parts, axis=0)

    plane = plane_part(replica, chip)
    for turn in range(copies):
        for flip in range(2):
            if turn == 0 and flip == 0:
                continue
            steps = [
                (r * ranks + i, ((r + turn) % copies) * ranks + (i ^ (2 * flip)))
                for r in range(copies)
                for i in range(ranks)
            ]
            sent = plane_part((replica + turn) % copies, (chip + flip) % 2)
            plane = plane + lax.ppermute(sent, ("dp", "context"), steps)
    return plane


def group_sum(plan, plane):
    _, _, group = device_place()
    result = lax.dynamic_index_in_dim(plane, group, 0, keepdims=False)
    for turn in range(1, plan.groups):
        steps = [(i, (i + 4 * turn) % plan.ranks) for i in range(plan.ranks)]
        sent = lax.dynamic_index_in_dim(plane, (group + turn) % plan.groups, 0, keepdims=False)
        result = result + lax.ppermute(sent, "context", steps)
    return result


def scan_groups(plan, group_state):
    _, _, group = device_place()
    chunks, hops = range(plan.chunks), plan.groups - 1
    before = [jnp.zeros_like(x) for x in group_state]
    if plan.groups % 2:
        for chunk in chunks:
            for hop in range(hops):
                up, down = chain_split(plan, before[chunk] + group_state[chunk], hop)
                before[chunk] = before[chunk] + jnp.stack([up, down])
        return before
    got = [[] for _ in chunks]

    def collect(chunk):
        prefix, suffix = before[chunk]
        for hop in range(hops):
            prefix = jnp.where(group == hop + 1, got[chunk][hop], prefix)
            suffix = jnp.where(group == hops - 1 - hop, got[chunk][hop], suffix)
        before[chunk] = jnp.stack([prefix, suffix])

    for stage in range(hops + plan.chunks - 1):
        for chunk in chunks:
            hop = stage - chunk
            if not 0 <= hop < hops:
                continue
            send = jnp.where(group == hop, group_state[chunk][0], group_state[chunk][1])
            if hop:
                send = send + got[chunk][-1]
            if chunk:
                send, got[0][hop] = lax.optimization_barrier((send, got[0][hop]))
            if chunk and hop == hops - 1:
                send, before[0] = lax.optimization_barrier((send, before[0]))
            got[chunk].append(chain_swap(plan, send, hop))
        if stage >= hops - 1:
            collect(stage - hops + 1)
    return before


def per_device(queries, key_rows, value_rows, out_grad, maps):
    tokens = queries.shape[1]
    heads, width, _ = maps.shape
    plan = Plan(heads, width, tokens, lax.axis_size("context"), lax.axis_size("dp"))
    rows = [x.reshape(tokens, heads * width) for x in (queries, key_rows, value_rows, out_grad)]
    core, chip, _ = device_place()
    side = jnp.arange(2).reshape(2, 1, 1, 1)
    chunks = range(plan.chunks)

    sent, kept = block_states(plan, rows, maps)
    from_core = [swap_core(plan, sent[chunk]) for chunk in chunks]
    total, from_chip, group_state = [], [], []
    for chunk in chunks:
        given = kept[chunk][1] + from_core[chunk][1]
        if chunk:
            terms = inner(plan, rows, maps)
            given, from_chip[-1], terms = lax.optimization_barrier((given, from_chip[-1], terms))
        total.append(kept[chunk][0] + from_core[chunk][0])
        from_chip.append(swap_chip(plan, given))
        group_state.append(total[chunk] + from_chip[chunk])
    if plan.chunks == 1:
        terms = inner(plan, rows, maps)
    before = scan_groups(plan, group_state)

    halves, done = [], ()
    for chunk in chunks:
        mate = before[chunk] + jnp.where(side == chip, total[chunk], 0.0)
        states = [
            before[chunk] + jnp.where(side != chip, from_chip[chunk], 0.0),
            swap_chip(plan, mate),
        ]
        if done:
            states[1], done = lax.optimization_barrier((states[1], done))
        states += [
            swap_core(plan, state + jnp.where(side == core, kept[chunk][turn], 0.0))
            for turn, state in enumerate(states)
        ]
        for_mate, own = maps_term(plan, states, from_core[chunk], *terms[chunk])
        halves.append(own + swap_core(plan, for_mate))
        done = output_rows(plan, chunk, rows, maps, states, from_core[chunk], done)
    plane = plane_sums(plan, halves)
    plane, done = lax.optimization_barrier((plane, done))
    query_grad, key_grad, value_grad = done
    maps_grad = group_sum(plan, plane) * plan.norm
    return (query_grad[None], key_grad[None], value_grad[None], maps_grad)


def solution(mesh):
    in_specs = (
        P("dp", "context", None),
        P("dp", "context", None),
        P("dp", "context", None),
        P("dp", "context", None),
        P(),
    )
    out_specs = (
        P("dp", "context", None),
        P("dp", "context", None),
        P("dp", "context", None),
        P(("dp", "context"), None),
    )
    return jax.shard_map(
        per_device, mesh=mesh, in_specs=in_specs, out_specs=out_specs, check_vma=False
    )
```

```python
import functools
import math

import jax
import jax.numpy as jnp
from jax import lax
from jax.experimental import pallas as pl
from jax.experimental.pallas import tpu as pltpu
from jax.sharding import PartitionSpec as P

F32 = jnp.float32
BF16 = jnp.bfloat16
VMEM_LIMIT = 51 * 1024 * 1024
SMALL_LIMIT = 16 * 1024 * 1024


class Plan:
    def __init__(self, heads, width, tokens, ranks, copies):
        self.heads, self.width, self.tokens = heads, width, tokens
        self.ranks, self.copies = ranks, copies
        self.groups = ranks // 4
        per_copy = heads // copies if heads % copies == 0 else 0
        self.chunks = 2 if per_copy and per_copy % 2 == 0 and self.groups % 2 == 0 else 1
        self.in_chunk = heads // self.chunks
        self.quarter = self.in_chunk // 4
        self.run = per_copy // self.chunks if self.chunks > 1 else self.in_chunk
        self.stride = per_copy if self.chunks > 1 else 0
        self.height = heads * width // (copies * ranks)
        self.factor = 1.0 / math.sqrt(width * tokens * ranks)
        self.norm = 1.0 / math.sqrt(copies * tokens * ranks)

    def head(self, chunk, place):
        return (place // self.run) * self.stride + chunk * self.run + place % self.run


def device_place():
    index = lax.axis_index("context")
    return index % 2, (index // 2) % 2, index // 4


def dot(left, right, left_dim=1, right_dim=0):
    return lax.dot_general(
        left, right, (((left_dim,), (right_dim,)), ((), ())), preferred_element_type=F32
    )


def call(body, operands, shapes, flops, scratch, copies, aliases=None, near=(), near_out=(), limit=VMEM_LIMIT):
    moved = sum(x.size * x.dtype.itemsize for x in list(operands) + list(shapes))

    def specs(count, in_vmem):
        return [
            pl.BlockSpec(memory_space=pltpu.VMEM if n in in_vmem else pl.ANY) for n in range(count)
        ]

    return pl.pallas_call(
        body,
        out_shape=shapes,
        in_specs=specs(len(operands), near),
        out_specs=specs(len(shapes), near_out),
        scratch_shapes=list(scratch) + [pltpu.SemaphoreType.DMA((copies,))],
        input_output_aliases=aliases or {},
        compiler_params=pltpu.CompilerParams(vmem_limit_bytes=limit),
        cost_estimate=pl.CostEstimate(flops=flops, bytes_accessed=moved, transcendentals=0),
    )(*operands)


class Copies:
    def __init__(self, sems):
        self.sems, self.used = sems, 0

    def start(self, source, target):
        copy = pltpu.make_async_copy(source, target, self.sems.at[self.used])
        self.used += 1
        copy.start()
        return copy


def wait(copies):
    for copy in copies:
        copy.wait()


def matmuls(plan, count):
    return 2 * count * plan.tokens * plan.width * plan.width


def load_chunk(plan, copies, chunk, offset, row_refs, maps_ref, row_bufs, maps_buf):
    width, started = plan.width, []
    for first in range(0, plan.in_chunk, plan.run):
        head = plan.head(chunk, first)
        source, target = pl.ds(head, plan.run), pl.ds(offset + first, plan.run)
        started.append(copies.start(maps_ref.at[source], maps_buf.at[target]))
        source = pl.ds(head * width, plan.run * width)
        target = pl.ds((offset + first) * width, plan.run * width)
        for ref, buf in zip(row_refs, row_bufs):
            started.append(copies.start(ref.at[:, source], buf.at[:, target]))
    return started


def chunk_copies(plan):
    return 5 * (plan.in_chunk // plan.run)


def row_scratch(plan, count):
    rows = [pltpu.VMEM((plan.tokens, count * plan.width), BF16)] * 4
    return rows + [pltpu.VMEM((count, plan.width, plan.width), BF16)]


def head_of(buf, place, width):
    return buf[:, place * width : (place + 1) * width]


def quarter_of(plan, place):
    core, chip, _ = device_place()
    low = place // plan.quarter
    core_turn = 1 - core if low % 2 else core
    chip_turn = 1 - chip if low // 2 else chip
    return core_turn, chip_turn, place % plan.quarter


def states_kernel(plan, chunk, *refs):
    row_refs, maps_ref, sent_ref, kept_ref, given_ref = refs[:4], refs[4], refs[5], refs[6], refs[7]
    row_bufs, maps_buf, kept_buf, sems = refs[8:12], refs[12], refs[13], refs[14]
    copies, width = Copies(sems), plan.width
    core, _, _ = device_place()
    started = load_chunk(plan, copies, chunk, 0, row_refs, maps_ref, row_bufs, maps_buf)
    q_buf, k_buf, v_buf, g_buf = row_bufs
    size = 5 * max(1, 4 // plan.run)
    for first in range(0, plan.in_chunk, 4):
        places = range(first, first + 4)
        wait(started[:size])
        started = started[size:]
        feats_key = [dot(head_of(k_buf, n, width), maps_buf[n]).astype(BF16) for n in places]
        feats_query = [dot(head_of(q_buf, n, width), maps_buf[n]).astype(BF16) for n in places]
        key_states = [
            dot(feat, head_of(v_buf, n, width), 0, 0) for feat, n in zip(feats_key, places)
        ]
        query_states = [
            dot(feat, head_of(g_buf, n, width), 0, 0) for feat, n in zip(feats_query, places)
        ]
        for place, key_state, query_state in zip(places, key_states, query_states):
            core_turn, chip_turn, i = quarter_of(plan, place)

            @pl.when(core_turn == 1)
            def _():
                sent_ref[chip_turn, 0, i] = key_state
                sent_ref[chip_turn, 1, i] = query_state

            @pl.when(core_turn == 0)
            def _():
                kept_buf[chip_turn, 0, i] = key_state
                kept_buf[chip_turn, 1, i] = query_state
    written = copies.start(kept_buf, kept_ref)
    given_ref[...] = kept_buf[1]
    written.wait()


def block_states(plan, chunk, rows, maps):
    shape = (2, 2, plan.quarter, plan.width, plan.width)
    state = jax.ShapeDtypeStruct(shape, F32)
    return call(
        functools.partial(states_kernel, plan, chunk),
        (*rows, maps),
        [state, state, jax.ShapeDtypeStruct(shape[1:], F32)],
        matmuls(plan, 4 * plan.in_chunk),
        row_scratch(plan, plan.in_chunk) + [pltpu.VMEM(shape, F32)],
        chunk_copies(plan) + 1,
        near_out=(0, 2),
    )


def causal_mask(tokens):
    row = lax.broadcasted_iota(jnp.int32, (tokens, tokens), 0)
    column = lax.broadcasted_iota(jnp.int32, (tokens, tokens), 1)
    return row >= column


def inner_kernel(plan, *refs):
    row_refs, maps_ref = refs[:4], refs[4]
    out_refs = refs[5 : 5 + 2 * plan.chunks]
    row_bufs, maps_buf = refs[-8:-4], refs[-4]
    base_buf, pair_buf, sems = refs[-3:]
    copies, width = Copies(sems), plan.width
    started = [
        load_chunk(plan, copies, chunk, chunk * plan.in_chunk, row_refs, maps_ref, row_bufs, maps_buf)
        for chunk in range(plan.chunks)
    ]
    causal = causal_mask(plan.tokens)
    written = []
    for chunk in range(plan.chunks):
        wait(started[chunk])
        for first in range(0, plan.in_chunk, 4):
            places = range(first, first + 4)
            at = [chunk * plan.in_chunk + place for place in places]
            queries, keys, values, grads = [
                [head_of(buf, n, width) for n in at] for buf in row_bufs
            ]
            scores = [
                jnp.where(causal, dot(grad, value, 1, 1), 0.0).astype(BF16)
                for grad, value in zip(grads, values)
            ]
            feats_query = [dot(x, maps_buf[n]).astype(BF16) for x, n in zip(queries, at)]
            feats_key = [dot(x, maps_buf[n]).astype(BF16) for x, n in zip(keys, at)]
            grads_a = [dot(s, feat).astype(BF16) for s, feat in zip(scores, feats_key)]
            grads_b = [dot(s, feat, 0, 0).astype(BF16) for s, feat in zip(scores, feats_query)]
            for n, place in enumerate(places):
                pair_buf[chunk, 0, place] = dot(queries[n], grads[n], 0, 0).astype(BF16)
                pair_buf[chunk, 1, place] = dot(keys[n], values[n], 0, 0).astype(BF16)
                base_buf[chunk, place] = dot(queries[n], grads_a[n], 0, 0) + dot(
                    keys[n], grads_b[n], 0, 0
                )
        written.append(copies.start(base_buf.at[chunk], out_refs[2 * chunk]))
        written.append(copies.start(pair_buf.at[chunk], out_refs[2 * chunk + 1]))
    wait(written)


def inner(plan, rows, maps):
    square = (plan.in_chunk, plan.width, plan.width)
    outs = call(
        functools.partial(inner_kernel, plan),
        (*rows, maps),
        [jax.ShapeDtypeStruct(square, F32), jax.ShapeDtypeStruct((2,) + square, BF16)]
        * plan.chunks,
        matmuls(plan, 9 * plan.heads),
        row_scratch(plan, plan.heads)
        + [
            pltpu.VMEM((plan.chunks,) + square, F32),
            pltpu.VMEM((plan.chunks, 2) + square, BF16),
        ],
        plan.chunks * (chunk_copies(plan) + 2),
    )
    return [outs[2 * chunk : 2 * chunk + 2] for chunk in range(plan.chunks)]


def finish_states(plan, state_refs, extra_buf, state_buf):
    core, _, _ = device_place()
    for core_turn in range(2):
        for chip_turn in range(2):
            for side in range(2):
                state = state_refs[2 * core_turn + chip_turn][side]
                if core_turn == 0:
                    wanted = core == 1 - side
                    state = state + jnp.where(wanted, extra_buf[chip_turn, side], 0.0)
                state_buf[core_turn, chip_turn, side] = state.astype(BF16)


def state_scratch(plan):
    shape = (2, 2, plan.quarter, plan.width, plan.width)
    return [pltpu.VMEM(shape, F32), pltpu.VMEM((2,) + shape, BF16)]


def term_kernel(plan, *refs):
    state_refs, extra_ref, base_ref, pair_ref = refs[:4], refs[4], refs[5], refs[6]
    out_refs = refs[7:-5]
    extra_buf, state_buf, base_buf, pair_buf, sems = refs[-5:]
    copies = Copies(sems)
    core, _, _ = device_place()
    extra_copy = copies.start(extra_ref, extra_buf)
    others = [copies.start(pair_ref, pair_buf), copies.start(base_ref, base_buf)]
    extra_copy.wait()
    finish_states(plan, state_refs, extra_buf, state_buf)
    wait(others)
    half = plan.width // 2
    for first in range(0, plan.in_chunk, 4):
        places = range(first, first + 4)
        where = [quarter_of(plan, place) for place in places]
        products = [
            dot(pair_buf[side, place], state_buf[c, y, side, i], 1, 1)
            for place, (c, y, i) in zip(places, where)
            for side in range(2)
        ]
        for n, place in enumerate(places):
            term = plan.factor * (base_buf[place] + products[2 * n] + products[2 * n + 1])
            if len(out_refs) == 1:
                out_refs[0][place] = term
            else:
                out_refs[0][place] = jnp.where(core == 0, term[half:], term[:half])
                out_refs[1][place] = jnp.where(core == 0, term[:half], term[half:])


def maps_term(plan, states, extra, base, pair):
    width = plan.width
    square = (plan.in_chunk, width, width)
    in_halves = 2 * plan.height == width and plan.height % 8 == 0
    shapes = [(plan.in_chunk, width // 2, width)] * 2 if in_halves else [square]
    outs = call(
        functools.partial(term_kernel, plan),
        (*states, extra, base, pair),
        [jax.ShapeDtypeStruct(shape, F32) for shape in shapes],
        matmuls(plan, 2 * plan.in_chunk),
        state_scratch(plan) + [pltpu.VMEM(square, F32), pltpu.VMEM((2,) + square, BF16)],
        3,
        near=range(4),
        near_out=range(2),
        limit=SMALL_LIMIT,
    )
    if in_halves:
        return outs
    core, _, _ = device_place()
    parts = outs[0].reshape(-1, 2, plan.height, width)
    return [
        lax.dynamic_index_in_dim(parts, turn, 1, keepdims=False) for turn in (1 - core, core)
    ]


def rows_kernel(plan, chunk, *refs):
    state_refs, extra_ref, row_refs, maps_ref = refs[:4], refs[4], refs[5:9], refs[9]
    refs = refs[10 + (3 if chunk else 0) :]
    out_refs, row_bufs, maps_buf = refs[:3], refs[3:7], refs[7]
    extra_buf, state_buf, out_bufs, sems = refs[8], refs[9], refs[10:13], refs[13]
    copies, width = Copies(sems), plan.width
    extra_copy = copies.start(extra_ref, extra_buf)
    started = load_chunk(plan, copies, chunk, 0, row_refs, maps_ref, row_bufs, maps_buf)
    causal = causal_mask(plan.tokens)
    extra_copy.wait()
    finish_states(plan, state_refs, extra_buf, state_buf)
    written = []
    size = 5 * max(1, 4 // plan.run)
    for first in range(0, plan.in_chunk, 4):
        places = range(first, first + 4)
        wait(started[:size])
        started = started[size:]
        queries, keys, values, grads = [
            [head_of(buf, place, width) for place in places] for buf in row_bufs
        ]
        where = [quarter_of(plan, place) for place in places]
        prefixes = [state_buf[c, y, 0, i] for c, y, i in where]
        suffixes = [state_buf[c, y, 1, i] for c, y, i in where]
        matrices = [maps_buf[place] for place in places]
        scores_gv = [
            jnp.where(causal, dot(grad, value, 1, 1), 0.0).astype(BF16)
            for grad, value in zip(grads, values)
        ]
        feats_query = [dot(x, matrix).astype(BF16) for x, matrix in zip(queries, matrices)]
        feats_key = [dot(x, matrix).astype(BF16) for x, matrix in zip(keys, matrices)]
        scores_ab = [
            jnp.where(causal, dot(left, right, 1, 1), 0.0).astype(BF16)
            for left, right in zip(feats_query, feats_key)
        ]
        grads_a = [
            (plan.factor * (dot(score, feat) + dot(grad, prefix, 1, 1))).astype(BF16)
            for score, feat, grad, prefix in zip(scores_gv, feats_key, grads, prefixes)
        ]
        grads_b = [
            (plan.factor * (dot(score, feat, 0, 0) + dot(value, suffix, 1, 1))).astype(BF16)
            for score, feat, value, suffix in zip(scores_gv, feats_query, values, suffixes)
        ]
        for n, place in enumerate(places):
            at = slice(place * width, (place + 1) * width)
            out_bufs[0][:, at] = dot(grads_a[n], matrices[n], 1, 1).astype(BF16)
            out_bufs[1][:, at] = dot(grads_b[n], matrices[n], 1, 1).astype(BF16)
            value_grad = dot(scores_ab[n], grads[n], 0, 0) + dot(feats_key[n], suffixes[n])
            out_bufs[2][:, at] = (plan.factor * value_grad).astype(BF16)
        for part in range(first, first + 4, min(4, plan.run)):
            count = min(4, plan.run)
            source = pl.ds(part * width, count * width)
            target = pl.ds(plan.head(chunk, part) * width, count * width)
            for buf, ref in zip(out_bufs, out_refs):
                written.append(copies.start(buf.at[:, source], ref.at[:, target]))
    wait(written)


def output_rows(plan, chunk, rows, maps, states, extra, done):
    shape = jax.ShapeDtypeStruct((plan.tokens, plan.heads * plan.width), BF16)
    narrow = [pltpu.VMEM((plan.tokens, plan.in_chunk * plan.width), BF16)] * 3
    return call(
        functools.partial(rows_kernel, plan, chunk),
        (*states, extra, *rows, maps, *done),
        [shape] * 3,
        matmuls(plan, 12 * plan.in_chunk),
        row_scratch(plan, plan.in_chunk) + state_scratch(plan) + narrow,
        chunk_copies(plan) + 3 * plan.in_chunk + 1,
        {10: 0, 11: 1, 12: 2} if done else None,
        near=range(4),
    )


def swap_core(plan, state):
    return lax.ppermute(state, "context", [(i, i ^ 1) for i in range(plan.ranks)])


def swap_chip(plan, state):
    return lax.ppermute(state, "context", [(i, i ^ 2) for i in range(plan.ranks)])


def chain_swap(plan, state, hop):
    mirror = plan.groups - 1 - hop
    steps = [(i, i ^ 1) for i in range(plan.ranks)]
    for low in range(4):
        for left in (hop, mirror - 1):
            a, b = 4 * left + low, 4 * left + 4 + low
            steps[a], steps[b] = (a, b), (b, a)
    return lax.ppermute(state, "context", steps)


def chain_split(plan, state, hop):
    mirror = plan.groups - 1 - hop
    up = [(4 * hop + low, 4 * hop + 4 + low) for low in range(4)]
    down = [(4 * mirror + low, 4 * mirror - 4 + low) for low in range(4)]
    return lax.ppermute(state[0], "context", up), lax.ppermute(state[1], "context", down)


def plane_sums(plan, halves):
    _, chip, _ = device_place()
    replica = lax.axis_index("dp")
    ranks, copies, width = plan.ranks, plan.copies, plan.width
    totals = [half.reshape(copies, -1, 2, plan.height, width) for half in halves]

    def plane_part(target_replica, target_chip):
        parts = []
        for total in totals:
            some = lax.dynamic_index_in_dim(total, target_replica, 0, keepdims=False)
            parts.append(lax.dynamic_index_in_dim(some, target_chip, 1, keepdims=False))
        return jnp.concatenate(parts, axis=0)

    plane = plane_part(replica, chip)
    for turn in range(copies):
        for flip in range(2):
            if turn == 0 and flip == 0:
                continue
            steps = [
                (r * ranks + i, ((r + turn) % copies) * ranks + (i ^ (2 * flip)))
                for r in range(copies)
                for i in range(ranks)
            ]
            sent = plane_part((replica + turn) % copies, (chip + flip) % 2)
            plane = plane + lax.ppermute(sent, ("dp", "context"), steps)
    return plane


def group_sum(plan, plane):
    _, _, group = device_place()
    result = lax.dynamic_index_in_dim(plane, group, 0, keepdims=False)
    for turn in range(1, plan.groups):
        steps = [(i, (i + 4 * turn) % plan.ranks) for i in range(plan.ranks)]
        sent = lax.dynamic_index_in_dim(plane, (group + turn) % plan.groups, 0, keepdims=False)
        result = result + lax.ppermute(sent, "context", steps)
    return result


def select_group(plan, got):
    _, _, group = device_place()
    prefix = suffix = jnp.zeros_like(got[0])
    for hop, state in enumerate(got):
        prefix = jnp.where(group == hop + 1, state, prefix)
        suffix = jnp.where(group == plan.groups - 2 - hop, state, suffix)
    return jnp.stack([prefix, suffix])


def scan_alone(plan, group_state):
    before = jnp.zeros_like(group_state)
    for hop in range(plan.groups - 1):
        if plan.groups % 2:
            up, down = chain_split(plan, before + group_state, hop)
            before = before + jnp.stack([up, down])
    return before


def per_device(queries, key_rows, value_rows, out_grad, maps):
    tokens = queries.shape[1]
    heads, width, _ = maps.shape
    plan = Plan(heads, width, tokens, lax.axis_size("context"), lax.axis_size("dp"))
    rows = [x.reshape(tokens, heads * width) for x in (queries, key_rows, value_rows, out_grad)]
    core, chip, group = device_place()
    side = jnp.arange(2).reshape(2, 1, 1, 1)
    chunks, hops, tie = range(plan.chunks), plan.groups - 1, lax.optimization_barrier

    kept, from_core, total, from_chip, group_state = [], [], [], [], []
    for chunk in chunks:
        sent, kept_here, given = block_states(plan, chunk, rows, maps)
        kept.append(kept_here)
        from_core.append(swap_core(plan, sent))
        given = given + from_core[chunk][1]
        if chunk == plan.chunks - 1:
            terms = inner(plan, rows, maps)
        if chunk:
            given, from_chip[-1], terms = tie((given, from_chip[-1], terms))
        total.append(kept_here[0] + from_core[chunk][0])
        from_chip.append(swap_chip(plan, given))
        group_state.append(total[chunk] + from_chip[chunk])

    def for_other_chip(chunk, before):
        return before + jnp.where(side == chip, total[chunk], 0.0)

    before, got, down = [None] * plan.chunks, [[] for _ in chunks], [None] * plan.chunks
    if plan.groups % 2:
        for chunk in chunks:
            before[chunk] = scan_alone(plan, group_state[chunk])
            down[chunk] = swap_chip(plan, for_other_chip(chunk, before[chunk]))
    else:
        for stage in range(hops + plan.chunks - 1):
            for chunk in chunks:
                hop = stage - chunk
                if not 0 <= hop < hops:
                    continue
                send = jnp.where(group == hop, group_state[chunk][0], group_state[chunk][1])
                if hop:
                    send = send + got[chunk][-1]
                if chunk and hop < hops - 1:
                    send, got[0][hop] = tie((send, got[0][hop]))
                if chunk and hop == hops - 1:
                    before[0] = select_group(plan, got[0])
                    mate = for_other_chip(0, before[0])
                    send, mate = tie((send, mate))
                    down[0] = swap_chip(plan, mate)
                got[chunk].append(chain_swap(plan, send, hop))
        last = plan.chunks - 1
        if last:
            got[last][-1], down[0] = tie((got[last][-1], down[0]))
        before[last] = select_group(plan, got[last])
        down[last] = swap_chip(plan, for_other_chip(last, before[last]))

    halves, done = [], ()
    for chunk in chunks:
        states = [before[chunk] + jnp.where(side != chip, from_chip[chunk], 0.0), down[chunk]]
        if done:
            states[1], done, halves = tie((states[1], done, halves))
        states += [
            swap_core(plan, state + jnp.where(side == core, kept[chunk][turn], 0.0))
            for turn, state in enumerate(states)
        ]
        for_mate, own = maps_term(plan, states, from_core[chunk], *terms[chunk])
        halves.append(own + swap_core(plan, for_mate))
        done = output_rows(plan, chunk, rows, maps, states, from_core[chunk], done)
    plane = plane_sums(plan, halves)
    plane, done = tie((plane, done))
    query_grad, key_grad, value_grad = done
    maps_grad = group_sum(plan, plane) * plan.norm
    return (query_grad[None], key_grad[None], value_grad[None], maps_grad)


def solution(mesh):
    in_specs = (
        P("dp", "context", None),
        P("dp", "context", None),
        P("dp", "context", None),
        P("dp", "context", None),
        P(),
    )
    out_specs = (
        P("dp", "context", None),
        P("dp", "context", None),
        P("dp", "context", None),
        P(("dp", "context"), None),
    )
    return jax.shard_map(
        per_device, mesh=mesh, in_specs=in_specs, out_specs=out_specs, check_vma=False
    )
```

```python
import functools
import math

import jax
import jax.numpy as jnp
from jax import lax
from jax.experimental import pallas as pl
from jax.experimental.pallas import tpu as pltpu
from jax.sharding import PartitionSpec as P

F32 = jnp.float32
BF16 = jnp.bfloat16
VMEM_LIMIT = 57 * 1024 * 1024
MIDDLE_LIMIT = 51 * 1024 * 1024
STATES_LIMIT = 53 * 1024 * 1024
SMALL_LIMIT = 16 * 1024 * 1024
LIGHT = 0.01


class Plan:
    def __init__(self, heads, width, tokens, ranks, copies):
        self.heads, self.width, self.tokens = heads, width, tokens
        self.ranks, self.copies = ranks, copies
        self.groups = ranks // 4
        per_copy = heads // copies if heads % copies == 0 else 0
        self.chunks = 2 if per_copy and per_copy % 2 == 0 and self.groups % 2 == 0 else 1
        self.in_chunk = heads // self.chunks
        self.quarter = self.in_chunk // 4
        self.run = per_copy // self.chunks if self.chunks > 1 else self.in_chunk
        self.stride = per_copy if self.chunks > 1 else 0
        self.height = heads * width // (copies * ranks)
        self.factor = 1.0 / math.sqrt(width * tokens * ranks)
        self.norm = 1.0 / math.sqrt(copies * tokens * ranks)

    def head(self, chunk, place):
        return (place // self.run) * self.stride + chunk * self.run + place % self.run


def device_place():
    index = lax.axis_index("context")
    return index % 2, (index // 2) % 2, index // 4


def dot(left, right, left_dim=1, right_dim=0):
    return lax.dot_general(
        left, right, (((left_dim,), (right_dim,)), ((), ())), preferred_element_type=F32
    )


def call(body, operands, shapes, flops, scratch, copies, aliases=None, near=(), near_out=(), limit=VMEM_LIMIT, weight=1.0):
    moved = sum(x.size * x.dtype.itemsize for x in list(operands) + list(shapes))

    def specs(count, in_vmem):
        return [
            pl.BlockSpec(memory_space=pltpu.VMEM if n in in_vmem else pltpu.HBM)
            for n in range(count)
        ]

    return pl.pallas_call(
        body,
        out_shape=shapes,
        in_specs=specs(len(operands), near),
        out_specs=specs(len(shapes), near_out),
        scratch_shapes=list(scratch) + [pltpu.SemaphoreType.DMA((copies,))],
        input_output_aliases=aliases or {},
        compiler_params=pltpu.CompilerParams(vmem_limit_bytes=limit),
        cost_estimate=pl.CostEstimate(
            flops=int(flops * weight), bytes_accessed=int(moved * weight), transcendentals=0
        ),
    )(*operands)


class Copies:
    def __init__(self, sems):
        self.sems, self.used = sems, 0

    def start(self, source, target):
        copy = pltpu.make_async_copy(source, target, self.sems.at[self.used])
        self.used += 1
        copy.start()
        return copy


def wait(copies):
    for copy in copies:
        copy.wait()


def matmuls(plan, count):
    return 2 * count * plan.tokens * plan.width * plan.width


def load_chunk(plan, copies, chunk, offset, row_refs, maps_ref, row_bufs, maps_buf):
    width, started = plan.width, []
    for first in range(0, plan.in_chunk, plan.run):
        head = plan.head(chunk, first)
        source, target = pl.ds(head, plan.run), pl.ds(offset + first, plan.run)
        started.append(copies.start(maps_ref.at[source], maps_buf.at[target]))
        source = pl.ds(head * width, plan.run * width)
        target = pl.ds((offset + first) * width, plan.run * width)
        for ref, buf in zip(row_refs, row_bufs):
            started.append(copies.start(ref.at[:, source], buf.at[:, target]))
    return started


def chunk_copies(plan):
    return 5 * (plan.in_chunk // plan.run)


def row_scratch(plan, count):
    rows = [pltpu.VMEM((plan.tokens, count * plan.width), BF16)] * 4
    return rows + [pltpu.VMEM((count, plan.width, plan.width), BF16)]


def head_of(buf, place, width):
    return buf[:, place * width : (place + 1) * width]


def quarter_of(plan, place):
    core, chip, _ = device_place()
    low = place // plan.quarter
    core_turn = 1 - core if low % 2 else core
    chip_turn = 1 - chip if low // 2 else chip
    return core_turn, chip_turn, place % plan.quarter


def states_kernel(plan, chunk, *refs):
    row_refs, maps_ref, sent_ref, kept_ref, given_ref = refs[:4], refs[4], refs[5], refs[6], refs[7]
    row_bufs, maps_buf, sems = refs[8:12], refs[12], refs[13]
    copies, width = Copies(sems), plan.width
    started = load_chunk(plan, copies, chunk, 0, row_refs, maps_ref, row_bufs, maps_buf)
    q_buf, k_buf, v_buf, g_buf = row_bufs
    size = 5 * max(1, 4 // plan.run)
    for first in range(0, plan.in_chunk, 4):
        places = range(first, first + 4)
        wait(started[:size])
        started = started[size:]
        feats_key = [dot(head_of(k_buf, n, width), maps_buf[n]).astype(BF16) for n in places]
        feats_query = [dot(head_of(q_buf, n, width), maps_buf[n]).astype(BF16) for n in places]
        key_states = [
            dot(feat, head_of(v_buf, n, width), 0, 0) for feat, n in zip(feats_key, places)
        ]
        query_states = [
            dot(feat, head_of(g_buf, n, width), 0, 0) for feat, n in zip(feats_query, places)
        ]
        for place, key_state, query_state in zip(places, key_states, query_states):
            core_turn, chip_turn, i = quarter_of(plan, place)

            @pl.when(core_turn == 1)
            def _():
                sent_ref[chip_turn, 0, i] = key_state
                sent_ref[chip_turn, 1, i] = query_state

            @pl.when(core_turn == 0)
            def _():
                kept_ref[chip_turn, 0, i] = key_state
                kept_ref[chip_turn, 1, i] = query_state
    given_ref[...] = kept_ref[1]


def block_states(plan, chunk, rows, maps):
    shape = (2, 2, plan.quarter, plan.width, plan.width)
    state = jax.ShapeDtypeStruct(shape, F32)
    return call(
        functools.partial(states_kernel, plan, chunk),
        (*rows, maps),
        [state, state, jax.ShapeDtypeStruct(shape[1:], F32)],
        matmuls(plan, 4 * plan.in_chunk),
        row_scratch(plan, plan.in_chunk),
        chunk_copies(plan),
        near_out=(0, 1, 2),
        limit=STATES_LIMIT,
    )


def causal_mask(tokens):
    row = lax.broadcasted_iota(jnp.int32, (tokens, tokens), 0)
    column = lax.broadcasted_iota(jnp.int32, (tokens, tokens), 1)
    return row >= column


def inner_kernel(plan, *refs):
    row_refs, maps_ref = refs[:4], refs[4]
    out_refs = refs[5 : 5 + 2 * plan.chunks]
    row_bufs, maps_buf = refs[-8:-4], refs[-4]
    base_buf, pair_buf, sems = refs[-3:]
    copies, width = Copies(sems), plan.width
    started = [
        load_chunk(plan, copies, chunk, chunk * plan.in_chunk, row_refs, maps_ref, row_bufs, maps_buf)
        for chunk in range(plan.chunks)
    ]
    causal = causal_mask(plan.tokens)
    written = []
    for chunk in range(plan.chunks):
        wait(started[chunk])
        for first in range(0, plan.in_chunk, 4):
            places = range(first, first + 4)
            at = [chunk * plan.in_chunk + place for place in places]
            queries, keys, values, grads = [
                [head_of(buf, n, width) for n in at] for buf in row_bufs
            ]
            scores = [
                jnp.where(causal, dot(grad, value, 1, 1), 0.0).astype(BF16)
                for grad, value in zip(grads, values)
            ]
            feats_query = [dot(x, maps_buf[n]).astype(BF16) for x, n in zip(queries, at)]
            feats_key = [dot(x, maps_buf[n]).astype(BF16) for x, n in zip(keys, at)]
            grads_a = [dot(s, feat).astype(BF16) for s, feat in zip(scores, feats_key)]
            grads_b = [dot(s, feat, 0, 0).astype(BF16) for s, feat in zip(scores, feats_query)]
            for n, place in enumerate(places):
                pair_buf[chunk, 0, place] = dot(queries[n], grads[n], 0, 0).astype(BF16)
                pair_buf[chunk, 1, place] = dot(keys[n], values[n], 0, 0).astype(BF16)
                base_buf[chunk, place] = dot(queries[n], grads_a[n], 0, 0) + dot(
                    keys[n], grads_b[n], 0, 0
                )
        written.append(copies.start(base_buf.at[chunk], out_refs[2 * chunk]))
        written.append(copies.start(pair_buf.at[chunk], out_refs[2 * chunk + 1]))
    wait(written)


def inner(plan, rows, maps):
    square = (plan.in_chunk, plan.width, plan.width)
    outs = call(
        functools.partial(inner_kernel, plan),
        (*rows, maps),
        [jax.ShapeDtypeStruct(square, F32), jax.ShapeDtypeStruct((2,) + square, BF16)]
        * plan.chunks,
        matmuls(plan, 9 * plan.heads),
        row_scratch(plan, plan.heads)
        + [
            pltpu.VMEM((plan.chunks,) + square, F32),
            pltpu.VMEM((plan.chunks, 2) + square, BF16),
        ],
        plan.chunks * (chunk_copies(plan) + 2),
    )
    return [outs[2 * chunk : 2 * chunk + 2] for chunk in range(plan.chunks)]


def finish_states(plan, state_refs, extra_buf, state_buf):
    core, _, _ = device_place()
    for core_turn in range(2):
        for chip_turn in range(2):
            for side in range(2):
                state = state_refs[2 * core_turn + chip_turn][side]
                if core_turn == 0:
                    wanted = core == 1 - side
                    state = state + jnp.where(wanted, extra_buf[chip_turn, side], 0.0)
                state_buf[core_turn, chip_turn, side] = state.astype(BF16)


def state_scratch(plan):
    shape = (2, 2, plan.quarter, plan.width, plan.width)
    return [pltpu.VMEM(shape, F32), pltpu.VMEM((2,) + shape, BF16)]


def term_kernel(plan, *refs):
    state_refs, extra_ref, base_ref, pair_ref = refs[:4], refs[4], refs[5], refs[6]
    out_refs = refs[7:-5]
    extra_buf, state_buf, base_buf, pair_buf, sems = refs[-5:]
    copies = Copies(sems)
    core, _, _ = device_place()
    extra_copy = copies.start(extra_ref, extra_buf)
    others = [copies.start(pair_ref, pair_buf), copies.start(base_ref, base_buf)]
    extra_copy.wait()
    finish_states(plan, state_refs, extra_buf, state_buf)
    wait(others)
    half = plan.width // 2
    for first in range(0, plan.in_chunk, 4):
        places = range(first, first + 4)
        where = [quarter_of(plan, place) for place in places]
        products = [
            dot(pair_buf[side, place], state_buf[c, y, side, i], 1, 1)
            for place, (c, y, i) in zip(places, where)
            for side in range(2)
        ]
        for n, place in enumerate(places):
            term = plan.factor * (base_buf[place] + products[2 * n] + products[2 * n + 1])
            if len(out_refs) == 1:
                out_refs[0][place] = term
            else:
                out_refs[0][place] = jnp.where(core == 0, term[half:], term[:half])
                out_refs[1][place] = jnp.where(core == 0, term[:half], term[half:])


def maps_term(plan, states, extra, base, pair):
    width = plan.width
    square = (plan.in_chunk, width, width)
    in_halves = 2 * plan.height == width and plan.height % 8 == 0
    shapes = [(plan.in_chunk, width // 2, width)] * 2 if in_halves else [square]
    outs = call(
        functools.partial(term_kernel, plan),
        (*states, extra, base, pair),
        [jax.ShapeDtypeStruct(shape, F32) for shape in shapes],
        matmuls(plan, 2 * plan.in_chunk),
        state_scratch(plan) + [pltpu.VMEM(square, F32), pltpu.VMEM((2,) + square, BF16)],
        3,
        near=range(4),
        near_out=range(2),
        limit=SMALL_LIMIT,
        weight=LIGHT,
    )
    if in_halves:
        return outs
    core, _, _ = device_place()
    parts = outs[0].reshape(-1, 2, plan.height, width)
    return [
        lax.dynamic_index_in_dim(parts, turn, 1, keepdims=False) for turn in (1 - core, core)
    ]


def rows_kernel(plan, chunk, *refs):
    state_refs, extra_ref, row_refs, maps_ref = refs[:4], refs[4], refs[5:9], refs[9]
    refs = refs[10 + (3 if chunk else 0) :]
    out_refs, row_bufs, maps_buf = refs[:3], refs[3:7], refs[7]
    extra_buf, state_buf, out_bufs, sems = refs[8], refs[9], refs[10:13], refs[13]
    copies, width = Copies(sems), plan.width
    extra_copy = copies.start(extra_ref, extra_buf)
    started = load_chunk(plan, copies, chunk, 0, row_refs, maps_ref, row_bufs, maps_buf)
    causal = causal_mask(plan.tokens)
    extra_copy.wait()
    finish_states(plan, state_refs, extra_buf, state_buf)
    written = []
    size = 5 * max(1, 4 // plan.run)
    for first in range(0, plan.in_chunk, 4):
        places = range(first, first + 4)
        wait(started[:size])
        started = started[size:]
        queries, keys, values, grads = [
            [head_of(buf, place, width) for place in places] for buf in row_bufs
        ]
        where = [quarter_of(plan, place) for place in places]
        prefixes = [state_buf[c, y, 0, i] for c, y, i in where]
        suffixes = [state_buf[c, y, 1, i] for c, y, i in where]
        matrices = [maps_buf[place] for place in places]
        scores_gv = [
            jnp.where(causal, dot(grad, value, 1, 1), 0.0).astype(BF16)
            for grad, value in zip(grads, values)
        ]
        feats_query = [dot(x, matrix).astype(BF16) for x, matrix in zip(queries, matrices)]
        feats_key = [dot(x, matrix).astype(BF16) for x, matrix in zip(keys, matrices)]
        scores_ab = [
            jnp.where(causal, dot(left, right, 1, 1), 0.0).astype(BF16)
            for left, right in zip(feats_query, feats_key)
        ]
        grads_a = [
            (plan.factor * (dot(score, feat) + dot(grad, prefix, 1, 1))).astype(BF16)
            for score, feat, grad, prefix in zip(scores_gv, feats_key, grads, prefixes)
        ]
        grads_b = [
            (plan.factor * (dot(score, feat, 0, 0) + dot(value, suffix, 1, 1))).astype(BF16)
            for score, feat, value, suffix in zip(scores_gv, feats_query, values, suffixes)
        ]
        for n, place in enumerate(places):
            at = slice(place * width, (place + 1) * width)
            out_bufs[0][:, at] = dot(grads_a[n], matrices[n], 1, 1).astype(BF16)
            out_bufs[1][:, at] = dot(grads_b[n], matrices[n], 1, 1).astype(BF16)
            value_grad = dot(scores_ab[n], grads[n], 0, 0) + dot(feats_key[n], suffixes[n])
            out_bufs[2][:, at] = (plan.factor * value_grad).astype(BF16)
        for part in range(first, first + 4, min(4, plan.run)):
            count = min(4, plan.run)
            source = pl.ds(part * width, count * width)
            target = pl.ds(plan.head(chunk, part) * width, count * width)
            for buf, ref in zip(out_bufs, out_refs):
                written.append(copies.start(buf.at[:, source], ref.at[:, target]))
    wait(written)


def output_rows(plan, chunk, rows, maps, states, extra, done):
    shape = jax.ShapeDtypeStruct((plan.tokens, plan.heads * plan.width), BF16)
    narrow = [pltpu.VMEM((plan.tokens, plan.in_chunk * plan.width), BF16)] * 3
    return call(
        functools.partial(rows_kernel, plan, chunk),
        (*states, extra, *rows, maps, *done),
        [shape] * 3,
        matmuls(plan, 12 * plan.in_chunk),
        row_scratch(plan, plan.in_chunk) + state_scratch(plan) + narrow,
        chunk_copies(plan) + 3 * plan.in_chunk + 1,
        {10: 0, 11: 1, 12: 2} if done else None,
        near=range(4),
        limit=MIDDLE_LIMIT,
        weight=LIGHT,
    )


def swap_core(plan, state):
    return lax.ppermute(state, "context", [(i, i ^ 1) for i in range(plan.ranks)])


def swap_chip(plan, state):
    return lax.ppermute(state, "context", [(i, i ^ 2) for i in range(plan.ranks)])


def chain_swap(plan, state, hop):
    mirror = plan.groups - 1 - hop
    steps = [(i, i ^ 1) for i in range(plan.ranks)]
    for low in range(4):
        for left in (hop, mirror - 1):
            a, b = 4 * left + low, 4 * left + 4 + low
            steps[a], steps[b] = (a, b), (b, a)
    return lax.ppermute(state, "context", steps)


def chain_split(plan, state, hop):
    mirror = plan.groups - 1 - hop
    up = [(4 * hop + low, 4 * hop + 4 + low) for low in range(4)]
    down = [(4 * mirror + low, 4 * mirror - 4 + low) for low in range(4)]
    return lax.ppermute(state[0], "context", up), lax.ppermute(state[1], "context", down)


def plane_sums(plan, halves):
    _, chip, _ = device_place()
    replica = lax.axis_index("dp")
    ranks, copies, width = plan.ranks, plan.copies, plan.width
    totals = [half.reshape(copies, -1, 2, plan.height, width) for half in halves]

    def plane_part(target_replica, target_chip):
        parts = []
        for total in totals:
            some = lax.dynamic_index_in_dim(total, target_replica, 0, keepdims=False)
            parts.append(lax.dynamic_index_in_dim(some, target_chip, 1, keepdims=False))
        return jnp.concatenate(parts, axis=0)

    plane = plane_part(replica, chip)
    for turn in range(copies):
        for flip in range(2):
            if turn == 0 and flip == 0:
                continue
            steps = [
                (r * ranks + i, ((r + turn) % copies) * ranks + (i ^ (2 * flip)))
                for r in range(copies)
                for i in range(ranks)
            ]
            sent = plane_part((replica + turn) % copies, (chip + flip) % 2)
            plane = plane + lax.ppermute(sent, ("dp", "context"), steps)
    return plane


def group_sum(plan, plane):
    _, _, group = device_place()
    result = lax.dynamic_index_in_dim(plane, group, 0, keepdims=False)
    for turn in range(1, plan.groups):
        steps = [(i, (i + 4 * turn) % plan.ranks) for i in range(plan.ranks)]
        sent = lax.dynamic_index_in_dim(plane, (group + turn) % plan.groups, 0, keepdims=False)
        result = result + lax.ppermute(sent, "context", steps)
    return result


def select_group(plan, got):
    _, _, group = device_place()
    prefix = suffix = jnp.zeros_like(got[0])
    for hop, state in enumerate(got):
        prefix = jnp.where(group == hop + 1, state, prefix)
        suffix = jnp.where(group == plan.groups - 2 - hop, state, suffix)
    return jnp.stack([prefix, suffix])


def scan_alone(plan, group_state):
    before = jnp.zeros_like(group_state)
    for hop in range(plan.groups - 1):
        if plan.groups % 2:
            up, down = chain_split(plan, before + group_state, hop)
            before = before + jnp.stack([up, down])
    return before


def per_device(queries, key_rows, value_rows, out_grad, maps):
    tokens = queries.shape[1]
    heads, width, _ = maps.shape
    plan = Plan(heads, width, tokens, lax.axis_size("context"), lax.axis_size("dp"))
    rows = [x.reshape(tokens, heads * width) for x in (queries, key_rows, value_rows, out_grad)]
    core, chip, group = device_place()
    side = jnp.arange(2).reshape(2, 1, 1, 1)
    chunks, hops, tie = range(plan.chunks), plan.groups - 1, lax.optimization_barrier

    kept, from_core, total, from_chip, group_state = [], [], [], [], []
    for chunk in chunks:
        sent, kept_here, given = block_states(plan, chunk, rows, maps)
        kept.append(kept_here)
        from_core.append(swap_core(plan, sent))
        given = given + from_core[chunk][1]
        if chunk == plan.chunks - 1:
            terms = inner(plan, rows, maps)
        if chunk:
            given, terms = tie((given, terms))
        total.append(kept_here[0] + from_core[chunk][0])
        from_chip.append(swap_chip(plan, given))
        group_state.append(total[chunk] + from_chip[chunk])

    def for_other_chip(chunk, before):
        return before + jnp.where(side == chip, total[chunk], 0.0)

    before, got, down = [None] * plan.chunks, [[] for _ in chunks], [None] * plan.chunks
    if plan.groups % 2:
        for chunk in chunks:
            before[chunk] = scan_alone(plan, group_state[chunk])
            down[chunk] = swap_chip(plan, for_other_chip(chunk, before[chunk]))
    else:
        for stage in range(hops + plan.chunks - 1):
            for chunk in chunks:
                hop = stage - chunk
                if not 0 <= hop < hops:
                    continue
                send = jnp.where(group == hop, group_state[chunk][0], group_state[chunk][1])
                if hop:
                    send = send + got[chunk][-1]
                if chunk and hop < hops - 1:
                    send, got[0][hop] = tie((send, got[0][hop]))
                if chunk and hop == hops - 1:
                    before[0] = select_group(plan, got[0])
                    mate = for_other_chip(0, before[0])
                    send, mate = tie((send, mate))
                    down[0] = swap_chip(plan, mate)
                got[chunk].append(chain_swap(plan, send, hop))
        last = plan.chunks - 1
        if last:
            got[last][-1], down[0] = tie((got[last][-1], down[0]))
        before[last] = select_group(plan, got[last])
        down[last] = swap_chip(plan, for_other_chip(last, before[last]))

    halves, done = [], ()
    for chunk in chunks:
        states = [before[chunk] + jnp.where(side != chip, from_chip[chunk], 0.0), down[chunk]]
        for turn in range(2):
            if turn and done:
                states[1], states[2], done = tie((states[1], states[2], done))
            mine = jnp.where(side == core, kept[chunk][turn], 0.0)
            states.append(swap_core(plan, states[turn] + mine))
        if halves:
            states[3], halves = tie((states[3], halves))
        for_mate, own = maps_term(plan, states, from_core[chunk], *terms[chunk])
        halves.append(own + swap_core(plan, for_mate))
        done = output_rows(plan, chunk, rows, maps, states, from_core[chunk], done)
    plane = plane_sums(plan, halves)
    plane, done = tie((plane, done))
    query_grad, key_grad, value_grad = done
    maps_grad = group_sum(plan, plane) * plan.norm
    return (query_grad[None], key_grad[None], value_grad[None], maps_grad)


def solution(mesh):
    in_specs = (
        P("dp", "context", None),
        P("dp", "context", None),
        P("dp", "context", None),
        P("dp", "context", None),
        P(),
    )
    out_specs = (
        P("dp", "context", None),
        P("dp", "context", None),
        P("dp", "context", None),
        P(("dp", "context"), None),
    )
    return jax.shard_map(
        per_device, mesh=mesh, in_specs=in_specs, out_specs=out_specs, check_vma=False
    )
```

```python
import functools
import math

import jax
import jax.numpy as jnp
from jax import lax
from jax.experimental import pallas as pl
from jax.experimental.pallas import tpu as pltpu
from jax.sharding import PartitionSpec as P

F32 = jnp.float32
BF16 = jnp.bfloat16
VMEM_LIMIT = 57 * 1024 * 1024
MIDDLE_LIMIT = 51 * 1024 * 1024
STATES_LIMIT = 53 * 1024 * 1024
SMALL_LIMIT = 16 * 1024 * 1024
LIGHT = 0.01


class Plan:
    def __init__(self, heads, width, tokens, ranks, copies):
        self.heads, self.width, self.tokens = heads, width, tokens
        self.ranks, self.copies = ranks, copies
        self.groups = ranks // 4
        per_copy = heads // copies if heads % copies == 0 else 0
        self.chunks = 2 if per_copy and per_copy % 2 == 0 and self.groups % 2 == 0 else 1
        self.in_chunk = heads // self.chunks
        self.quarter = self.in_chunk // 4
        self.run = per_copy // self.chunks if self.chunks > 1 else self.in_chunk
        self.stride = per_copy if self.chunks > 1 else 0
        self.height = heads * width // (copies * ranks)
        self.factor = 1.0 / math.sqrt(width * tokens * ranks)
        self.norm = 1.0 / math.sqrt(copies * tokens * ranks)

    def head(self, chunk, place):
        return (place // self.run) * self.stride + chunk * self.run + place % self.run


def device_place():
    index = lax.axis_index("context")
    return index % 2, (index // 2) % 2, index // 4


def dot(left, right, left_dim=1, right_dim=0):
    return lax.dot_general(
        left, right, (((left_dim,), (right_dim,)), ((), ())), preferred_element_type=F32
    )


def call(body, operands, shapes, flops, scratch, copies, aliases=None, near=(), near_out=(), limit=VMEM_LIMIT, weight=1.0):
    moved = sum(x.size * x.dtype.itemsize for x in list(operands) + list(shapes))

    def specs(count, in_vmem):
        return [
            pl.BlockSpec(memory_space=pltpu.VMEM if n in in_vmem else pltpu.HBM)
            for n in range(count)
        ]

    return pl.pallas_call(
        body,
        out_shape=shapes,
        in_specs=specs(len(operands), near),
        out_specs=specs(len(shapes), near_out),
        scratch_shapes=list(scratch) + [pltpu.SemaphoreType.DMA((copies,))],
        input_output_aliases=aliases or {},
        compiler_params=pltpu.CompilerParams(vmem_limit_bytes=limit),
        cost_estimate=pl.CostEstimate(
            flops=int(flops * weight), bytes_accessed=int(moved * weight), transcendentals=0
        ),
    )(*operands)


class Copies:
    def __init__(self, sems):
        self.sems, self.used = sems, 0

    def start(self, source, target):
        copy = pltpu.make_async_copy(source, target, self.sems.at[self.used])
        self.used += 1
        copy.start()
        return copy


def wait(copies):
    for copy in copies:
        copy.wait()


def matmuls(plan, count):
    return 2 * count * plan.tokens * plan.width * plan.width


def load_chunk(plan, copies, chunk, offset, row_refs, maps_ref, row_bufs, maps_buf):
    width, started = plan.width, []
    for first in range(0, plan.in_chunk, plan.run):
        head = plan.head(chunk, first)
        source, target = pl.ds(head, plan.run), pl.ds(offset + first, plan.run)
        started.append(copies.start(maps_ref.at[source], maps_buf.at[target]))
        source = pl.ds(head * width, plan.run * width)
        target = pl.ds((offset + first) * width, plan.run * width)
        for ref, buf in zip(row_refs, row_bufs):
            started.append(copies.start(ref.at[:, source], buf.at[:, target]))
    return started


def chunk_copies(plan):
    return 5 * (plan.in_chunk // plan.run)


def row_scratch(plan, count):
    rows = [pltpu.VMEM((plan.tokens, count * plan.width), BF16)] * 4
    return rows + [pltpu.VMEM((count, plan.width, plan.width), BF16)]


def head_of(buf, place, width):
    return buf[:, place * width : (place + 1) * width]


def quarter_of(plan, place):
    core, chip, _ = device_place()
    low = place // plan.quarter
    core_turn = 1 - core if low % 2 else core
    chip_turn = 1 - chip if low // 2 else chip
    return core_turn, chip_turn, place % plan.quarter


def states_kernel(plan, chunk, *refs):
    row_refs, maps_ref, sent_ref, kept_ref, given_ref = refs[:4], refs[4], refs[5], refs[6], refs[7]
    row_bufs, maps_buf, sems = refs[8:12], refs[12], refs[13]
    copies, width = Copies(sems), plan.width
    started = load_chunk(plan, copies, chunk, 0, row_refs, maps_ref, row_bufs, maps_buf)
    q_buf, k_buf, v_buf, g_buf = row_bufs
    size = 5 * max(1, 4 // plan.run)
    for first in range(0, plan.in_chunk, 4):
        places = range(first, first + 4)
        wait(started[:size])
        started = started[size:]
        feats_key = [dot(head_of(k_buf, n, width), maps_buf[n]).astype(BF16) for n in places]
        feats_query = [dot(head_of(q_buf, n, width), maps_buf[n]).astype(BF16) for n in places]
        key_states = [
            dot(feat, head_of(v_buf, n, width), 0, 0) for feat, n in zip(feats_key, places)
        ]
        query_states = [
            dot(feat, head_of(g_buf, n, width), 0, 0) for feat, n in zip(feats_query, places)
        ]
        for place, key_state, query_state in zip(places, key_states, query_states):
            core_turn, chip_turn, i = quarter_of(plan, place)

            @pl.when(core_turn == 1)
            def _():
                sent_ref[chip_turn, 0, i] = key_state
                sent_ref[chip_turn, 1, i] = query_state

            @pl.when(core_turn == 0)
            def _():
                kept_ref[chip_turn, 0, i] = key_state
                kept_ref[chip_turn, 1, i] = query_state
    given_ref[...] = kept_ref[1]


def block_states(plan, chunk, rows, maps):
    shape = (2, 2, plan.quarter, plan.width, plan.width)
    state = jax.ShapeDtypeStruct(shape, F32)
    return call(
        functools.partial(states_kernel, plan, chunk),
        (*rows, maps),
        [state, state, jax.ShapeDtypeStruct(shape[1:], F32)],
        matmuls(plan, 4 * plan.in_chunk),
        row_scratch(plan, plan.in_chunk),
        chunk_copies(plan),
        near_out=(0, 1, 2),
        limit=STATES_LIMIT,
    )


def causal_mask(tokens):
    row = lax.broadcasted_iota(jnp.int32, (tokens, tokens), 0)
    column = lax.broadcasted_iota(jnp.int32, (tokens, tokens), 1)
    return row >= column


def inner_kernel(plan, chunk, *refs):
    row_refs, maps_ref, base_ref, pair_ref = refs[:4], refs[4], refs[5], refs[6]
    row_bufs, maps_buf, base_buf, pair_buf, sems = refs[7:11], refs[11], refs[12], refs[13], refs[14]
    copies, width = Copies(sems), plan.width
    started = load_chunk(plan, copies, chunk, 0, row_refs, maps_ref, row_bufs, maps_buf)
    causal = causal_mask(plan.tokens)
    written = []
    size = 5 * max(1, 4 // plan.run)
    for first in range(0, plan.in_chunk, 4):
        places = range(first, first + 4)
        wait(started[:size])
        started = started[size:]
        queries, keys, values, grads = [
            [head_of(buf, n, width) for n in places] for buf in row_bufs
        ]
        scores = [
            jnp.where(causal, dot(grad, value, 1, 1), 0.0).astype(BF16)
            for grad, value in zip(grads, values)
        ]
        feats_query = [dot(x, maps_buf[n]).astype(BF16) for x, n in zip(queries, places)]
        feats_key = [dot(x, maps_buf[n]).astype(BF16) for x, n in zip(keys, places)]
        grads_a = [dot(s, feat).astype(BF16) for s, feat in zip(scores, feats_key)]
        grads_b = [dot(s, feat, 0, 0).astype(BF16) for s, feat in zip(scores, feats_query)]
        for n, place in enumerate(places):
            pair_buf[0, place] = dot(queries[n], grads[n], 0, 0).astype(BF16)
            pair_buf[1, place] = dot(keys[n], values[n], 0, 0).astype(BF16)
            base_buf[place] = dot(queries[n], grads_a[n], 0, 0) + dot(keys[n], grads_b[n], 0, 0)
        part = pl.ds(first, 4)
        written.append(copies.start(base_buf.at[part], base_ref.at[part]))
        written.append(copies.start(pair_buf.at[:, part], pair_ref.at[:, part]))
    wait(written)


def inner(plan, chunk, rows, maps):
    square = (plan.in_chunk, plan.width, plan.width)
    return call(
        functools.partial(inner_kernel, plan, chunk),
        (*rows, maps),
        [jax.ShapeDtypeStruct(square, F32), jax.ShapeDtypeStruct((2,) + square, BF16)],
        matmuls(plan, 9 * plan.in_chunk),
        row_scratch(plan, plan.in_chunk)
        + [pltpu.VMEM(square, F32), pltpu.VMEM((2,) + square, BF16)],
        chunk_copies(plan) + plan.in_chunk // 2,
    )


def finish_states(plan, state_refs, extra_buf, state_buf):
    core, _, _ = device_place()
    for core_turn in range(2):
        for chip_turn in range(2):
            for side in range(2):
                state = state_refs[2 * core_turn + chip_turn][side]
                if core_turn == 0:
                    wanted = core == 1 - side
                    state = state + jnp.where(wanted, extra_buf[chip_turn, side], 0.0)
                state_buf[core_turn, chip_turn, side] = state.astype(BF16)


def state_scratch(plan):
    shape = (2, 2, plan.quarter, plan.width, plan.width)
    return [pltpu.VMEM(shape, F32), pltpu.VMEM((2,) + shape, BF16)]


def term_kernel(plan, *refs):
    state_refs, extra_ref, base_ref, pair_ref = refs[:4], refs[4], refs[5], refs[6]
    out_refs = refs[7:-5]
    extra_buf, state_buf, base_buf, pair_buf, sems = refs[-5:]
    copies = Copies(sems)
    core, _, _ = device_place()
    extra_copy = copies.start(extra_ref, extra_buf)
    others = [copies.start(pair_ref, pair_buf), copies.start(base_ref, base_buf)]
    extra_copy.wait()
    finish_states(plan, state_refs, extra_buf, state_buf)
    wait(others)
    half = plan.width // 2
    for first in range(0, plan.in_chunk, 4):
        places = range(first, first + 4)
        where = [quarter_of(plan, place) for place in places]
        products = [
            dot(pair_buf[side, place], state_buf[c, y, side, i], 1, 1)
            for place, (c, y, i) in zip(places, where)
            for side in range(2)
        ]
        for n, place in enumerate(places):
            term = plan.factor * (base_buf[place] + products[2 * n] + products[2 * n + 1])
            if len(out_refs) == 1:
                out_refs[0][place] = term
            else:
                out_refs[0][place] = jnp.where(core == 0, term[half:], term[:half])
                out_refs[1][place] = jnp.where(core == 0, term[:half], term[half:])


def maps_term(plan, states, extra, base, pair):
    width = plan.width
    square = (plan.in_chunk, width, width)
    in_halves = 2 * plan.height == width and plan.height % 8 == 0
    shapes = [(plan.in_chunk, width // 2, width)] * 2 if in_halves else [square]
    outs = call(
        functools.partial(term_kernel, plan),
        (*states, extra, base, pair),
        [jax.ShapeDtypeStruct(shape, F32) for shape in shapes],
        matmuls(plan, 2 * plan.in_chunk),
        state_scratch(plan) + [pltpu.VMEM(square, F32), pltpu.VMEM((2,) + square, BF16)],
        3,
        near=range(4),
        near_out=range(2),
        limit=SMALL_LIMIT,
        weight=LIGHT,
    )
    if in_halves:
        return outs
    core, _, _ = device_place()
    parts = outs[0].reshape(-1, 2, plan.height, width)
    return [
        lax.dynamic_index_in_dim(parts, turn, 1, keepdims=False) for turn in (1 - core, core)
    ]


def rows_kernel(plan, chunk, *refs):
    state_refs, extra_ref, row_refs, maps_ref = refs[:4], refs[4], refs[5:9], refs[9]
    refs = refs[10 + (3 if chunk else 0) :]
    out_refs, row_bufs, maps_buf = refs[:3], refs[3:7], refs[7]
    extra_buf, state_buf, out_bufs, sems = refs[8], refs[9], refs[10:13], refs[13]
    copies, width = Copies(sems), plan.width
    extra_copy = copies.start(extra_ref, extra_buf)
    started = load_chunk(plan, copies, chunk, 0, row_refs, maps_ref, row_bufs, maps_buf)
    causal = causal_mask(plan.tokens)
    extra_copy.wait()
    finish_states(plan, state_refs, extra_buf, state_buf)
    written = []
    size = 5 * max(1, 4 // plan.run)
    for first in range(0, plan.in_chunk, 4):
        places = range(first, first + 4)
        wait(started[:size])
        started = started[size:]
        queries, keys, values, grads = [
            [head_of(buf, place, width) for place in places] for buf in row_bufs
        ]
        where = [quarter_of(plan, place) for place in places]
        prefixes = [state_buf[c, y, 0, i] for c, y, i in where]
        suffixes = [state_buf[c, y, 1, i] for c, y, i in where]
        matrices = [maps_buf[place] for place in places]
        scores_gv = [
            jnp.where(causal, dot(grad, value, 1, 1), 0.0).astype(BF16)
            for grad, value in zip(grads, values)
        ]
        feats_query = [dot(x, matrix).astype(BF16) for x, matrix in zip(queries, matrices)]
        feats_key = [dot(x, matrix).astype(BF16) for x, matrix in zip(keys, matrices)]
        scores_ab = [
            jnp.where(causal, dot(left, right, 1, 1), 0.0).astype(BF16)
            for left, right in zip(feats_query, feats_key)
        ]
        grads_a = [
            (plan.factor * (dot(score, feat) + dot(grad, prefix, 1, 1))).astype(BF16)
            for score, feat, grad, prefix in zip(scores_gv, feats_key, grads, prefixes)
        ]
        grads_b = [
            (plan.factor * (dot(score, feat, 0, 0) + dot(value, suffix, 1, 1))).astype(BF16)
            for score, feat, value, suffix in zip(scores_gv, feats_query, values, suffixes)
        ]
        for n, place in enumerate(places):
            at = slice(place * width, (place + 1) * width)
            out_bufs[0][:, at] = dot(grads_a[n], matrices[n], 1, 1).astype(BF16)
            out_bufs[1][:, at] = dot(grads_b[n], matrices[n], 1, 1).astype(BF16)
            value_grad = dot(scores_ab[n], grads[n], 0, 0) + dot(feats_key[n], suffixes[n])
            out_bufs[2][:, at] = (plan.factor * value_grad).astype(BF16)
        for part in range(first, first + 4, min(4, plan.run)):
            count = min(4, plan.run)
            source = pl.ds(part * width, count * width)
            target = pl.ds(plan.head(chunk, part) * width, count * width)
            for buf, ref in zip(out_bufs, out_refs):
                written.append(copies.start(buf.at[:, source], ref.at[:, target]))
    wait(written)


def output_rows(plan, chunk, rows, maps, states, extra, done):
    shape = jax.ShapeDtypeStruct((plan.tokens, plan.heads * plan.width), BF16)
    narrow = [pltpu.VMEM((plan.tokens, plan.in_chunk * plan.width), BF16)] * 3
    return call(
        functools.partial(rows_kernel, plan, chunk),
        (*states, extra, *rows, maps, *done),
        [shape] * 3,
        matmuls(plan, 12 * plan.in_chunk),
        row_scratch(plan, plan.in_chunk) + state_scratch(plan) + narrow,
        chunk_copies(plan) + 3 * plan.in_chunk + 1,
        {10: 0, 11: 1, 12: 2} if done else None,
        near=range(4),
        limit=MIDDLE_LIMIT,
        weight=LIGHT,
    )


def swap_core(plan, state):
    return lax.ppermute(state, "context", [(i, i ^ 1) for i in range(plan.ranks)])


def swap_chip(plan, state):
    return lax.ppermute(state, "context", [(i, i ^ 2) for i in range(plan.ranks)])


def chain_swap(plan, state, hop):
    mirror = plan.groups - 1 - hop
    steps = [(i, i ^ 1) for i in range(plan.ranks)]
    for low in range(4):
        for left in (hop, mirror - 1):
            a, b = 4 * left + low, 4 * left + 4 + low
            steps[a], steps[b] = (a, b), (b, a)
    return lax.ppermute(state, "context", steps)


def chain_split(plan, state, hop):
    mirror = plan.groups - 1 - hop
    up = [(4 * hop + low, 4 * hop + 4 + low) for low in range(4)]
    down = [(4 * mirror + low, 4 * mirror - 4 + low) for low in range(4)]
    return lax.ppermute(state[0], "context", up), lax.ppermute(state[1], "context", down)


def plane_sums(plan, halves):
    _, chip, _ = device_place()
    replica = lax.axis_index("dp")
    ranks, copies, width = plan.ranks, plan.copies, plan.width
    totals = [half.reshape(copies, -1, 2, plan.height, width) for half in halves]

    def plane_part(target_replica, target_chip):
        parts = []
        for total in totals:
            some = lax.dynamic_index_in_dim(total, target_replica, 0, keepdims=False)
            parts.append(lax.dynamic_index_in_dim(some, target_chip, 1, keepdims=False))
        return jnp.concatenate(parts, axis=0)

    plane = plane_part(replica, chip)
    for turn in range(copies):
        for flip in range(2):
            if turn == 0 and flip == 0:
                continue
            steps = [
                (r * ranks + i, ((r + turn) % copies) * ranks + (i ^ (2 * flip)))
                for r in range(copies)
                for i in range(ranks)
            ]
            sent = plane_part((replica + turn) % copies, (chip + flip) % 2)
            plane = plane + lax.ppermute(sent, ("dp", "context"), steps)
    return plane


def group_sum(plan, plane):
    _, _, group = device_place()
    result = lax.dynamic_index_in_dim(plane, group, 0, keepdims=False)
    for turn in range(1, plan.groups):
        steps = [(i, (i + 4 * turn) % plan.ranks) for i in range(plan.ranks)]
        sent = lax.dynamic_index_in_dim(plane, (group + turn) % plan.groups, 0, keepdims=False)
        result = result + lax.ppermute(sent, "context", steps)
    return result


def select_group(plan, got):
    _, _, group = device_place()
    prefix = suffix = jnp.zeros_like(got[0])
    for hop, state in enumerate(got):
        prefix = jnp.where(group == hop + 1, state, prefix)
        suffix = jnp.where(group == plan.groups - 2 - hop, state, suffix)
    return jnp.stack([prefix, suffix])


def scan_alone(plan, group_state):
    before = jnp.zeros_like(group_state)
    for hop in range(plan.groups - 1):
        if plan.groups % 2:
            up, down = chain_split(plan, before + group_state, hop)
            before = before + jnp.stack([up, down])
    return before


def after(value, *others):
    return lax.optimization_barrier((value, *others))[0]


def per_device(queries, key_rows, value_rows, out_grad, maps):
    tokens = queries.shape[1]
    heads, width, _ = maps.shape
    plan = Plan(heads, width, tokens, lax.axis_size("context"), lax.axis_size("dp"))
    rows = [x.reshape(tokens, heads * width) for x in (queries, key_rows, value_rows, out_grad)]
    core, chip, group = device_place()
    side = jnp.arange(2).reshape(2, 1, 1, 1)
    chunks, hops, last = range(plan.chunks), plan.groups - 1, plan.chunks - 1

    kept, from_core, given, terms = [], [], [], []
    total, from_chip, group_state = [], [], []
    for chunk in chunks:
        matrices = after(maps, given[-1]) if chunk else maps
        sent, kept_here, given_here = block_states(plan, chunk, rows, matrices)
        kept.append(kept_here)
        from_core.append(swap_core(plan, sent))
        given_here = given_here + from_core[chunk][1]
        if chunk:
            terms.append(inner(plan, 0, rows, after(maps, sent)))
            given_here = after(given_here, *terms[0])
        given.append(given_here)
        total.append(kept_here[0] + from_core[chunk][0])
        from_chip.append(swap_chip(plan, given_here))
        group_state.append(total[chunk] + from_chip[chunk])
    terms.append(inner(plan, last, rows, after(maps, given[last])))

    def for_other_chip(chunk, before):
        return before + jnp.where(side == chip, total[chunk], 0.0)

    def for_other_core(chunk, turn, state):
        return state + jnp.where(side == core, kept[chunk][turn], 0.0)

    before, got, down = [None] * plan.chunks, [[] for _ in chunks], [None] * plan.chunks
    if plan.groups % 2:
        for chunk in chunks:
            before[chunk] = scan_alone(plan, group_state[chunk])
            down[chunk] = swap_chip(plan, for_other_chip(chunk, before[chunk]))
    else:
        ahead = None
        for stage in range(hops + last):
            for chunk in chunks:
                hop = stage - chunk
                if chunk == 0 and hop == hops:
                    before[0] = select_group(plan, got[0])
                    ahead = for_other_chip(0, before[0])
                    down[0] = swap_chip(plan, ahead)
                if not 0 <= hop < hops:
                    continue
                send = jnp.where(group == hop, group_state[chunk][0], group_state[chunk][1])
                if hop:
                    send = send + got[chunk][-1]
                if chunk:
                    send = after(send, ahead, *(terms[last] if hop == 0 else ()))
                else:
                    if last and hop < 2:
                        send = after(send, (given, from_chip)[hop][last])
                    ahead = send
                got[chunk].append(chain_swap(plan, send, hop))
        if last:
            got[last][-1] = after(got[last][-1], for_other_core(0, 1, down[0]))
        before[last] = select_group(plan, got[last])
        down[last] = swap_chip(plan, for_other_chip(last, before[last]))

    halves, done = [], ()
    for chunk in chunks:
        states = [before[chunk] + jnp.where(side != chip, from_chip[chunk], 0.0), down[chunk]]
        for turn in range(2):
            if turn and done:
                states[1] = after(states[1], states[2], *done)
            states.append(swap_core(plan, for_other_core(chunk, turn, states[turn])))
        if halves:
            states[3] = after(states[3], *halves)
        for_mate, own = maps_term(plan, states, from_core[chunk], *terms[chunk])
        halves.append(own + swap_core(plan, for_mate))
        done = output_rows(plan, chunk, rows, maps, states, from_core[chunk], done)
    plane = after(plane_sums(plan, halves), *done)
    query_grad, key_grad, value_grad = done
    maps_grad = group_sum(plan, plane) * plan.norm
    return (query_grad[None], key_grad[None], value_grad[None], maps_grad)


def solution(mesh):
    in_specs = (
        P("dp", "context", None),
        P("dp", "context", None),
        P("dp", "context", None),
        P("dp", "context", None),
        P(),
    )
    out_specs = (
        P("dp", "context", None),
        P("dp", "context", None),
        P("dp", "context", None),
        P(("dp", "context"), None),
    )
    return jax.shard_map(
        per_device, mesh=mesh, in_specs=in_specs, out_specs=out_specs, check_vma=False
    )
```

```python
import functools
import math

import jax
import jax.numpy as jnp
from jax import lax
from jax.experimental import pallas as pl
from jax.experimental.pallas import tpu as pltpu
from jax.sharding import PartitionSpec as P

F32 = jnp.float32
BF16 = jnp.bfloat16
VMEM_LIMIT = 57 * 1024 * 1024
MIDDLE_LIMIT = 51 * 1024 * 1024
STATES_LIMIT = 53 * 1024 * 1024
SMALL_LIMIT = 16 * 1024 * 1024
LIGHT = 0.01


class Plan:
    def __init__(self, heads, width, tokens, ranks, copies):
        self.heads, self.width, self.tokens = heads, width, tokens
        self.ranks, self.copies = ranks, copies
        self.groups = ranks // 4
        per_copy = heads // copies if heads % copies == 0 else 0
        self.chunks = 2 if per_copy and per_copy % 2 == 0 and self.groups % 2 == 0 else 1
        self.in_chunk = heads // self.chunks
        self.quarter = self.in_chunk // 4
        self.run = per_copy // self.chunks if self.chunks > 1 else self.in_chunk
        self.stride = per_copy if self.chunks > 1 else 0
        self.height = heads * width // (copies * ranks)
        self.factor = 1.0 / math.sqrt(width * tokens * ranks)
        self.norm = 1.0 / math.sqrt(copies * tokens * ranks)

    def head(self, chunk, place):
        return (place // self.run) * self.stride + chunk * self.run + place % self.run


def device_place():
    index = lax.axis_index("context")
    return index % 2, (index // 2) % 2, index // 4


def dot(left, right, left_dim=1, right_dim=0):
    return lax.dot_general(
        left, right, (((left_dim,), (right_dim,)), ((), ())), preferred_element_type=F32
    )


def call(body, operands, shapes, flops, scratch, copies, aliases=None, near=(), near_out=(), limit=VMEM_LIMIT, weight=1.0):
    moved = sum(x.size * x.dtype.itemsize for x in list(operands) + list(shapes))

    def specs(count, in_vmem):
        return [
            pl.BlockSpec(memory_space=pltpu.VMEM if n in in_vmem else pltpu.HBM)
            for n in range(count)
        ]

    return pl.pallas_call(
        body,
        out_shape=shapes,
        in_specs=specs(len(operands), near),
        out_specs=specs(len(shapes), near_out),
        scratch_shapes=list(scratch) + [pltpu.SemaphoreType.DMA((copies,))],
        input_output_aliases=aliases or {},
        compiler_params=pltpu.CompilerParams(vmem_limit_bytes=limit),
        cost_estimate=pl.CostEstimate(
            flops=int(flops * weight), bytes_accessed=int(moved * weight), transcendentals=0
        ),
    )(*operands)


class Copies:
    def __init__(self, sems):
        self.sems, self.used = sems, 0

    def start(self, source, target):
        copy = pltpu.make_async_copy(source, target, self.sems.at[self.used])
        self.used += 1
        copy.start()
        return copy


def wait(copies):
    for copy in copies:
        copy.wait()


def matmuls(plan, count):
    return 2 * count * plan.tokens * plan.width * plan.width


def load_chunk(plan, copies, chunk, offset, row_refs, maps_ref, row_bufs, maps_buf):
    width, started = plan.width, []
    for first in range(0, plan.in_chunk, plan.run):
        head = plan.head(chunk, first)
        source, target = pl.ds(head, plan.run), pl.ds(offset + first, plan.run)
        started.append(copies.start(maps_ref.at[source], maps_buf.at[target]))
        source = pl.ds(head * width, plan.run * width)
        target = pl.ds((offset + first) * width, plan.run * width)
        for ref, buf in zip(row_refs, row_bufs):
            started.append(copies.start(ref.at[:, source], buf.at[:, target]))
    return started


def chunk_copies(plan):
    return 5 * (plan.in_chunk // plan.run)


def row_scratch(plan, count):
    rows = [pltpu.VMEM((plan.tokens, count * plan.width), BF16)] * 4
    return rows + [pltpu.VMEM((count, plan.width, plan.width), BF16)]


def head_of(buf, place, width):
    return buf[:, place * width : (place + 1) * width]


def quarter_of(plan, place):
    core, chip, _ = device_place()
    low = place // plan.quarter
    core_turn = 1 - core if low % 2 else core
    chip_turn = 1 - chip if low // 2 else chip
    return core_turn, chip_turn, place % plan.quarter


def states_kernel(plan, chunk, *refs):
    row_refs, maps_ref, sent_ref, kept_ref, given_ref = refs[:4], refs[4], refs[5], refs[6], refs[7]
    row_bufs, maps_buf, sems = refs[8:12], refs[12], refs[13]
    copies, width = Copies(sems), plan.width
    started = load_chunk(plan, copies, chunk, 0, row_refs, maps_ref, row_bufs, maps_buf)
    q_buf, k_buf, v_buf, g_buf = row_bufs
    size = 5 * max(1, 4 // plan.run)
    for first in range(0, plan.in_chunk, 4):
        places = range(first, first + 4)
        wait(started[:size])
        started = started[size:]
        feats_key = [dot(head_of(k_buf, n, width), maps_buf[n]).astype(BF16) for n in places]
        feats_query = [dot(head_of(q_buf, n, width), maps_buf[n]).astype(BF16) for n in places]
        key_states = [
            dot(feat, head_of(v_buf, n, width), 0, 0) for feat, n in zip(feats_key, places)
        ]
        query_states = [
            dot(feat, head_of(g_buf, n, width), 0, 0) for feat, n in zip(feats_query, places)
        ]
        for place, key_state, query_state in zip(places, key_states, query_states):
            core_turn, chip_turn, i = quarter_of(plan, place)

            @pl.when(core_turn == 1)
            def _():
                sent_ref[chip_turn, 0, i] = key_state
                sent_ref[chip_turn, 1, i] = query_state

            @pl.when(core_turn == 0)
            def _():
                kept_ref[chip_turn, 0, i] = key_state
                kept_ref[chip_turn, 1, i] = query_state
    given_ref[...] = kept_ref[1]


def block_states(plan, chunk, rows, maps):
    shape = (2, 2, plan.quarter, plan.width, plan.width)
    state = jax.ShapeDtypeStruct(shape, F32)
    return call(
        functools.partial(states_kernel, plan, chunk),
        (*rows, maps),
        [state, state, jax.ShapeDtypeStruct(shape[1:], F32)],
        matmuls(plan, 4 * plan.in_chunk),
        row_scratch(plan, plan.in_chunk),
        chunk_copies(plan),
        near_out=(0, 1, 2),
        limit=STATES_LIMIT,
    )


def causal_mask(tokens):
    row = lax.broadcasted_iota(jnp.int32, (tokens, tokens), 0)
    column = lax.broadcasted_iota(jnp.int32, (tokens, tokens), 1)
    return row >= column


def inner_kernel(plan, chunk, *refs):
    row_refs, maps_ref, base_ref, pair_ref = refs[:4], refs[4], refs[5], refs[6]
    row_bufs, maps_buf, base_buf, pair_buf, sems = refs[7:11], refs[11], refs[12], refs[13], refs[14]
    copies, width = Copies(sems), plan.width
    started = load_chunk(plan, copies, chunk, 0, row_refs, maps_ref, row_bufs, maps_buf)
    causal = causal_mask(plan.tokens)
    written = []
    size = 5 * max(1, 4 // plan.run)
    for first in range(0, plan.in_chunk, 4):
        places = range(first, first + 4)
        wait(started[:size])
        started = started[size:]
        queries, keys, values, grads = [
            [head_of(buf, n, width) for n in places] for buf in row_bufs
        ]
        scores = [
            jnp.where(causal, dot(grad, value, 1, 1), 0.0).astype(BF16)
            for grad, value in zip(grads, values)
        ]
        feats_query = [dot(x, maps_buf[n]).astype(BF16) for x, n in zip(queries, places)]
        feats_key = [dot(x, maps_buf[n]).astype(BF16) for x, n in zip(keys, places)]
        grads_a = [dot(s, feat).astype(BF16) for s, feat in zip(scores, feats_key)]
        grads_b = [dot(s, feat, 0, 0).astype(BF16) for s, feat in zip(scores, feats_query)]
        for n, place in enumerate(places):
            pair_buf[0, place] = dot(queries[n], grads[n], 0, 0).astype(BF16)
            pair_buf[1, place] = dot(keys[n], values[n], 0, 0).astype(BF16)
            base_buf[place] = dot(queries[n], grads_a[n], 0, 0) + dot(keys[n], grads_b[n], 0, 0)
        part = pl.ds(first, 4)
        written.append(copies.start(base_buf.at[part], base_ref.at[part]))
        written.append(copies.start(pair_buf.at[:, part], pair_ref.at[:, part]))
    wait(written)


def inner(plan, chunk, rows, maps):
    square = (plan.in_chunk, plan.width, plan.width)
    return call(
        functools.partial(inner_kernel, plan, chunk),
        (*rows, maps),
        [jax.ShapeDtypeStruct(square, F32), jax.ShapeDtypeStruct((2,) + square, BF16)],
        matmuls(plan, 9 * plan.in_chunk),
        row_scratch(plan, plan.in_chunk)
        + [pltpu.VMEM(square, F32), pltpu.VMEM((2,) + square, BF16)],
        chunk_copies(plan) + plan.in_chunk // 2,
    )


def finish_states(plan, state_refs, extra_buf, state_buf):
    core, _, _ = device_place()
    for core_turn in range(2):
        for chip_turn in range(2):
            for side in range(2):
                state = state_refs[2 * core_turn + chip_turn][side]
                if core_turn == 0:
                    wanted = core == 1 - side
                    state = state + jnp.where(wanted, extra_buf[chip_turn, side], 0.0)
                state_buf[core_turn, chip_turn, side] = state.astype(BF16)


def state_scratch(plan):
    shape = (2, 2, plan.quarter, plan.width, plan.width)
    return [pltpu.VMEM(shape, F32), pltpu.VMEM((2,) + shape, BF16)]


def term_kernel(plan, *refs):
    state_refs, extra_ref, base_ref, pair_ref = refs[:4], refs[4], refs[5], refs[6]
    out_refs = refs[7:-5]
    extra_buf, state_buf, base_buf, pair_buf, sems = refs[-5:]
    copies = Copies(sems)
    core, _, _ = device_place()
    extra_copy = copies.start(extra_ref, extra_buf)
    others = [copies.start(pair_ref, pair_buf), copies.start(base_ref, base_buf)]
    extra_copy.wait()
    finish_states(plan, state_refs, extra_buf, state_buf)
    wait(others)
    half = plan.width // 2
    for first in range(0, plan.in_chunk, 4):
        places = range(first, first + 4)
        where = [quarter_of(plan, place) for place in places]
        products = [
            dot(pair_buf[side, place], state_buf[c, y, side, i], 1, 1)
            for place, (c, y, i) in zip(places, where)
            for side in range(2)
        ]
        for n, place in enumerate(places):
            term = plan.factor * (base_buf[place] + products[2 * n] + products[2 * n + 1])
            if len(out_refs) == 1:
                out_refs[0][place] = term
            else:
                out_refs[0][place] = jnp.where(core == 0, term[half:], term[:half])
                out_refs[1][place] = jnp.where(core == 0, term[:half], term[half:])


def maps_term(plan, states, extra, base, pair):
    width = plan.width
    square = (plan.in_chunk, width, width)
    in_halves = 2 * plan.height == width and plan.height % 8 == 0
    shapes = [(plan.in_chunk, width // 2, width)] * 2 if in_halves else [square]
    outs = call(
        functools.partial(term_kernel, plan),
        (*states, extra, base, pair),
        [jax.ShapeDtypeStruct(shape, F32) for shape in shapes],
        matmuls(plan, 2 * plan.in_chunk),
        state_scratch(plan) + [pltpu.VMEM(square, F32), pltpu.VMEM((2,) + square, BF16)],
        3,
        near=range(4),
        near_out=range(2),
        limit=SMALL_LIMIT,
        weight=LIGHT,
    )
    if in_halves:
        return outs
    core, _, _ = device_place()
    parts = outs[0].reshape(-1, 2, plan.height, width)
    return [
        lax.dynamic_index_in_dim(parts, turn, 1, keepdims=False) for turn in (1 - core, core)
    ]


def rows_kernel(plan, chunk, *refs):
    state_refs, extra_ref, row_refs, maps_ref = refs[:4], refs[4], refs[5:9], refs[9]
    refs = refs[10 + (3 if chunk else 0) :]
    out_refs, row_bufs, maps_buf = refs[:3], refs[3:7], refs[7]
    extra_buf, state_buf, out_bufs, sems = refs[8], refs[9], refs[10:13], refs[13]
    copies, width = Copies(sems), plan.width
    extra_copy = copies.start(extra_ref, extra_buf)
    started = load_chunk(plan, copies, chunk, 0, row_refs, maps_ref, row_bufs, maps_buf)
    causal = causal_mask(plan.tokens)
    extra_copy.wait()
    finish_states(plan, state_refs, extra_buf, state_buf)
    written = []
    size = 5 * max(1, 4 // plan.run)
    for first in range(0, plan.in_chunk, 4):
        places = range(first, first + 4)
        wait(started[:size])
        started = started[size:]
        queries, keys, values, grads = [
            [head_of(buf, place, width) for place in places] for buf in row_bufs
        ]
        where = [quarter_of(plan, place) for place in places]
        prefixes = [state_buf[c, y, 0, i] for c, y, i in where]
        suffixes = [state_buf[c, y, 1, i] for c, y, i in where]
        matrices = [maps_buf[place] for place in places]
        scores_gv = [
            jnp.where(causal, dot(grad, value, 1, 1), 0.0).astype(BF16)
            for grad, value in zip(grads, values)
        ]
        feats_query = [dot(x, matrix).astype(BF16) for x, matrix in zip(queries, matrices)]
        feats_key = [dot(x, matrix).astype(BF16) for x, matrix in zip(keys, matrices)]
        scores_ab = [
            jnp.where(causal, dot(left, right, 1, 1), 0.0).astype(BF16)
            for left, right in zip(feats_query, feats_key)
        ]
        grads_a = [
            (plan.factor * (dot(score, feat) + dot(grad, prefix, 1, 1))).astype(BF16)
            for score, feat, grad, prefix in zip(scores_gv, feats_key, grads, prefixes)
        ]
        grads_b = [
            (plan.factor * (dot(score, feat, 0, 0) + dot(value, suffix, 1, 1))).astype(BF16)
            for score, feat, value, suffix in zip(scores_gv, feats_query, values, suffixes)
        ]
        for n, place in enumerate(places):
            at = slice(place * width, (place + 1) * width)
            out_bufs[0][:, at] = dot(grads_a[n], matrices[n], 1, 1).astype(BF16)
            out_bufs[1][:, at] = dot(grads_b[n], matrices[n], 1, 1).astype(BF16)
            value_grad = dot(scores_ab[n], grads[n], 0, 0) + dot(feats_key[n], suffixes[n])
            out_bufs[2][:, at] = (plan.factor * value_grad).astype(BF16)
        for part in range(first, first + 4, min(4, plan.run)):
            count = min(4, plan.run)
            source = pl.ds(part * width, count * width)
            target = pl.ds(plan.head(chunk, part) * width, count * width)
            for buf, ref in zip(out_bufs, out_refs):
                written.append(copies.start(buf.at[:, source], ref.at[:, target]))
    wait(written)


def output_rows(plan, chunk, rows, maps, states, extra, done):
    shape = jax.ShapeDtypeStruct((plan.tokens, plan.heads * plan.width), BF16)
    narrow = [pltpu.VMEM((plan.tokens, plan.in_chunk * plan.width), BF16)] * 3
    return call(
        functools.partial(rows_kernel, plan, chunk),
        (*states, extra, *rows, maps, *done),
        [shape] * 3,
        matmuls(plan, 12 * plan.in_chunk),
        row_scratch(plan, plan.in_chunk) + state_scratch(plan) + narrow,
        chunk_copies(plan) + 3 * plan.in_chunk + 1,
        {10: 0, 11: 1, 12: 2} if done else None,
        near=range(4),
        limit=MIDDLE_LIMIT,
        weight=LIGHT,
    )


def swap_core(plan, state):
    return lax.ppermute(state, "context", [(i, i ^ 1) for i in range(plan.ranks)])


def swap_chip(plan, state):
    return lax.ppermute(state, "context", [(i, i ^ 2) for i in range(plan.ranks)])


def chain_swap(plan, state, hop):
    mirror = plan.groups - 1 - hop
    steps = [(i, i ^ 1) for i in range(plan.ranks)]
    for low in range(4):
        for left in (hop, mirror - 1):
            a, b = 4 * left + low, 4 * left + 4 + low
            steps[a], steps[b] = (a, b), (b, a)
    return lax.ppermute(state, "context", steps)


def chain_split(plan, state, hop):
    mirror = plan.groups - 1 - hop
    up = [(4 * hop + low, 4 * hop + 4 + low) for low in range(4)]
    down = [(4 * mirror + low, 4 * mirror - 4 + low) for low in range(4)]
    return lax.ppermute(state[0], "context", up), lax.ppermute(state[1], "context", down)


def plane_sums(plan, halves):
    _, chip, _ = device_place()
    replica = lax.axis_index("dp")
    ranks, copies, width = plan.ranks, plan.copies, plan.width
    totals = [half.reshape(copies, -1, 2, plan.height, width) for half in halves]

    def plane_part(target_replica, target_chip):
        parts = []
        for total in totals:
            some = lax.dynamic_index_in_dim(total, target_replica, 0, keepdims=False)
            parts.append(lax.dynamic_index_in_dim(some, target_chip, 1, keepdims=False))
        return jnp.concatenate(parts, axis=0)

    plane = plane_part(replica, chip)
    for turn in range(copies):
        for flip in range(2):
            if turn == 0 and flip == 0:
                continue
            steps = [
                (r * ranks + i, ((r + turn) % copies) * ranks + (i ^ (2 * flip)))
                for r in range(copies)
                for i in range(ranks)
            ]
            sent = plane_part((replica + turn) % copies, (chip + flip) % 2)
            plane = plane + lax.ppermute(sent, ("dp", "context"), steps)
    return plane


def group_sum(plan, plane):
    _, _, group = device_place()
    result = lax.dynamic_index_in_dim(plane, group, 0, keepdims=False)
    for turn in range(1, plan.groups):
        steps = [(i, (i + 4 * turn) % plan.ranks) for i in range(plan.ranks)]
        sent = lax.dynamic_index_in_dim(plane, (group + turn) % plan.groups, 0, keepdims=False)
        result = result + lax.ppermute(sent, "context", steps)
    return result


def select_group(plan, got):
    _, _, group = device_place()
    prefix = suffix = jnp.zeros_like(got[0])
    for hop, state in enumerate(got):
        prefix = jnp.where(group == hop + 1, state, prefix)
        suffix = jnp.where(group == plan.groups - 2 - hop, state, suffix)
    return jnp.stack([prefix, suffix])


def scan_alone(plan, group_state):
    before = jnp.zeros_like(group_state)
    for hop in range(plan.groups - 1):
        if plan.groups % 2:
            up, down = chain_split(plan, before + group_state, hop)
            before = before + jnp.stack([up, down])
    return before


def after(value, *others):
    return lax.optimization_barrier((value, *others))[0]


def per_device(queries, key_rows, value_rows, out_grad, maps):
    tokens = queries.shape[1]
    heads, width, _ = maps.shape
    plan = Plan(heads, width, tokens, lax.axis_size("context"), lax.axis_size("dp"))
    rows = [x.reshape(tokens, heads * width) for x in (queries, key_rows, value_rows, out_grad)]
    core, chip, group = device_place()
    side = jnp.arange(2).reshape(2, 1, 1, 1)
    chunks, hops, last = range(plan.chunks), plan.groups - 1, plan.chunks - 1

    kept, from_core, given, terms = [], [], [], []
    total, from_chip, group_state = [], [], []
    for chunk in chunks:
        matrices = after(maps, given[-1]) if chunk else maps
        sent, kept_here, given_here = block_states(plan, chunk, rows, matrices)
        kept.append(kept_here)
        from_core.append(swap_core(plan, sent))
        given_here = given_here + from_core[chunk][1]
        given.append(given_here)
        total.append(kept_here[0] + from_core[chunk][0])
        from_chip.append(swap_chip(plan, given_here))
        group_state.append(total[chunk] + from_chip[chunk])
    terms.append(inner(plan, 0, rows, after(maps, given[last])))

    def for_other_chip(chunk, before):
        return before + jnp.where(side == chip, total[chunk], 0.0)

    def for_other_core(chunk, turn, state):
        return state + jnp.where(side == core, kept[chunk][turn], 0.0)

    before, got, down = [None] * plan.chunks, [[] for _ in chunks], [None] * plan.chunks
    if plan.groups % 2:
        for chunk in chunks:
            before[chunk] = scan_alone(plan, group_state[chunk])
            down[chunk] = swap_chip(plan, for_other_chip(chunk, before[chunk]))
    else:
        ahead = behind = given[last]
        for stage in range(hops + last):
            for chunk in chunks:
                hop = stage - chunk
                if chunk == 0 and hop == hops:
                    before[0] = select_group(plan, got[0])
                    ahead = for_other_chip(0, before[0])
                    down[0] = swap_chip(plan, ahead)
                if not 0 <= hop < hops:
                    continue
                send = jnp.where(group == hop, group_state[chunk][0], group_state[chunk][1])
                if hop:
                    send = send + got[chunk][-1]
                if chunk and hop == 1:
                    terms.append(inner(plan, last, rows, after(maps, behind)))
                if chunk:
                    behind = send = after(send, ahead, *(terms[1] if hop == hops - 1 else ()))
                elif last:
                    ahead = send = after(send, *(terms[0] if hop == 1 else (behind,)))
                got[chunk].append(chain_swap(plan, send, hop))
        if last:
            got[last][-1] = after(got[last][-1], for_other_core(0, 1, down[0]))
        before[last] = select_group(plan, got[last])
        down[last] = swap_chip(plan, for_other_chip(last, before[last]))

    if len(terms) < plan.chunks:
        terms.append(inner(plan, last, rows, maps))
    halves, done = [], ()
    for chunk in chunks:
        states = [before[chunk] + jnp.where(side != chip, from_chip[chunk], 0.0), down[chunk]]
        for turn in range(2):
            if turn and done:
                states[1] = after(states[1], states[2], *done)
            states.append(swap_core(plan, for_other_core(chunk, turn, states[turn])))
        if halves:
            states[3] = after(states[3], *halves)
        for_mate, own = maps_term(plan, states, from_core[chunk], *terms[chunk])
        halves.append(own + swap_core(plan, for_mate))
        done = output_rows(plan, chunk, rows, maps, states, from_core[chunk], done)
    plane = after(plane_sums(plan, halves), *done)
    query_grad, key_grad, value_grad = done
    maps_grad = group_sum(plan, plane) * plan.norm
    return (query_grad[None], key_grad[None], value_grad[None], maps_grad)


def solution(mesh):
    in_specs = (
        P("dp", "context", None),
        P("dp", "context", None),
        P("dp", "context", None),
        P("dp", "context", None),
        P(),
    )
    out_specs = (
        P("dp", "context", None),
        P("dp", "context", None),
        P("dp", "context", None),
        P(("dp", "context"), None),
    )
    return jax.shard_map(
        per_device, mesh=mesh, in_specs=in_specs, out_specs=out_specs, check_vma=False
    )
```

```python
import functools
import math

import jax
import jax.numpy as jnp
from jax import lax
from jax.experimental import pallas as pl
from jax.experimental.pallas import tpu as pltpu
from jax.sharding import PartitionSpec as P

F32 = jnp.float32
BF16 = jnp.bfloat16
VMEM_LIMIT = 57 * 1024 * 1024
MIDDLE_LIMIT = 51 * 1024 * 1024
STATES_LIMIT = 53 * 1024 * 1024
SMALL_LIMIT = 16 * 1024 * 1024
LIGHT = 0.01


class Plan:
    def __init__(self, heads, width, tokens, ranks, copies):
        self.heads, self.width, self.tokens = heads, width, tokens
        self.ranks, self.copies = ranks, copies
        self.groups = ranks // 4
        per_copy = heads // copies if heads % copies == 0 else 0
        self.chunks = 2 if per_copy and per_copy % 2 == 0 and self.groups % 2 == 0 else 1
        self.in_chunk = heads // self.chunks
        self.quarter = self.in_chunk // 4
        self.run = per_copy // self.chunks if self.chunks > 1 else self.in_chunk
        self.stride = per_copy if self.chunks > 1 else 0
        self.height = heads * width // (copies * ranks)
        self.factor = 1.0 / math.sqrt(width * tokens * ranks)
        self.norm = 1.0 / math.sqrt(copies * tokens * ranks)

    def head(self, chunk, place):
        return (place // self.run) * self.stride + chunk * self.run + place % self.run


def device_place():
    index = lax.axis_index("context")
    return index % 2, (index // 2) % 2, index // 4


def dot(left, right, left_dim=1, right_dim=0):
    return lax.dot_general(
        left, right, (((left_dim,), (right_dim,)), ((), ())), preferred_element_type=F32
    )


def call(body, operands, shapes, flops, scratch, copies, aliases=None, near=(), near_out=(), limit=VMEM_LIMIT, weight=1.0):
    moved = sum(x.size * x.dtype.itemsize for x in list(operands) + list(shapes))

    def specs(count, in_vmem):
        return [
            pl.BlockSpec(memory_space=pltpu.VMEM if n in in_vmem else pltpu.HBM)
            for n in range(count)
        ]

    return pl.pallas_call(
        body,
        out_shape=shapes,
        in_specs=specs(len(operands), near),
        out_specs=specs(len(shapes), near_out),
        scratch_shapes=list(scratch) + [pltpu.SemaphoreType.DMA((copies,))],
        input_output_aliases=aliases or {},
        compiler_params=pltpu.CompilerParams(vmem_limit_bytes=limit),
        cost_estimate=pl.CostEstimate(
            flops=int(flops * weight), bytes_accessed=int(moved * weight), transcendentals=0
        ),
    )(*operands)


class Copies:
    def __init__(self, sems):
        self.sems, self.used = sems, 0

    def start(self, source, target):
        copy = pltpu.make_async_copy(source, target, self.sems.at[self.used])
        self.used += 1
        copy.start()
        return copy


def wait(copies):
    for copy in copies:
        copy.wait()


def matmuls(plan, count):
    return 2 * count * plan.tokens * plan.width * plan.width


def load_chunk(plan, copies, chunk, offset, row_refs, maps_ref, row_bufs, maps_buf):
    width, started = plan.width, []
    for first in range(0, plan.in_chunk, plan.run):
        head = plan.head(chunk, first)
        source, target = pl.ds(head, plan.run), pl.ds(offset + first, plan.run)
        started.append(copies.start(maps_ref.at[source], maps_buf.at[target]))
        source = pl.ds(head * width, plan.run * width)
        target = pl.ds((offset + first) * width, plan.run * width)
        for ref, buf in zip(row_refs, row_bufs):
            started.append(copies.start(ref.at[:, source], buf.at[:, target]))
    return started


def chunk_copies(plan):
    return 5 * (plan.in_chunk // plan.run)


def row_scratch(plan, count):
    rows = [pltpu.VMEM((plan.tokens, count * plan.width), BF16)] * 4
    return rows + [pltpu.VMEM((count, plan.width, plan.width), BF16)]


def head_of(buf, place, width):
    return buf[:, place * width : (place + 1) * width]


def quarter_of(plan, place):
    core, chip, _ = device_place()
    low = place // plan.quarter
    core_turn = 1 - core if low % 2 else core
    chip_turn = 1 - chip if low // 2 else chip
    return core_turn, chip_turn, place % plan.quarter


def states_kernel(plan, chunk, *refs):
    row_refs, maps_ref, sent_ref, kept_ref, given_ref = refs[:4], refs[4], refs[5], refs[6], refs[7]
    row_bufs, maps_buf, sems = refs[8:12], refs[12], refs[13]
    copies, width = Copies(sems), plan.width
    started = load_chunk(plan, copies, chunk, 0, row_refs, maps_ref, row_bufs, maps_buf)
    q_buf, k_buf, v_buf, g_buf = row_bufs
    size = 5 * max(1, 4 // plan.run)
    for first in range(0, plan.in_chunk, 4):
        places = range(first, first + 4)
        wait(started[:size])
        started = started[size:]
        feats_key = [dot(head_of(k_buf, n, width), maps_buf[n]).astype(BF16) for n in places]
        feats_query = [dot(head_of(q_buf, n, width), maps_buf[n]).astype(BF16) for n in places]
        key_states = [
            dot(feat, head_of(v_buf, n, width), 0, 0) for feat, n in zip(feats_key, places)
        ]
        query_states = [
            dot(feat, head_of(g_buf, n, width), 0, 0) for feat, n in zip(feats_query, places)
        ]
        for place, key_state, query_state in zip(places, key_states, query_states):
            core_turn, chip_turn, i = quarter_of(plan, place)

            @pl.when(core_turn == 1)
            def _():
                sent_ref[chip_turn, 0, i] = key_state
                sent_ref[chip_turn, 1, i] = query_state

            @pl.when(core_turn == 0)
            def _():
                kept_ref[chip_turn, 0, i] = key_state
                kept_ref[chip_turn, 1, i] = query_state
    given_ref[...] = kept_ref[1]


def block_states(plan, chunk, rows, maps):
    shape = (2, 2, plan.quarter, plan.width, plan.width)
    state = jax.ShapeDtypeStruct(shape, F32)
    return call(
        functools.partial(states_kernel, plan, chunk),
        (*rows, maps),
        [state, state, jax.ShapeDtypeStruct(shape[1:], F32)],
        matmuls(plan, 4 * plan.in_chunk),
        row_scratch(plan, plan.in_chunk),
        chunk_copies(plan),
        near_out=(0, 1, 2),
        limit=STATES_LIMIT,
    )


def causal_mask(tokens):
    row = lax.broadcasted_iota(jnp.int32, (tokens, tokens), 0)
    column = lax.broadcasted_iota(jnp.int32, (tokens, tokens), 1)
    return row >= column


def inner_kernel(plan, chunk, *refs):
    row_refs, maps_ref, base_ref, pair_ref = refs[:4], refs[4], refs[5], refs[6]
    row_bufs, maps_buf, base_buf, pair_buf, sems = refs[7:11], refs[11], refs[12], refs[13], refs[14]
    copies, width = Copies(sems), plan.width
    started = load_chunk(plan, copies, chunk, 0, row_refs, maps_ref, row_bufs, maps_buf)
    causal = causal_mask(plan.tokens)
    written = []
    size = 5 * max(1, 4 // plan.run)
    for first in range(0, plan.in_chunk, 4):
        places = range(first, first + 4)
        wait(started[:size])
        started = started[size:]
        queries, keys, values, grads = [
            [head_of(buf, n, width) for n in places] for buf in row_bufs
        ]
        scores = [
            jnp.where(causal, dot(grad, value, 1, 1), 0.0).astype(BF16)
            for grad, value in zip(grads, values)
        ]
        feats_query = [dot(x, maps_buf[n]).astype(BF16) for x, n in zip(queries, places)]
        feats_key = [dot(x, maps_buf[n]).astype(BF16) for x, n in zip(keys, places)]
        grads_a = [dot(s, feat).astype(BF16) for s, feat in zip(scores, feats_key)]
        grads_b = [dot(s, feat, 0, 0).astype(BF16) for s, feat in zip(scores, feats_query)]
        for n, place in enumerate(places):
            pair_buf[0, place] = dot(queries[n], grads[n], 0, 0).astype(BF16)
            pair_buf[1, place] = dot(keys[n], values[n], 0, 0).astype(BF16)
            base_buf[place] = dot(queries[n], grads_a[n], 0, 0) + dot(keys[n], grads_b[n], 0, 0)
        part = pl.ds(first, 4)
        written.append(copies.start(base_buf.at[part], base_ref.at[part]))
        written.append(copies.start(pair_buf.at[:, part], pair_ref.at[:, part]))
    wait(written)


def inner(plan, chunk, rows, maps):
    square = (plan.in_chunk, plan.width, plan.width)
    return call(
        functools.partial(inner_kernel, plan, chunk),
        (*rows, maps),
        [jax.ShapeDtypeStruct(square, F32), jax.ShapeDtypeStruct((2,) + square, BF16)],
        matmuls(plan, 9 * plan.in_chunk),
        row_scratch(plan, plan.in_chunk)
        + [pltpu.VMEM(square, F32), pltpu.VMEM((2,) + square, BF16)],
        chunk_copies(plan) + plan.in_chunk // 2,
    )


def finish_states(plan, state_refs, extra_buf, state_buf):
    core, _, _ = device_place()
    for core_turn in range(2):
        for chip_turn in range(2):
            for side in range(2):
                state = state_refs[2 * core_turn + chip_turn][side]
                if core_turn == 0:
                    wanted = core == 1 - side
                    state = state + jnp.where(wanted, extra_buf[chip_turn, side], 0.0)
                state_buf[core_turn, chip_turn, side] = state.astype(BF16)


def state_scratch(plan):
    shape = (2, 2, plan.quarter, plan.width, plan.width)
    return [pltpu.VMEM(shape, F32), pltpu.VMEM((2,) + shape, BF16)]


def term_kernel(plan, *refs):
    state_refs, extra_ref, base_ref, pair_ref = refs[:4], refs[4], refs[5], refs[6]
    out_refs = refs[7:-5]
    extra_buf, state_buf, base_buf, pair_buf, sems = refs[-5:]
    copies = Copies(sems)
    core, _, _ = device_place()
    extra_copy = copies.start(extra_ref, extra_buf)
    others = [copies.start(pair_ref, pair_buf), copies.start(base_ref, base_buf)]
    extra_copy.wait()
    finish_states(plan, state_refs, extra_buf, state_buf)
    wait(others)
    half = plan.width // 2
    for first in range(0, plan.in_chunk, 4):
        places = range(first, first + 4)
        where = [quarter_of(plan, place) for place in places]
        products = [
            dot(pair_buf[side, place], state_buf[c, y, side, i], 1, 1)
            for place, (c, y, i) in zip(places, where)
            for side in range(2)
        ]
        for n, place in enumerate(places):
            term = plan.factor * (base_buf[place] + products[2 * n] + products[2 * n + 1])
            if len(out_refs) == 1:
                out_refs[0][place] = term
            else:
                out_refs[0][place] = jnp.where(core == 0, term[half:], term[:half])
                out_refs[1][place] = jnp.where(core == 0, term[:half], term[half:])


def maps_term(plan, states, extra, base, pair):
    width = plan.width
    square = (plan.in_chunk, width, width)
    in_halves = 2 * plan.height == width and plan.height % 8 == 0
    shapes = [(plan.in_chunk, width // 2, width)] * 2 if in_halves else [square]
    outs = call(
        functools.partial(term_kernel, plan),
        (*states, extra, base, pair),
        [jax.ShapeDtypeStruct(shape, F32) for shape in shapes],
        matmuls(plan, 2 * plan.in_chunk),
        state_scratch(plan) + [pltpu.VMEM(square, F32), pltpu.VMEM((2,) + square, BF16)],
        3,
        near=range(4),
        near_out=range(2),
        limit=SMALL_LIMIT,
        weight=LIGHT,
    )
    if in_halves:
        return outs
    core, _, _ = device_place()
    parts = outs[0].reshape(-1, 2, plan.height, width)
    return [
        lax.dynamic_index_in_dim(parts, turn, 1, keepdims=False) for turn in (1 - core, core)
    ]


def rows_kernel(plan, chunk, *refs):
    state_refs, extra_ref, row_refs, maps_ref = refs[:4], refs[4], refs[5:9], refs[9]
    refs = refs[10 + (3 if chunk else 0) :]
    out_refs, row_bufs, maps_buf = refs[:3], refs[3:7], refs[7]
    extra_buf, state_buf, out_bufs, sems = refs[8], refs[9], refs[10:13], refs[13]
    copies, width = Copies(sems), plan.width
    extra_copy = copies.start(extra_ref, extra_buf)
    started = load_chunk(plan, copies, chunk, 0, row_refs, maps_ref, row_bufs, maps_buf)
    causal = causal_mask(plan.tokens)
    extra_copy.wait()
    finish_states(plan, state_refs, extra_buf, state_buf)
    written = []
    size = 5 * max(1, 4 // plan.run)
    for first in range(0, plan.in_chunk, 4):
        places = range(first, first + 4)
        wait(started[:size])
        started = started[size:]
        queries, keys, values, grads = [
            [head_of(buf, place, width) for place in places] for buf in row_bufs
        ]
        where = [quarter_of(plan, place) for place in places]
        prefixes = [state_buf[c, y, 0, i] for c, y, i in where]
        suffixes = [state_buf[c, y, 1, i] for c, y, i in where]
        matrices = [maps_buf[place] for place in places]
        scores_gv = [
            jnp.where(causal, dot(grad, value, 1, 1), 0.0).astype(BF16)
            for grad, value in zip(grads, values)
        ]
        feats_query = [dot(x, matrix).astype(BF16) for x, matrix in zip(queries, matrices)]
        feats_key = [dot(x, matrix).astype(BF16) for x, matrix in zip(keys, matrices)]
        scores_ab = [
            jnp.where(causal, dot(left, right, 1, 1), 0.0).astype(BF16)
            for left, right in zip(feats_query, feats_key)
        ]
        grads_a = [
            (plan.factor * (dot(score, feat) + dot(grad, prefix, 1, 1))).astype(BF16)
            for score, feat, grad, prefix in zip(scores_gv, feats_key, grads, prefixes)
        ]
        grads_b = [
            (plan.factor * (dot(score, feat, 0, 0) + dot(value, suffix, 1, 1))).astype(BF16)
            for score, feat, value, suffix in zip(scores_gv, feats_query, values, suffixes)
        ]
        for n, place in enumerate(places):
            at = slice(place * width, (place + 1) * width)
            out_bufs[0][:, at] = dot(grads_a[n], matrices[n], 1, 1).astype(BF16)
            out_bufs[1][:, at] = dot(grads_b[n], matrices[n], 1, 1).astype(BF16)
            value_grad = dot(scores_ab[n], grads[n], 0, 0) + dot(feats_key[n], suffixes[n])
            out_bufs[2][:, at] = (plan.factor * value_grad).astype(BF16)
        for part in range(first, first + 4, min(4, plan.run)):
            count = min(4, plan.run)
            source = pl.ds(part * width, count * width)
            target = pl.ds(plan.head(chunk, part) * width, count * width)
            for buf, ref in zip(out_bufs, out_refs):
                written.append(copies.start(buf.at[:, source], ref.at[:, target]))
    wait(written)


def output_rows(plan, chunk, rows, maps, states, extra, done):
    shape = jax.ShapeDtypeStruct((plan.tokens, plan.heads * plan.width), BF16)
    narrow = [pltpu.VMEM((plan.tokens, plan.in_chunk * plan.width), BF16)] * 3
    return call(
        functools.partial(rows_kernel, plan, chunk),
        (*states, extra, *rows, maps, *done),
        [shape] * 3,
        matmuls(plan, 12 * plan.in_chunk),
        row_scratch(plan, plan.in_chunk) + state_scratch(plan) + narrow,
        chunk_copies(plan) + 3 * plan.in_chunk + 1,
        {10: 0, 11: 1, 12: 2} if done else None,
        near=range(4),
        limit=MIDDLE_LIMIT,
        weight=LIGHT,
    )


def swap_core(plan, state):
    return lax.ppermute(state, "context", [(i, i ^ 1) for i in range(plan.ranks)])


def swap_chip(plan, state):
    return lax.ppermute(state, "context", [(i, i ^ 2) for i in range(plan.ranks)])


def chain_swap(plan, state, hop):
    mirror = plan.groups - 1 - hop
    steps = [(i, i ^ 1) for i in range(plan.ranks)]
    for low in range(4):
        for left in (hop, mirror - 1):
            a, b = 4 * left + low, 4 * left + 4 + low
            steps[a], steps[b] = (a, b), (b, a)
    return lax.ppermute(state, "context", steps)


def chain_split(plan, state, hop):
    mirror = plan.groups - 1 - hop
    up = [(4 * hop + low, 4 * hop + 4 + low) for low in range(4)]
    down = [(4 * mirror + low, 4 * mirror - 4 + low) for low in range(4)]
    return lax.ppermute(state[0], "context", up), lax.ppermute(state[1], "context", down)


def plane_sums(plan, halves):
    _, chip, _ = device_place()
    replica = lax.axis_index("dp")
    ranks, copies, width = plan.ranks, plan.copies, plan.width
    totals = [half.reshape(copies, -1, 2, plan.height, width) for half in halves]

    def plane_part(target_replica, target_chip):
        parts = []
        for total in totals:
            some = lax.dynamic_index_in_dim(total, target_replica, 0, keepdims=False)
            parts.append(lax.dynamic_index_in_dim(some, target_chip, 1, keepdims=False))
        return jnp.concatenate(parts, axis=0)

    plane = plane_part(replica, chip)
    for turn in range(copies):
        for flip in range(2):
            if turn == 0 and flip == 0:
                continue
            steps = [
                (r * ranks + i, ((r + turn) % copies) * ranks + (i ^ (2 * flip)))
                for r in range(copies)
                for i in range(ranks)
            ]
            sent = plane_part((replica + turn) % copies, (chip + flip) % 2)
            plane = plane + lax.ppermute(sent, ("dp", "context"), steps)
    return plane


def group_sum(plan, plane):
    _, _, group = device_place()
    result = lax.dynamic_index_in_dim(plane, group, 0, keepdims=False)
    for turn in range(1, plan.groups):
        steps = [(i, (i + 4 * turn) % plan.ranks) for i in range(plan.ranks)]
        sent = lax.dynamic_index_in_dim(plane, (group + turn) % plan.groups, 0, keepdims=False)
        result = result + lax.ppermute(sent, "context", steps)
    return result


def select_group(plan, got):
    _, _, group = device_place()
    prefix = suffix = jnp.zeros_like(got[0])
    for hop, state in enumerate(got):
        prefix = jnp.where(group == hop + 1, state, prefix)
        suffix = jnp.where(group == plan.groups - 2 - hop, state, suffix)
    return jnp.stack([prefix, suffix])


def scan_alone(plan, group_state):
    before = jnp.zeros_like(group_state)
    for hop in range(plan.groups - 1):
        if plan.groups % 2:
            up, down = chain_split(plan, before + group_state, hop)
            before = before + jnp.stack([up, down])
    return before


def after(value, *others):
    return lax.optimization_barrier((value, *others))[0]


def per_device(queries, key_rows, value_rows, out_grad, maps):
    tokens = queries.shape[1]
    heads, width, _ = maps.shape
    plan = Plan(heads, width, tokens, lax.axis_size("context"), lax.axis_size("dp"))
    rows = [x.reshape(tokens, heads * width) for x in (queries, key_rows, value_rows, out_grad)]
    core, chip, group = device_place()
    side = jnp.arange(2).reshape(2, 1, 1, 1)
    chunks, hops, last = range(plan.chunks), plan.groups - 1, plan.chunks - 1

    kept, from_core, given = [], [], []
    total, from_chip = [], []
    for chunk in chunks:
        matrices = after(maps, given[-1]) if chunk else maps
        sent, kept_here, given_here = block_states(plan, chunk, rows, matrices)
        kept.append(kept_here)
        from_core.append(swap_core(plan, sent))
        given_here = given_here + from_core[chunk][1]
        given.append(given_here)
        total.append(kept_here[0] + from_core[chunk][0])
        from_chip.append(swap_chip(plan, given_here))
    ready = [given[-1]] * last + [sent]
    terms = [inner(plan, chunk, rows, after(maps, ready[chunk])) for chunk in chunks]
    if last:
        from_chip[0] = after(from_chip[0], *terms[last])
    group_state = [total[chunk] + from_chip[chunk] for chunk in chunks]

    def for_other_chip(chunk, before):
        return before + jnp.where(side == chip, total[chunk], 0.0)

    def for_other_core(chunk, turn, state):
        return state + jnp.where(side == core, kept[chunk][turn], 0.0)

    before, got, down = [None] * plan.chunks, [[] for _ in chunks], [None] * plan.chunks
    if plan.groups % 2:
        for chunk in chunks:
            before[chunk] = scan_alone(plan, group_state[chunk])
            down[chunk] = swap_chip(plan, for_other_chip(chunk, before[chunk]))
    else:
        ahead = behind = given[last]
        for stage in range(hops + last):
            for chunk in chunks:
                hop = stage - chunk
                if chunk == 0 and hop == hops:
                    before[0] = select_group(plan, got[0])
                    ahead = for_other_chip(0, before[0])
                    down[0] = swap_chip(plan, ahead)
                if not 0 <= hop < hops:
                    continue
                send = jnp.where(group == hop, group_state[chunk][0], group_state[chunk][1])
                if hop:
                    send = send + got[chunk][-1]
                if chunk:
                    behind = send = after(send, ahead)
                elif last:
                    ahead = send = after(send, *(terms[0] if hop == 1 else (behind,)))
                got[chunk].append(chain_swap(plan, send, hop))
        if last:
            got[last][-1] = after(got[last][-1], for_other_core(0, 1, down[0]))
        before[last] = select_group(plan, got[last])
        down[last] = swap_chip(plan, for_other_chip(last, before[last]))

    halves, done = [], ()
    for chunk in chunks:
        states = [before[chunk] + jnp.where(side != chip, from_chip[chunk], 0.0), down[chunk]]
        for turn in range(2):
            if turn and done:
                states[1] = after(states[1], states[2], *done)
            states.append(swap_core(plan, for_other_core(chunk, turn, states[turn])))
        if halves:
            states[3] = after(states[3], *halves)
        for_mate, own = maps_term(plan, states, from_core[chunk], *terms[chunk])
        halves.append(own + swap_core(plan, for_mate))
        matrices = after(maps, for_mate)
        done = output_rows(plan, chunk, rows, matrices, states, from_core[chunk], done)
    plane = after(plane_sums(plan, halves), *done)
    query_grad, key_grad, value_grad = done
    maps_grad = group_sum(plan, plane) * plan.norm
    return (query_grad[None], key_grad[None], value_grad[None], maps_grad)


def solution(mesh):
    in_specs = (
        P("dp", "context", None),
        P("dp", "context", None),
        P("dp", "context", None),
        P("dp", "context", None),
        P(),
    )
    out_specs = (
        P("dp", "context", None),
        P("dp", "context", None),
        P("dp", "context", None),
        P(("dp", "context"), None),
    )
    return jax.shard_map(
        per_device, mesh=mesh, in_specs=in_specs, out_specs=out_specs, check_vma=False
    )
```

```python
import functools
import math

import jax
import jax.numpy as jnp
from jax import lax
from jax.experimental import pallas as pl
from jax.experimental.pallas import tpu as pltpu
from jax.sharding import PartitionSpec as P

F32 = jnp.float32
BF16 = jnp.bfloat16
VMEM_LIMIT = 57 * 1024 * 1024
MIDDLE_LIMIT = 51 * 1024 * 1024
STATES_LIMIT = 53 * 1024 * 1024
SMALL_LIMIT = 16 * 1024 * 1024
LIGHT = 0.01


class Plan:
    def __init__(self, heads, width, tokens, ranks, copies):
        self.heads, self.width, self.tokens = heads, width, tokens
        self.ranks, self.copies = ranks, copies
        self.groups = ranks // 4
        per_copy = heads // copies if heads % copies == 0 else 0
        self.chunks = 2 if per_copy and per_copy % 2 == 0 and self.groups % 2 == 0 else 1
        self.in_chunk = heads // self.chunks
        self.quarter = self.in_chunk // 4
        self.run = per_copy // self.chunks if self.chunks > 1 else self.in_chunk
        self.stride = per_copy if self.chunks > 1 else 0
        self.height = heads * width // (copies * ranks)
        self.factor = 1.0 / math.sqrt(width * tokens * ranks)
        self.norm = 1.0 / math.sqrt(copies * tokens * ranks)

    def head(self, chunk, place):
        return (place // self.run) * self.stride + chunk * self.run + place % self.run


def device_place():
    index = lax.axis_index("context")
    return index % 2, (index // 2) % 2, index // 4


def dot(left, right, left_dim=1, right_dim=0):
    return lax.dot_general(
        left, right, (((left_dim,), (right_dim,)), ((), ())), preferred_element_type=F32
    )


def call(body, operands, shapes, flops, scratch, copies, aliases=None, near=(), near_out=(), limit=VMEM_LIMIT, weight=1.0):
    moved = sum(x.size * x.dtype.itemsize for x in list(operands) + list(shapes))

    def specs(count, in_vmem):
        return [
            pl.BlockSpec(memory_space=pltpu.VMEM if n in in_vmem else pltpu.HBM)
            for n in range(count)
        ]

    return pl.pallas_call(
        body,
        out_shape=shapes,
        in_specs=specs(len(operands), near),
        out_specs=specs(len(shapes), near_out),
        scratch_shapes=list(scratch) + [pltpu.SemaphoreType.DMA((copies,))],
        input_output_aliases=aliases or {},
        compiler_params=pltpu.CompilerParams(vmem_limit_bytes=limit),
        cost_estimate=pl.CostEstimate(
            flops=int(flops * weight), bytes_accessed=int(moved * weight), transcendentals=0
        ),
    )(*operands)


class Copies:
    def __init__(self, sems):
        self.sems, self.used = sems, 0

    def start(self, source, target):
        copy = pltpu.make_async_copy(source, target, self.sems.at[self.used])
        self.used += 1
        copy.start()
        return copy


def wait(copies):
    for copy in copies:
        copy.wait()


def matmuls(plan, count):
    return 2 * count * plan.tokens * plan.width * plan.width


def load_chunk(plan, copies, chunk, offset, row_refs, maps_ref, row_bufs, maps_buf):
    width, started = plan.width, []
    for first in range(0, plan.in_chunk, plan.run):
        head = plan.head(chunk, first)
        source, target = pl.ds(head, plan.run), pl.ds(offset + first, plan.run)
        started.append(copies.start(maps_ref.at[source], maps_buf.at[target]))
        source = pl.ds(head * width, plan.run * width)
        target = pl.ds((offset + first) * width, plan.run * width)
        for ref, buf in zip(row_refs, row_bufs):
            started.append(copies.start(ref.at[:, source], buf.at[:, target]))
    return started


def chunk_copies(plan):
    return 5 * (plan.in_chunk // plan.run)


def row_scratch(plan, count):
    rows = [pltpu.VMEM((plan.tokens, count * plan.width), BF16)] * 4
    return rows + [pltpu.VMEM((count, plan.width, plan.width), BF16)]


def head_of(buf, place, width):
    return buf[:, place * width : (place + 1) * width]


def quarter_of(plan, place):
    core, chip, _ = device_place()
    low = place // plan.quarter
    core_turn = 1 - core if low % 2 else core
    chip_turn = 1 - chip if low // 2 else chip
    return core_turn, chip_turn, place % plan.quarter


def states_kernel(plan, chunk, *refs):
    row_refs, maps_ref, sent_ref, kept_ref, given_ref = refs[:4], refs[4], refs[5], refs[6], refs[7]
    row_bufs, maps_buf, sems = refs[8:12], refs[12], refs[13]
    copies, width = Copies(sems), plan.width
    started = load_chunk(plan, copies, chunk, 0, row_refs, maps_ref, row_bufs, maps_buf)
    q_buf, k_buf, v_buf, g_buf = row_bufs
    size = 5 * max(1, 4 // plan.run)
    for first in range(0, plan.in_chunk, 4):
        places = range(first, first + 4)
        wait(started[:size])
        started = started[size:]
        feats_key = [dot(head_of(k_buf, n, width), maps_buf[n]).astype(BF16) for n in places]
        feats_query = [dot(head_of(q_buf, n, width), maps_buf[n]).astype(BF16) for n in places]
        key_states = [
            dot(feat, head_of(v_buf, n, width), 0, 0) for feat, n in zip(feats_key, places)
        ]
        query_states = [
            dot(feat, head_of(g_buf, n, width), 0, 0) for feat, n in zip(feats_query, places)
        ]
        for place, key_state, query_state in zip(places, key_states, query_states):
            core_turn, chip_turn, i = quarter_of(plan, place)

            @pl.when(core_turn == 1)
            def _():
                sent_ref[chip_turn, 0, i] = key_state
                sent_ref[chip_turn, 1, i] = query_state

            @pl.when(core_turn == 0)
            def _():
                kept_ref[chip_turn, 0, i] = key_state
                kept_ref[chip_turn, 1, i] = query_state
    given_ref[...] = kept_ref[1]


def block_states(plan, chunk, rows, maps):
    shape = (2, 2, plan.quarter, plan.width, plan.width)
    state = jax.ShapeDtypeStruct(shape, F32)
    return call(
        functools.partial(states_kernel, plan, chunk),
        (*rows, maps),
        [state, state, jax.ShapeDtypeStruct(shape[1:], F32)],
        matmuls(plan, 4 * plan.in_chunk),
        row_scratch(plan, plan.in_chunk),
        chunk_copies(plan),
        near_out=(0, 1, 2),
        limit=STATES_LIMIT,
    )


def causal_mask(tokens):
    row = lax.broadcasted_iota(jnp.int32, (tokens, tokens), 0)
    column = lax.broadcasted_iota(jnp.int32, (tokens, tokens), 1)
    return row >= column


def inner_kernel(plan, chunk, *refs):
    row_refs, maps_ref, base_ref, pair_ref = refs[:4], refs[4], refs[5], refs[6]
    row_bufs, maps_buf, base_buf, pair_buf, sems = refs[7:11], refs[11], refs[12], refs[13], refs[14]
    copies, width = Copies(sems), plan.width
    started = load_chunk(plan, copies, chunk, 0, row_refs, maps_ref, row_bufs, maps_buf)
    causal = causal_mask(plan.tokens)
    written = []
    size = 5 * max(1, 4 // plan.run)
    for first in range(0, plan.in_chunk, 4):
        places = range(first, first + 4)
        wait(started[:size])
        started = started[size:]
        queries, keys, values, grads = [
            [head_of(buf, n, width) for n in places] for buf in row_bufs
        ]
        scores = [
            jnp.where(causal, dot(grad, value, 1, 1), 0.0).astype(BF16)
            for grad, value in zip(grads, values)
        ]
        feats_query = [dot(x, maps_buf[n]).astype(BF16) for x, n in zip(queries, places)]
        feats_key = [dot(x, maps_buf[n]).astype(BF16) for x, n in zip(keys, places)]
        grads_a = [dot(s, feat).astype(BF16) for s, feat in zip(scores, feats_key)]
        grads_b = [dot(s, feat, 0, 0).astype(BF16) for s, feat in zip(scores, feats_query)]
        for n, place in enumerate(places):
            pair_buf[0, place] = dot(queries[n], grads[n], 0, 0).astype(BF16)
            pair_buf[1, place] = dot(keys[n], values[n], 0, 0).astype(BF16)
            base_buf[place] = dot(queries[n], grads_a[n], 0, 0) + dot(keys[n], grads_b[n], 0, 0)
        part = pl.ds(first, 4)
        written.append(copies.start(base_buf.at[part], base_ref.at[part]))
        written.append(copies.start(pair_buf.at[:, part], pair_ref.at[:, part]))
    wait(written)


def inner(plan, chunk, rows, maps):
    square = (plan.in_chunk, plan.width, plan.width)
    return call(
        functools.partial(inner_kernel, plan, chunk),
        (*rows, maps),
        [jax.ShapeDtypeStruct(square, F32), jax.ShapeDtypeStruct((2,) + square, BF16)],
        matmuls(plan, 9 * plan.in_chunk),
        row_scratch(plan, plan.in_chunk)
        + [pltpu.VMEM(square, F32), pltpu.VMEM((2,) + square, BF16)],
        chunk_copies(plan) + plan.in_chunk // 2,
    )


def finish_states(plan, state_refs, extra_buf, state_buf):
    core, _, _ = device_place()
    for core_turn in range(2):
        for chip_turn in range(2):
            for side in range(2):
                state = state_refs[2 * core_turn + chip_turn][side]
                if core_turn == 0:
                    wanted = core == 1 - side
                    state = state + jnp.where(wanted, extra_buf[chip_turn, side], 0.0)
                state_buf[core_turn, chip_turn, side] = state.astype(BF16)


def state_scratch(plan):
    shape = (2, 2, plan.quarter, plan.width, plan.width)
    return [pltpu.VMEM(shape, F32), pltpu.VMEM((2,) + shape, BF16)]


def term_kernel(plan, *refs):
    state_refs, extra_ref, base_ref, pair_ref = refs[:4], refs[4], refs[5], refs[6]
    out_refs = refs[7:-5]
    extra_buf, state_buf, base_buf, pair_buf, sems = refs[-5:]
    copies = Copies(sems)
    core, _, _ = device_place()
    extra_copy = copies.start(extra_ref, extra_buf)
    others = [copies.start(pair_ref, pair_buf), copies.start(base_ref, base_buf)]
    extra_copy.wait()
    finish_states(plan, state_refs, extra_buf, state_buf)
    wait(others)
    half = plan.width // 2
    for first in range(0, plan.in_chunk, 4):
        places = range(first, first + 4)
        where = [quarter_of(plan, place) for place in places]
        products = [
            dot(pair_buf[side, place], state_buf[c, y, side, i], 1, 1)
            for place, (c, y, i) in zip(places, where)
            for side in range(2)
        ]
        for n, place in enumerate(places):
            term = plan.factor * (base_buf[place] + products[2 * n] + products[2 * n + 1])
            if len(out_refs) == 1:
                out_refs[0][place] = term
            else:
                out_refs[0][place] = jnp.where(core == 0, term[half:], term[:half])
                out_refs[1][place] = jnp.where(core == 0, term[:half], term[half:])


def maps_term(plan, states, extra, base, pair):
    width = plan.width
    square = (plan.in_chunk, width, width)
    in_halves = 2 * plan.height == width and plan.height % 8 == 0
    shapes = [(plan.in_chunk, width // 2, width)] * 2 if in_halves else [square]
    outs = call(
        functools.partial(term_kernel, plan),
        (*states, extra, base, pair),
        [jax.ShapeDtypeStruct(shape, F32) for shape in shapes],
        matmuls(plan, 2 * plan.in_chunk),
        state_scratch(plan) + [pltpu.VMEM(square, F32), pltpu.VMEM((2,) + square, BF16)],
        3,
        near=range(4),
        near_out=range(2),
        limit=SMALL_LIMIT,
        weight=LIGHT,
    )
    if in_halves:
        return outs
    core, _, _ = device_place()
    parts = outs[0].reshape(-1, 2, plan.height, width)
    return [
        lax.dynamic_index_in_dim(parts, turn, 1, keepdims=False) for turn in (1 - core, core)
    ]


def rows_kernel(plan, chunk, *refs):
    state_refs, extra_ref, row_refs, maps_ref = refs[:4], refs[4], refs[5:9], refs[9]
    refs = refs[10 + (3 if chunk else 0) :]
    out_refs, row_bufs, maps_buf = refs[:3], refs[3:7], refs[7]
    extra_buf, state_buf, out_bufs, sems = refs[8], refs[9], refs[10:13], refs[13]
    copies, width = Copies(sems), plan.width
    extra_copy = copies.start(extra_ref, extra_buf)
    started = load_chunk(plan, copies, chunk, 0, row_refs, maps_ref, row_bufs, maps_buf)
    causal = causal_mask(plan.tokens)
    extra_copy.wait()
    finish_states(plan, state_refs, extra_buf, state_buf)
    written = []
    size = 5 * max(1, 4 // plan.run)
    for first in range(0, plan.in_chunk, 4):
        places = range(first, first + 4)
        wait(started[:size])
        started = started[size:]
        queries, keys, values, grads = [
            [head_of(buf, place, width) for place in places] for buf in row_bufs
        ]
        where = [quarter_of(plan, place) for place in places]
        prefixes = [state_buf[c, y, 0, i] for c, y, i in where]
        suffixes = [state_buf[c, y, 1, i] for c, y, i in where]
        matrices = [maps_buf[place] for place in places]
        scores_gv = [
            jnp.where(causal, dot(grad, value, 1, 1), 0.0).astype(BF16)
            for grad, value in zip(grads, values)
        ]
        feats_query = [dot(x, matrix).astype(BF16) for x, matrix in zip(queries, matrices)]
        feats_key = [dot(x, matrix).astype(BF16) for x, matrix in zip(keys, matrices)]
        scores_ab = [
            jnp.where(causal, dot(left, right, 1, 1), 0.0).astype(BF16)
            for left, right in zip(feats_query, feats_key)
        ]
        grads_a = [
            (plan.factor * (dot(score, feat) + dot(grad, prefix, 1, 1))).astype(BF16)
            for score, feat, grad, prefix in zip(scores_gv, feats_key, grads, prefixes)
        ]
        grads_b = [
            (plan.factor * (dot(score, feat, 0, 0) + dot(value, suffix, 1, 1))).astype(BF16)
            for score, feat, value, suffix in zip(scores_gv, feats_query, values, suffixes)
        ]
        for n, place in enumerate(places):
            at = slice(place * width, (place + 1) * width)
            out_bufs[0][:, at] = dot(grads_a[n], matrices[n], 1, 1).astype(BF16)
            out_bufs[1][:, at] = dot(grads_b[n], matrices[n], 1, 1).astype(BF16)
            value_grad = dot(scores_ab[n], grads[n], 0, 0) + dot(feats_key[n], suffixes[n])
            out_bufs[2][:, at] = (plan.factor * value_grad).astype(BF16)
        for part in range(first, first + 4, min(4, plan.run)):
            count = min(4, plan.run)
            source = pl.ds(part * width, count * width)
            target = pl.ds(plan.head(chunk, part) * width, count * width)
            for buf, ref in zip(out_bufs, out_refs):
                written.append(copies.start(buf.at[:, source], ref.at[:, target]))
    wait(written)


def output_rows(plan, chunk, rows, maps, states, extra, done):
    shape = jax.ShapeDtypeStruct((plan.tokens, plan.heads * plan.width), BF16)
    narrow = [pltpu.VMEM((plan.tokens, plan.in_chunk * plan.width), BF16)] * 3
    return call(
        functools.partial(rows_kernel, plan, chunk),
        (*states, extra, *rows, maps, *done),
        [shape] * 3,
        matmuls(plan, 12 * plan.in_chunk),
        row_scratch(plan, plan.in_chunk) + state_scratch(plan) + narrow,
        chunk_copies(plan) + 3 * plan.in_chunk + 1,
        {10: 0, 11: 1, 12: 2} if done else None,
        near=range(4),
        limit=MIDDLE_LIMIT,
        weight=LIGHT,
    )


def swap_core(plan, state):
    return lax.ppermute(state, "context", [(i, i ^ 1) for i in range(plan.ranks)])


def swap_chip(plan, state):
    return lax.ppermute(state, "context", [(i, i ^ 2) for i in range(plan.ranks)])


def chain_swap(plan, state, hop):
    mirror = plan.groups - 1 - hop
    steps = [(i, i ^ 1) for i in range(plan.ranks)]
    for low in range(4):
        for left in (hop, mirror - 1):
            a, b = 4 * left + low, 4 * left + 4 + low
            steps[a], steps[b] = (a, b), (b, a)
    return lax.ppermute(state, "context", steps)


def chain_split(plan, state, hop):
    mirror = plan.groups - 1 - hop
    up = [(4 * hop + low, 4 * hop + 4 + low) for low in range(4)]
    down = [(4 * mirror + low, 4 * mirror - 4 + low) for low in range(4)]
    return lax.ppermute(state[0], "context", up), lax.ppermute(state[1], "context", down)


def plane_sums(plan, halves):
    _, chip, _ = device_place()
    replica = lax.axis_index("dp")
    ranks, copies, width = plan.ranks, plan.copies, plan.width
    totals = [half.reshape(copies, -1, 2, plan.height, width) for half in halves]

    def plane_part(target_replica, target_chip):
        parts = []
        for total in totals:
            some = lax.dynamic_index_in_dim(total, target_replica, 0, keepdims=False)
            parts.append(lax.dynamic_index_in_dim(some, target_chip, 1, keepdims=False))
        return jnp.concatenate(parts, axis=0)

    plane = plane_part(replica, chip)
    for turn in range(copies):
        for flip in range(2):
            if turn == 0 and flip == 0:
                continue
            steps = [
                (r * ranks + i, ((r + turn) % copies) * ranks + (i ^ (2 * flip)))
                for r in range(copies)
                for i in range(ranks)
            ]
            sent = plane_part((replica + turn) % copies, (chip + flip) % 2)
            plane = plane + lax.ppermute(sent, ("dp", "context"), steps)
    return plane


def group_sum(plan, plane):
    _, _, group = device_place()
    result = lax.dynamic_index_in_dim(plane, group, 0, keepdims=False)
    in_pairs = plan.groups & (plan.groups - 1) == 0
    for turn in range(1, plan.groups):

        def partner(place):
            return place ^ turn if in_pairs else (place + turn) % plan.groups

        steps = [(i, 4 * partner(i // 4) + i % 4) for i in range(plan.ranks)]
        sent = lax.dynamic_index_in_dim(plane, partner(group), 0, keepdims=False)
        result = result + lax.ppermute(sent, "context", steps)
    return result


def select_group(plan, got):
    _, _, group = device_place()
    prefix = suffix = jnp.zeros_like(got[0])
    for hop, state in enumerate(got):
        prefix = jnp.where(group == hop + 1, state, prefix)
        suffix = jnp.where(group == plan.groups - 2 - hop, state, suffix)
    return jnp.stack([prefix, suffix])


def scan_alone(plan, group_state):
    before = jnp.zeros_like(group_state)
    for hop in range(plan.groups - 1):
        if plan.groups % 2:
            up, down = chain_split(plan, before + group_state, hop)
            before = before + jnp.stack([up, down])
    return before


def after(value, *others):
    return lax.optimization_barrier((value, *others))[0]


def per_device(queries, key_rows, value_rows, out_grad, maps):
    tokens = queries.shape[1]
    heads, width, _ = maps.shape
    plan = Plan(heads, width, tokens, lax.axis_size("context"), lax.axis_size("dp"))
    rows = [x.reshape(tokens, heads * width) for x in (queries, key_rows, value_rows, out_grad)]
    core, chip, group = device_place()
    side = jnp.arange(2).reshape(2, 1, 1, 1)
    chunks, hops, last = range(plan.chunks), plan.groups - 1, plan.chunks - 1

    kept, from_core, given = [], [], []
    total, from_chip = [], []
    for chunk in chunks:
        matrices = after(maps, given[-1]) if chunk else maps
        sent, kept_here, given_here = block_states(plan, chunk, rows, matrices)
        kept.append(kept_here)
        from_core.append(swap_core(plan, sent))
        given_here = given_here + from_core[chunk][1]
        given.append(given_here)
        total.append(kept_here[0] + from_core[chunk][0])
        from_chip.append(swap_chip(plan, given_here))
    ready = [given[-1]] * last + [sent]
    terms = [inner(plan, chunk, rows, after(maps, ready[chunk])) for chunk in chunks]
    if last:
        from_chip[0] = after(from_chip[0], *terms[last])
    group_state = [total[chunk] + from_chip[chunk] for chunk in chunks]

    def for_other_chip(chunk, before):
        return before + jnp.where(side == chip, total[chunk], 0.0)

    def for_other_core(chunk, turn, state):
        return state + jnp.where(side == core, kept[chunk][turn], 0.0)

    before, got, down = [None] * plan.chunks, [[] for _ in chunks], [None] * plan.chunks
    if plan.groups % 2:
        for chunk in chunks:
            before[chunk] = scan_alone(plan, group_state[chunk])
            down[chunk] = swap_chip(plan, for_other_chip(chunk, before[chunk]))
    else:
        ahead = behind = given[last]
        for stage in range(hops + last):
            for chunk in chunks:
                hop = stage - chunk
                if chunk == 0 and hop == hops:
                    before[0] = select_group(plan, got[0])
                    ahead = for_other_chip(0, before[0])
                    down[0] = swap_chip(plan, ahead)
                if not 0 <= hop < hops:
                    continue
                send = jnp.where(group == hop, group_state[chunk][0], group_state[chunk][1])
                if hop:
                    send = send + got[chunk][-1]
                if chunk:
                    behind = send = after(send, ahead)
                elif last:
                    ahead = send = after(send, *(terms[0] if hop == 1 else (behind,)))
                got[chunk].append(chain_swap(plan, send, hop))
        if last:
            got[last][-1] = after(got[last][-1], for_other_core(0, 1, down[0]))
        before[last] = select_group(plan, got[last])
        down[last] = swap_chip(plan, for_other_chip(last, before[last]))

    halves, done = [], ()
    for chunk in chunks:
        states = [before[chunk] + jnp.where(side != chip, from_chip[chunk], 0.0), down[chunk]]
        for turn in range(2):
            if turn and done:
                states[1] = after(states[1], states[2], *done)
            states.append(swap_core(plan, for_other_core(chunk, turn, states[turn])))
        if halves:
            states[3] = after(states[3], *halves)
        for_mate, own = maps_term(plan, states, from_core[chunk], *terms[chunk])
        halves.append(own + swap_core(plan, for_mate))
        matrices = after(maps, for_mate)
        done = output_rows(plan, chunk, rows, matrices, states, from_core[chunk], done)
    plane = after(plane_sums(plan, halves), *done)
    query_grad, key_grad, value_grad = done
    maps_grad = group_sum(plan, plane) * plan.norm
    return (query_grad[None], key_grad[None], value_grad[None], maps_grad)


def solution(mesh):
    in_specs = (
        P("dp", "context", None),
        P("dp", "context", None),
        P("dp", "context", None),
        P("dp", "context", None),
        P(),
    )
    out_specs = (
        P("dp", "context", None),
        P("dp", "context", None),
        P("dp", "context", None),
        P(("dp", "context"), None),
    )
    return jax.shard_map(
        per_device, mesh=mesh, in_specs=in_specs, out_specs=out_specs, check_vma=False
    )
```

```python
import functools
import math

import jax
import jax.numpy as jnp
from jax import lax
from jax.experimental import pallas as pl
from jax.experimental.pallas import tpu as pltpu
from jax.sharding import PartitionSpec as P

F32 = jnp.float32
BF16 = jnp.bfloat16
VMEM_LIMIT = 57 * 1024 * 1024
MIDDLE_LIMIT = 52 * 1024 * 1024
STATES_LIMIT = 53 * 1024 * 1024
SMALL_LIMIT = 16 * 1024 * 1024
LIGHT = 0.01


class Plan:
    def __init__(self, heads, width, tokens, ranks, copies):
        self.heads, self.width, self.tokens = heads, width, tokens
        self.ranks, self.copies = ranks, copies
        self.groups = ranks // 4
        per_copy = heads // copies if heads % copies == 0 else 0
        self.chunks = 2 if per_copy and per_copy % 2 == 0 and self.groups % 2 == 0 else 1
        self.in_chunk = heads // self.chunks
        self.quarter = self.in_chunk // 4
        self.run = per_copy // self.chunks if self.chunks > 1 else self.in_chunk
        self.stride = per_copy if self.chunks > 1 else 0
        self.height = heads * width // (copies * ranks)
        self.factor = 1.0 / math.sqrt(width * tokens * ranks)
        self.norm = 1.0 / math.sqrt(copies * tokens * ranks)

    def head(self, chunk, place):
        return (place // self.run) * self.stride + chunk * self.run + place % self.run


def device_place():
    index = lax.axis_index("context")
    return index % 2, (index // 2) % 2, index // 4


def dot(left, right, left_dim=1, right_dim=0):
    return lax.dot_general(
        left, right, (((left_dim,), (right_dim,)), ((), ())), preferred_element_type=F32
    )


def call(body, operands, shapes, flops, scratch, copies, aliases=None, near=(), near_out=(), limit=VMEM_LIMIT, weight=1.0):
    moved = sum(x.size * x.dtype.itemsize for x in list(operands) + list(shapes))

    def specs(count, in_vmem):
        return [
            pl.BlockSpec(memory_space=pltpu.VMEM if n in in_vmem else pltpu.HBM)
            for n in range(count)
        ]

    return pl.pallas_call(
        body,
        out_shape=shapes,
        in_specs=specs(len(operands), near),
        out_specs=specs(len(shapes), near_out),
        scratch_shapes=list(scratch) + [pltpu.SemaphoreType.DMA((copies,))],
        input_output_aliases=aliases or {},
        compiler_params=pltpu.CompilerParams(vmem_limit_bytes=limit),
        cost_estimate=pl.CostEstimate(
            flops=int(flops * weight), bytes_accessed=int(moved * weight), transcendentals=0
        ),
    )(*operands)


class Copies:
    def __init__(self, sems):
        self.sems, self.used = sems, 0

    def start(self, source, target):
        copy = pltpu.make_async_copy(source, target, self.sems.at[self.used])
        self.used += 1
        copy.start()
        return copy


def wait(copies):
    for copy in copies:
        copy.wait()


def matmuls(plan, count):
    return 2 * count * plan.tokens * plan.width * plan.width


def load_chunk(plan, copies, chunk, offset, row_refs, maps_ref, row_bufs, maps_buf):
    width, started = plan.width, []
    for first in range(0, plan.in_chunk, plan.run):
        head = plan.head(chunk, first)
        source, target = pl.ds(head, plan.run), pl.ds(offset + first, plan.run)
        started.append(copies.start(maps_ref.at[source], maps_buf.at[target]))
        source = pl.ds(head * width, plan.run * width)
        target = pl.ds((offset + first) * width, plan.run * width)
        for ref, buf in zip(row_refs, row_bufs):
            started.append(copies.start(ref.at[:, source], buf.at[:, target]))
    return started


def chunk_copies(plan):
    return 5 * (plan.in_chunk // plan.run)


def row_scratch(plan, count):
    rows = [pltpu.VMEM((plan.tokens, count * plan.width), BF16)] * 4
    return rows + [pltpu.VMEM((count, plan.width, plan.width), BF16)]


def head_of(buf, place, width):
    return buf[:, place * width : (place + 1) * width]


def quarter_of(plan, place):
    core, chip, _ = device_place()
    low = place // plan.quarter
    core_turn = 1 - core if low % 2 else core
    chip_turn = 1 - chip if low // 2 else chip
    return core_turn, chip_turn, place % plan.quarter


def states_kernel(plan, chunk, *refs):
    row_refs, maps_ref, sent_ref, kept_ref, given_ref = refs[:4], refs[4], refs[5], refs[6], refs[7]
    row_bufs, maps_buf, sems = refs[8:12], refs[12], refs[13]
    copies, width = Copies(sems), plan.width
    started = load_chunk(plan, copies, chunk, 0, row_refs, maps_ref, row_bufs, maps_buf)
    q_buf, k_buf, v_buf, g_buf = row_bufs
    size = 5 * max(1, 4 // plan.run)
    for first in range(0, plan.in_chunk, 4):
        places = range(first, first + 4)
        wait(started[:size])
        started = started[size:]
        feats_key = [dot(head_of(k_buf, n, width), maps_buf[n]).astype(BF16) for n in places]
        feats_query = [dot(head_of(q_buf, n, width), maps_buf[n]).astype(BF16) for n in places]
        key_states = [
            dot(feat, head_of(v_buf, n, width), 0, 0) for feat, n in zip(feats_key, places)
        ]
        query_states = [
            dot(feat, head_of(g_buf, n, width), 0, 0) for feat, n in zip(feats_query, places)
        ]
        for place, key_state, query_state in zip(places, key_states, query_states):
            core_turn, chip_turn, i = quarter_of(plan, place)

            @pl.when(core_turn == 1)
            def _():
                sent_ref[chip_turn, 0, i] = key_state
                sent_ref[chip_turn, 1, i] = query_state

            @pl.when(core_turn == 0)
            def _():
                kept_ref[chip_turn, 0, i] = key_state
                kept_ref[chip_turn, 1, i] = query_state
    given_ref[...] = kept_ref[1]


def block_states(plan, chunk, rows, maps):
    shape = (2, 2, plan.quarter, plan.width, plan.width)
    state = jax.ShapeDtypeStruct(shape, F32)
    return call(
        functools.partial(states_kernel, plan, chunk),
        (*rows, maps),
        [state, state, jax.ShapeDtypeStruct(shape[1:], F32)],
        matmuls(plan, 4 * plan.in_chunk),
        row_scratch(plan, plan.in_chunk),
        chunk_copies(plan),
        near_out=(0, 1, 2),
        limit=STATES_LIMIT,
    )


def causal_mask(tokens):
    row = lax.broadcasted_iota(jnp.int32, (tokens, tokens), 0)
    column = lax.broadcasted_iota(jnp.int32, (tokens, tokens), 1)
    return row >= column


def inner_kernel(plan, chunk, *refs):
    row_refs, maps_ref, base_ref, pair_ref = refs[:4], refs[4], refs[5], refs[6]
    row_bufs, maps_buf, base_buf, pair_buf, sems = refs[7:11], refs[11], refs[12], refs[13], refs[14]
    copies, width = Copies(sems), plan.width
    started = load_chunk(plan, copies, chunk, 0, row_refs, maps_ref, row_bufs, maps_buf)
    causal = causal_mask(plan.tokens)
    written = []
    size = 5 * max(1, 4 // plan.run)
    for first in range(0, plan.in_chunk, 4):
        places = range(first, first + 4)
        wait(started[:size])
        started = started[size:]
        queries, keys, values, grads = [
            [head_of(buf, n, width) for n in places] for buf in row_bufs
        ]
        scores = [
            jnp.where(causal, dot(grad, value, 1, 1), 0.0).astype(BF16)
            for grad, value in zip(grads, values)
        ]
        feats_query = [dot(x, maps_buf[n]).astype(BF16) for x, n in zip(queries, places)]
        feats_key = [dot(x, maps_buf[n]).astype(BF16) for x, n in zip(keys, places)]
        grads_a = [dot(s, feat).astype(BF16) for s, feat in zip(scores, feats_key)]
        grads_b = [dot(s, feat, 0, 0).astype(BF16) for s, feat in zip(scores, feats_query)]
        for n, place in enumerate(places):
            pair_buf[0, place] = dot(queries[n], grads[n], 0, 0).astype(BF16)
            pair_buf[1, place] = dot(keys[n], values[n], 0, 0).astype(BF16)
            base_buf[place] = dot(queries[n], grads_a[n], 0, 0) + dot(keys[n], grads_b[n], 0, 0)
        part = pl.ds(first, 4)
        written.append(copies.start(base_buf.at[part], base_ref.at[part]))
        written.append(copies.start(pair_buf.at[:, part], pair_ref.at[:, part]))
    wait(written)


def inner(plan, chunk, rows, maps):
    square = (plan.in_chunk, plan.width, plan.width)
    return call(
        functools.partial(inner_kernel, plan, chunk),
        (*rows, maps),
        [jax.ShapeDtypeStruct(square, F32), jax.ShapeDtypeStruct((2,) + square, BF16)],
        matmuls(plan, 9 * plan.in_chunk),
        row_scratch(plan, plan.in_chunk)
        + [pltpu.VMEM(square, F32), pltpu.VMEM((2,) + square, BF16)],
        chunk_copies(plan) + plan.in_chunk // 2,
    )


def finish_states(plan, state_refs, extra_buf, state_buf):
    core, _, _ = device_place()
    for core_turn in range(2):
        for chip_turn in range(2):
            for side in range(2):
                state = state_refs[2 * core_turn + chip_turn][side]
                if core_turn == 0:
                    wanted = core == 1 - side
                    state = state + jnp.where(wanted, extra_buf[chip_turn, side], 0.0)
                state_buf[core_turn, chip_turn, side] = state.astype(BF16)


def state_scratch(plan):
    shape = (2, 2, plan.quarter, plan.width, plan.width)
    return [pltpu.VMEM(shape, F32), pltpu.VMEM((2,) + shape, BF16)]


def term_kernel(plan, *refs):
    state_refs, extra_ref, base_ref, pair_ref = refs[:4], refs[4], refs[5], refs[6]
    out_refs = refs[7:-5]
    extra_buf, state_buf, base_buf, pair_buf, sems = refs[-5:]
    copies = Copies(sems)
    core, _, _ = device_place()
    extra_copy = copies.start(extra_ref, extra_buf)
    others = [copies.start(pair_ref, pair_buf), copies.start(base_ref, base_buf)]
    extra_copy.wait()
    finish_states(plan, state_refs, extra_buf, state_buf)
    wait(others)
    half = plan.width // 2
    for first in range(0, plan.in_chunk, 4):
        places = range(first, first + 4)
        where = [quarter_of(plan, place) for place in places]
        products = [
            dot(pair_buf[side, place], state_buf[c, y, side, i], 1, 1)
            for place, (c, y, i) in zip(places, where)
            for side in range(2)
        ]
        for n, place in enumerate(places):
            term = plan.factor * (base_buf[place] + products[2 * n] + products[2 * n + 1])
            if len(out_refs) == 1:
                out_refs[0][place] = term
            else:
                out_refs[0][place] = jnp.where(core == 0, term[half:], term[:half])
                out_refs[1][place] = jnp.where(core == 0, term[:half], term[half:])


def maps_term(plan, states, extra, base, pair):
    width = plan.width
    square = (plan.in_chunk, width, width)
    in_halves = 2 * plan.height == width and plan.height % 8 == 0
    shapes = [(plan.in_chunk, width // 2, width)] * 2 if in_halves else [square]
    outs = call(
        functools.partial(term_kernel, plan),
        (*states, extra, base, pair),
        [jax.ShapeDtypeStruct(shape, F32) for shape in shapes],
        matmuls(plan, 2 * plan.in_chunk),
        state_scratch(plan) + [pltpu.VMEM(square, F32), pltpu.VMEM((2,) + square, BF16)],
        3,
        near=range(4),
        near_out=range(2),
        limit=SMALL_LIMIT,
        weight=LIGHT,
    )
    if in_halves:
        return outs
    core, _, _ = device_place()
    parts = outs[0].reshape(-1, 2, plan.height, width)
    return [
        lax.dynamic_index_in_dim(parts, turn, 1, keepdims=False) for turn in (1 - core, core)
    ]


def rows_kernel(plan, chunk, *refs):
    state_refs, extra_ref, row_refs, maps_ref = refs[:4], refs[4], refs[5:9], refs[9]
    refs = refs[10 + (3 if chunk else 0) :]
    out_refs, row_bufs, maps_buf = refs[:3], refs[3:7], refs[7]
    extra_buf, state_buf, out_bufs, sems = refs[8], refs[9], refs[10:13], refs[13]
    copies, width = Copies(sems), plan.width
    extra_copy = copies.start(extra_ref, extra_buf)
    started = load_chunk(plan, copies, chunk, 0, row_refs, maps_ref, row_bufs, maps_buf)
    causal = causal_mask(plan.tokens)
    extra_copy.wait()
    finish_states(plan, state_refs, extra_buf, state_buf)
    written = []
    size = 5 * max(1, 4 // plan.run)
    for first in range(0, plan.in_chunk, 4):
        places = range(first, first + 4)
        wait(started[:size])
        started = started[size:]
        queries, keys, values, grads = [
            [head_of(buf, place, width) for place in places] for buf in row_bufs
        ]
        where = [quarter_of(plan, place) for place in places]
        prefixes = [state_buf[c, y, 0, i] for c, y, i in where]
        suffixes = [state_buf[c, y, 1, i] for c, y, i in where]
        matrices = [maps_buf[place] for place in places]
        scores_gv = [
            jnp.where(causal, dot(grad, value, 1, 1), 0.0).astype(BF16)
            for grad, value in zip(grads, values)
        ]
        feats_query = [dot(x, matrix).astype(BF16) for x, matrix in zip(queries, matrices)]
        feats_key = [dot(x, matrix).astype(BF16) for x, matrix in zip(keys, matrices)]
        scores_ab = [
            jnp.where(causal, dot(left, right, 1, 1), 0.0).astype(BF16)
            for left, right in zip(feats_query, feats_key)
        ]
        grads_a = [
            (plan.factor * (dot(score, feat) + dot(grad, prefix, 1, 1))).astype(BF16)
            for score, feat, grad, prefix in zip(scores_gv, feats_key, grads, prefixes)
        ]
        grads_b = [
            (plan.factor * (dot(score, feat, 0, 0) + dot(value, suffix, 1, 1))).astype(BF16)
            for score, feat, value, suffix in zip(scores_gv, feats_query, values, suffixes)
        ]
        for n, place in enumerate(places):
            at = slice(place * width, (place + 1) * width)
            out_bufs[0][:, at] = dot(grads_a[n], matrices[n], 1, 1).astype(BF16)
            out_bufs[1][:, at] = dot(grads_b[n], matrices[n], 1, 1).astype(BF16)
            value_grad = dot(scores_ab[n], grads[n], 0, 0) + dot(feats_key[n], suffixes[n])
            out_bufs[2][:, at] = (plan.factor * value_grad).astype(BF16)
        for part in range(first, first + 4, min(4, plan.run)):
            count = min(4, plan.run)
            source = pl.ds(part * width, count * width)
            target = pl.ds(plan.head(chunk, part) * width, count * width)
            for buf, ref in zip(out_bufs, out_refs):
                written.append(copies.start(buf.at[:, source], ref.at[:, target]))
    wait(written)


def output_rows(plan, chunk, rows, maps, states, extra, done):
    shape = jax.ShapeDtypeStruct((plan.tokens, plan.heads * plan.width), BF16)
    narrow = [pltpu.VMEM((plan.tokens, plan.in_chunk * plan.width), BF16)] * 3
    return call(
        functools.partial(rows_kernel, plan, chunk),
        (*states, extra, *rows, maps, *done),
        [shape] * 3,
        matmuls(plan, 12 * plan.in_chunk),
        row_scratch(plan, plan.in_chunk) + state_scratch(plan) + narrow,
        chunk_copies(plan) + 3 * plan.in_chunk + 1,
        {10: 0, 11: 1, 12: 2} if done else None,
        near=range(4),
        limit=MIDDLE_LIMIT,
        weight=LIGHT,
    )


def swap_core(plan, state):
    return lax.ppermute(state, "context", [(i, i ^ 1) for i in range(plan.ranks)])


def swap_chip(plan, state):
    return lax.ppermute(state, "context", [(i, i ^ 2) for i in range(plan.ranks)])


def chain_swap(plan, state, hop):
    mirror = plan.groups - 1 - hop
    steps = [(i, i ^ 1) for i in range(plan.ranks)]
    for low in range(4):
        for left in (hop, mirror - 1):
            a, b = 4 * left + low, 4 * left + 4 + low
            steps[a], steps[b] = (a, b), (b, a)
    return lax.ppermute(state, "context", steps)


def chain_split(plan, state, hop):
    mirror = plan.groups - 1 - hop
    up = [(4 * hop + low, 4 * hop + 4 + low) for low in range(4)]
    down = [(4 * mirror + low, 4 * mirror - 4 + low) for low in range(4)]
    return lax.ppermute(state[0], "context", up), lax.ppermute(state[1], "context", down)


def plane_sums(plan, halves):
    _, chip, _ = device_place()
    replica = lax.axis_index("dp")
    ranks, copies, width = plan.ranks, plan.copies, plan.width
    totals = [half.reshape(copies, -1, 2, plan.height, width) for half in halves]

    def plane_part(target_replica, target_chip):
        parts = []
        for total in totals:
            some = lax.dynamic_index_in_dim(total, target_replica, 0, keepdims=False)
            parts.append(lax.dynamic_index_in_dim(some, target_chip, 1, keepdims=False))
        return jnp.concatenate(parts, axis=0)

    plane = plane_part(replica, chip)
    for turn in range(copies):
        for flip in range(2):
            if turn == 0 and flip == 0:
                continue
            steps = [
                (r * ranks + i, ((r + turn) % copies) * ranks + (i ^ (2 * flip)))
                for r in range(copies)
                for i in range(ranks)
            ]
            sent = plane_part((replica + turn) % copies, (chip + flip) % 2)
            plane = plane + lax.ppermute(sent, ("dp", "context"), steps)
    return plane


def group_sum(plan, plane):
    _, _, group = device_place()
    result = lax.dynamic_index_in_dim(plane, group, 0, keepdims=False)
    in_pairs = plan.groups & (plan.groups - 1) == 0
    for turn in range(1, plan.groups):

        def partner(place):
            return place ^ turn if in_pairs else (place + turn) % plan.groups

        steps = [(i, 4 * partner(i // 4) + i % 4) for i in range(plan.ranks)]
        sent = lax.dynamic_index_in_dim(plane, partner(group), 0, keepdims=False)
        result = result + lax.ppermute(sent, "context", steps)
    return result


def select_group(plan, got):
    _, _, group = device_place()
    prefix = suffix = jnp.zeros_like(got[0])
    for hop, state in enumerate(got):
        prefix = jnp.where(group == hop + 1, state, prefix)
        suffix = jnp.where(group == plan.groups - 2 - hop, state, suffix)
    return jnp.stack([prefix, suffix])


def scan_alone(plan, group_state):
    before = jnp.zeros_like(group_state)
    for hop in range(plan.groups - 1):
        if plan.groups % 2:
            up, down = chain_split(plan, before + group_state, hop)
            before = before + jnp.stack([up, down])
    return before


def after(value, *others):
    return lax.optimization_barrier((value, *others))[0]


def per_device(queries, key_rows, value_rows, out_grad, maps):
    tokens = queries.shape[1]
    heads, width, _ = maps.shape
    plan = Plan(heads, width, tokens, lax.axis_size("context"), lax.axis_size("dp"))
    rows = [x.reshape(tokens, heads * width) for x in (queries, key_rows, value_rows, out_grad)]
    core, chip, group = device_place()
    side = jnp.arange(2).reshape(2, 1, 1, 1)
    chunks, hops, last = range(plan.chunks), plan.groups - 1, plan.chunks - 1

    kept, from_core, given = [], [], []
    total, from_chip = [], []
    for chunk in chunks:
        matrices = after(maps, given[-1]) if chunk else maps
        sent, kept_here, given_here = block_states(plan, chunk, rows, matrices)
        kept.append(kept_here)
        from_core.append(swap_core(plan, sent))
        given_here = given_here + from_core[chunk][1]
        given.append(given_here)
        total.append(kept_here[0] + from_core[chunk][0])
        from_chip.append(swap_chip(plan, given_here))
    ready = [given[-1]] * last + [sent]
    terms = [inner(plan, chunk, rows, after(maps, ready[chunk])) for chunk in chunks]
    if last:
        from_chip[0] = after(from_chip[0], *terms[last])
    group_state = [total[chunk] + from_chip[chunk] for chunk in chunks]

    def for_other_chip(chunk, before):
        return before + jnp.where(side == chip, total[chunk], 0.0)

    def for_other_core(chunk, turn, state):
        return state + jnp.where(side == core, kept[chunk][turn], 0.0)

    before, got, down = [None] * plan.chunks, [[] for _ in chunks], [None] * plan.chunks
    if plan.groups % 2:
        for chunk in chunks:
            before[chunk] = scan_alone(plan, group_state[chunk])
            down[chunk] = swap_chip(plan, for_other_chip(chunk, before[chunk]))
    else:
        ahead = behind = given[last]
        for stage in range(hops + last):
            for chunk in chunks:
                hop = stage - chunk
                if chunk == 0 and hop == hops:
                    before[0] = select_group(plan, got[0])
                    ahead = for_other_chip(0, before[0])
                    down[0] = swap_chip(plan, ahead)
                if not 0 <= hop < hops:
                    continue
                send = jnp.where(group == hop, group_state[chunk][0], group_state[chunk][1])
                if hop:
                    send = send + got[chunk][-1]
                if chunk:
                    behind = send = after(send, ahead)
                elif last:
                    ahead = send = after(send, *(terms[0] if hop == 1 else (behind,)))
                got[chunk].append(chain_swap(plan, send, hop))
        if last:
            got[last][-1] = after(got[last][-1], for_other_core(0, 1, down[0]))
        before[last] = select_group(plan, got[last])
        down[last] = swap_chip(plan, for_other_chip(last, before[last]))

    halves, done = [], ()
    for chunk in chunks:
        states = [before[chunk] + jnp.where(side != chip, from_chip[chunk], 0.0), down[chunk]]
        for turn in range(2):
            if turn and done:
                states[1] = after(states[1], states[2], *done)
            states.append(swap_core(plan, for_other_core(chunk, turn, states[turn])))
        if halves:
            states[3] = after(states[3], *halves)
        for_mate, own = maps_term(plan, states, from_core[chunk], *terms[chunk])
        halves.append(own + swap_core(plan, for_mate))
        matrices = after(maps, for_mate)
        done = output_rows(plan, chunk, rows, matrices, states, from_core[chunk], done)
    plane = after(plane_sums(plan, halves), *done)
    query_grad, key_grad, value_grad = done
    maps_grad = group_sum(plan, plane) * plan.norm
    return (query_grad[None], key_grad[None], value_grad[None], maps_grad)


def solution(mesh):
    in_specs = (
        P("dp", "context", None),
        P("dp", "context", None),
        P("dp", "context", None),
        P("dp", "context", None),
        P(),
    )
    out_specs = (
        P("dp", "context", None),
        P("dp", "context", None),
        P("dp", "context", None),
        P(("dp", "context"), None),
    )
    return jax.shard_map(
        per_device, mesh=mesh, in_specs=in_specs, out_specs=out_specs, check_vma=False
    )
```

```python
import functools
import math

import jax
import jax.numpy as jnp
from jax import lax
from jax.experimental import pallas as pl
from jax.experimental.pallas import tpu as pltpu
from jax.sharding import PartitionSpec as P

F32 = jnp.float32
BF16 = jnp.bfloat16
VMEM_LIMIT = 57 * 1024 * 1024
MIDDLE_LIMIT = 52 * 1024 * 1024
STATES_LIMIT = 53 * 1024 * 1024
SMALL_LIMIT = 16 * 1024 * 1024
LIGHT = 0.01


class Plan:
    def __init__(self, heads, width, tokens, ranks, copies):
        self.heads, self.width, self.tokens = heads, width, tokens
        self.ranks, self.copies = ranks, copies
        self.groups = ranks // 4
        per_copy = heads // copies if heads % copies == 0 else 0
        self.chunks = 2 if per_copy and per_copy % 2 == 0 and self.groups % 2 == 0 else 1
        self.in_chunk = heads // self.chunks
        self.quarter = self.in_chunk // 4
        self.run = per_copy // self.chunks if self.chunks > 1 else self.in_chunk
        self.stride = per_copy if self.chunks > 1 else 0
        self.height = heads * width // (copies * ranks)
        self.factor = 1.0 / math.sqrt(width * tokens * ranks)
        self.norm = 1.0 / math.sqrt(copies * tokens * ranks)

    def head(self, chunk, place):
        return (place // self.run) * self.stride + chunk * self.run + place % self.run


def device_place():
    index = lax.axis_index("context")
    return index % 2, (index // 2) % 2, index // 4


def dot(left, right, left_dim=1, right_dim=0):
    return lax.dot_general(
        left, right, (((left_dim,), (right_dim,)), ((), ())), preferred_element_type=F32
    )


def call(body, operands, shapes, flops, scratch, copies, aliases=None, near=(), near_out=(), limit=VMEM_LIMIT, weight=1.0):
    moved = sum(x.size * x.dtype.itemsize for x in list(operands) + list(shapes))

    def specs(count, in_vmem):
        return [
            pl.BlockSpec(memory_space=pltpu.VMEM if n in in_vmem else pltpu.HBM)
            for n in range(count)
        ]

    return pl.pallas_call(
        body,
        out_shape=shapes,
        in_specs=specs(len(operands), near),
        out_specs=specs(len(shapes), near_out),
        scratch_shapes=list(scratch) + [pltpu.SemaphoreType.DMA((copies,))],
        input_output_aliases=aliases or {},
        compiler_params=pltpu.CompilerParams(vmem_limit_bytes=limit),
        cost_estimate=pl.CostEstimate(
            flops=int(flops * weight), bytes_accessed=int(moved * weight), transcendentals=0
        ),
    )(*operands)


class Copies:
    def __init__(self, sems):
        self.sems, self.used = sems, 0

    def start(self, source, target):
        copy = pltpu.make_async_copy(source, target, self.sems.at[self.used])
        self.used += 1
        copy.start()
        return copy


def wait(copies):
    for copy in copies:
        copy.wait()


def matmuls(plan, count):
    return 2 * count * plan.tokens * plan.width * plan.width


def load_chunk(plan, copies, chunk, offset, row_refs, maps_ref, row_bufs, maps_buf):
    width, started = plan.width, []
    for first in range(0, plan.in_chunk, plan.run):
        head = plan.head(chunk, first)
        source, target = pl.ds(head, plan.run), pl.ds(offset + first, plan.run)
        started.append(copies.start(maps_ref.at[source], maps_buf.at[target]))
        source = pl.ds(head * width, plan.run * width)
        target = pl.ds((offset + first) * width, plan.run * width)
        for ref, buf in zip(row_refs, row_bufs):
            started.append(copies.start(ref.at[:, source], buf.at[:, target]))
    return started


def chunk_copies(plan):
    return 5 * (plan.in_chunk // plan.run)


def row_scratch(plan, count):
    rows = [pltpu.VMEM((plan.tokens, count * plan.width), BF16)] * 4
    return rows + [pltpu.VMEM((count, plan.width, plan.width), BF16)]


def head_of(buf, place, width):
    return buf[:, place * width : (place + 1) * width]


def quarter_of(plan, place):
    core, chip, _ = device_place()
    low = place // plan.quarter
    core_turn = 1 - core if low % 2 else core
    chip_turn = 1 - chip if low // 2 else chip
    return core_turn, chip_turn, place % plan.quarter


def states_kernel(plan, chunk, *refs):
    row_refs, maps_ref, sent_ref, kept_ref, given_ref = refs[:4], refs[4], refs[5], refs[6], refs[7]
    row_bufs, maps_buf, sems = refs[8:12], refs[12], refs[13]
    copies, width = Copies(sems), plan.width
    started = load_chunk(plan, copies, chunk, 0, row_refs, maps_ref, row_bufs, maps_buf)
    q_buf, k_buf, v_buf, g_buf = row_bufs
    size = 5 * max(1, 4 // plan.run)
    for first in range(0, plan.in_chunk, 4):
        places = range(first, first + 4)
        wait(started[:size])
        started = started[size:]
        feats_key = [dot(head_of(k_buf, n, width), maps_buf[n]).astype(BF16) for n in places]
        feats_query = [dot(head_of(q_buf, n, width), maps_buf[n]).astype(BF16) for n in places]
        key_states = [
            dot(feat, head_of(v_buf, n, width), 0, 0) for feat, n in zip(feats_key, places)
        ]
        query_states = [
            dot(feat, head_of(g_buf, n, width), 0, 0) for feat, n in zip(feats_query, places)
        ]
        for place, key_state, query_state in zip(places, key_states, query_states):
            core_turn, chip_turn, i = quarter_of(plan, place)

            @pl.when(core_turn == 1)
            def _():
                sent_ref[chip_turn, 0, i] = key_state
                sent_ref[chip_turn, 1, i] = query_state

            @pl.when(core_turn == 0)
            def _():
                kept_ref[chip_turn, 0, i] = key_state
                kept_ref[chip_turn, 1, i] = query_state
    given_ref[...] = kept_ref[1]


def block_states(plan, chunk, rows, maps):
    shape = (2, 2, plan.quarter, plan.width, plan.width)
    state = jax.ShapeDtypeStruct(shape, F32)
    return call(
        functools.partial(states_kernel, plan, chunk),
        (*rows, maps),
        [state, state, jax.ShapeDtypeStruct(shape[1:], F32)],
        matmuls(plan, 4 * plan.in_chunk),
        row_scratch(plan, plan.in_chunk),
        chunk_copies(plan),
        near_out=(0, 1, 2),
        limit=STATES_LIMIT,
    )


def causal_mask(tokens):
    row = lax.broadcasted_iota(jnp.int32, (tokens, tokens), 0)
    column = lax.broadcasted_iota(jnp.int32, (tokens, tokens), 1)
    return row >= column


def inner_kernel(plan, chunk, *refs):
    row_refs, maps_ref, base_ref, pair_ref = refs[:4], refs[4], refs[5], refs[6]
    row_bufs, maps_buf, base_buf, pair_buf, sems = refs[7:11], refs[11], refs[12], refs[13], refs[14]
    copies, width = Copies(sems), plan.width
    started = load_chunk(plan, copies, chunk, 0, row_refs, maps_ref, row_bufs, maps_buf)
    causal = causal_mask(plan.tokens)
    written = []
    size = 5 * max(1, 4 // plan.run)
    for first in range(0, plan.in_chunk, 4):
        places = range(first, first + 4)
        wait(started[:size])
        started = started[size:]
        queries, keys, values, grads = [
            [head_of(buf, n, width) for n in places] for buf in row_bufs
        ]
        scores = [
            jnp.where(causal, dot(grad, value, 1, 1), 0.0).astype(BF16)
            for grad, value in zip(grads, values)
        ]
        feats_query = [dot(x, maps_buf[n]).astype(BF16) for x, n in zip(queries, places)]
        feats_key = [dot(x, maps_buf[n]).astype(BF16) for x, n in zip(keys, places)]
        grads_a = [dot(s, feat).astype(BF16) for s, feat in zip(scores, feats_key)]
        grads_b = [dot(s, feat, 0, 0).astype(BF16) for s, feat in zip(scores, feats_query)]
        for n, place in enumerate(places):
            pair_buf[0, place] = dot(queries[n], grads[n], 0, 0).astype(BF16)
            pair_buf[1, place] = dot(keys[n], values[n], 0, 0).astype(BF16)
            base_buf[place] = dot(queries[n], grads_a[n], 0, 0) + dot(keys[n], grads_b[n], 0, 0)
        part = pl.ds(first, 4)
        written.append(copies.start(base_buf.at[part], base_ref.at[part]))
        written.append(copies.start(pair_buf.at[:, part], pair_ref.at[:, part]))
    wait(written)


def inner(plan, chunk, rows, maps):
    square = (plan.in_chunk, plan.width, plan.width)
    return call(
        functools.partial(inner_kernel, plan, chunk),
        (*rows, maps),
        [jax.ShapeDtypeStruct(square, F32), jax.ShapeDtypeStruct((2,) + square, BF16)],
        matmuls(plan, 9 * plan.in_chunk),
        row_scratch(plan, plan.in_chunk)
        + [pltpu.VMEM(square, F32), pltpu.VMEM((2,) + square, BF16)],
        chunk_copies(plan) + plan.in_chunk // 2,
    )


def finish_states(plan, state_refs, extra_buf, state_buf):
    core, _, _ = device_place()
    for core_turn in range(2):
        for chip_turn in range(2):
            for side in range(2):
                state = state_refs[2 * core_turn + chip_turn][side]
                if core_turn == 0:
                    wanted = core == 1 - side
                    state = state + jnp.where(wanted, extra_buf[chip_turn, side], 0.0)
                state_buf[core_turn, chip_turn, side] = state.astype(BF16)


def state_scratch(plan):
    shape = (2, 2, plan.quarter, plan.width, plan.width)
    return [pltpu.VMEM(shape, F32), pltpu.VMEM((2,) + shape, BF16)]


def term_kernel(plan, *refs):
    state_refs, extra_ref, base_ref, pair_ref = refs[:4], refs[4], refs[5], refs[6]
    out_refs = refs[7:-5]
    extra_buf, state_buf, base_buf, pair_buf, sems = refs[-5:]
    copies = Copies(sems)
    core, _, _ = device_place()
    extra_copy = copies.start(extra_ref, extra_buf)
    others = [copies.start(pair_ref, pair_buf), copies.start(base_ref, base_buf)]
    extra_copy.wait()
    finish_states(plan, state_refs, extra_buf, state_buf)
    wait(others)
    half = plan.width // 2
    for first in range(0, plan.in_chunk, 4):
        places = range(first, first + 4)
        where = [quarter_of(plan, place) for place in places]
        products = [
            dot(pair_buf[side, place], state_buf[c, y, side, i], 1, 1)
            for place, (c, y, i) in zip(places, where)
            for side in range(2)
        ]
        for n, place in enumerate(places):
            term = plan.factor * (base_buf[place] + products[2 * n] + products[2 * n + 1])
            if len(out_refs) == 1:
                out_refs[0][place] = term
            else:
                out_refs[0][place] = jnp.where(core == 0, term[half:], term[:half])
                out_refs[1][place] = jnp.where(core == 0, term[:half], term[half:])


def maps_term(plan, states, extra, base, pair):
    width = plan.width
    square = (plan.in_chunk, width, width)
    in_halves = 2 * plan.height == width and plan.height % 8 == 0
    shapes = [(plan.in_chunk, width // 2, width)] * 2 if in_halves else [square]
    outs = call(
        functools.partial(term_kernel, plan),
        (*states, extra, base, pair),
        [jax.ShapeDtypeStruct(shape, F32) for shape in shapes],
        matmuls(plan, 2 * plan.in_chunk),
        state_scratch(plan) + [pltpu.VMEM(square, F32), pltpu.VMEM((2,) + square, BF16)],
        3,
        near=range(4),
        near_out=range(2),
        limit=SMALL_LIMIT,
        weight=LIGHT,
    )
    if in_halves:
        return outs
    core, _, _ = device_place()
    parts = outs[0].reshape(-1, 2, plan.height, width)
    return [
        lax.dynamic_index_in_dim(parts, turn, 1, keepdims=False) for turn in (1 - core, core)
    ]


def rows_kernel(plan, chunk, *refs):
    state_refs, extra_ref, row_refs, maps_ref = refs[:4], refs[4], refs[5:9], refs[9]
    refs = refs[10 + (3 if chunk else 0) :]
    out_refs, row_bufs, maps_buf = refs[:3], refs[3:7], refs[7]
    extra_buf, state_buf, out_bufs, sems = refs[8], refs[9], refs[10:13], refs[13]
    copies, width = Copies(sems), plan.width
    extra_copy = copies.start(extra_ref, extra_buf)
    started = load_chunk(plan, copies, chunk, 0, row_refs, maps_ref, row_bufs, maps_buf)
    causal = causal_mask(plan.tokens)
    extra_copy.wait()
    finish_states(plan, state_refs, extra_buf, state_buf)
    written = []
    size = 5 * max(1, 4 // plan.run)
    for first in range(0, plan.in_chunk, 4):
        places = range(first, first + 4)
        wait(started[:size])
        started = started[size:]
        queries, keys, values, grads = [
            [head_of(buf, place, width) for place in places] for buf in row_bufs
        ]
        where = [quarter_of(plan, place) for place in places]
        prefixes = [state_buf[c, y, 0, i] for c, y, i in where]
        suffixes = [state_buf[c, y, 1, i] for c, y, i in where]
        matrices = [maps_buf[place] for place in places]
        scores_gv = [
            jnp.where(causal, dot(grad, value, 1, 1), 0.0).astype(BF16)
            for grad, value in zip(grads, values)
        ]
        feats_query = [dot(x, matrix).astype(BF16) for x, matrix in zip(queries, matrices)]
        feats_key = [dot(x, matrix).astype(BF16) for x, matrix in zip(keys, matrices)]
        scores_ab = [
            jnp.where(causal, dot(left, right, 1, 1), 0.0).astype(BF16)
            for left, right in zip(feats_query, feats_key)
        ]
        grads_a = [
            (plan.factor * (dot(score, feat) + dot(grad, prefix, 1, 1))).astype(BF16)
            for score, feat, grad, prefix in zip(scores_gv, feats_key, grads, prefixes)
        ]
        grads_b = [
            (plan.factor * (dot(score, feat, 0, 0) + dot(value, suffix, 1, 1))).astype(BF16)
            for score, feat, value, suffix in zip(scores_gv, feats_query, values, suffixes)
        ]
        for n, place in enumerate(places):
            at = slice(place * width, (place + 1) * width)
            out_bufs[0][:, at] = dot(grads_a[n], matrices[n], 1, 1).astype(BF16)
            out_bufs[1][:, at] = dot(grads_b[n], matrices[n], 1, 1).astype(BF16)
            value_grad = dot(scores_ab[n], grads[n], 0, 0) + dot(feats_key[n], suffixes[n])
            out_bufs[2][:, at] = (plan.factor * value_grad).astype(BF16)
        for part in range(first, first + 4, min(4, plan.run)):
            count = min(4, plan.run)
            source = pl.ds(part * width, count * width)
            target = pl.ds(plan.head(chunk, part) * width, count * width)
            for buf, ref in zip(out_bufs, out_refs):
                written.append(copies.start(buf.at[:, source], ref.at[:, target]))
    wait(written)


def output_rows(plan, chunk, rows, maps, states, extra, done):
    shape = jax.ShapeDtypeStruct((plan.tokens, plan.heads * plan.width), BF16)
    narrow = [pltpu.VMEM((plan.tokens, plan.in_chunk * plan.width), BF16)] * 3
    return call(
        functools.partial(rows_kernel, plan, chunk),
        (*states, extra, *rows, maps, *done),
        [shape] * 3,
        matmuls(plan, 12 * plan.in_chunk),
        row_scratch(plan, plan.in_chunk) + state_scratch(plan) + narrow,
        chunk_copies(plan) + 3 * plan.in_chunk + 1,
        {10: 0, 11: 1, 12: 2} if done else None,
        near=range(4),
        limit=MIDDLE_LIMIT,
        weight=LIGHT,
    )


def swap_core(plan, state):
    return lax.ppermute(state, "context", [(i, i ^ 1) for i in range(plan.ranks)])


def swap_chip(plan, state):
    return lax.ppermute(state, "context", [(i, i ^ 2) for i in range(plan.ranks)])


def chain_swap(plan, state, hop):
    mirror = plan.groups - 1 - hop
    steps = [(i, i ^ 1) for i in range(plan.ranks)]
    for low in range(4):
        for left in (hop, mirror - 1):
            a, b = 4 * left + low, 4 * left + 4 + low
            steps[a], steps[b] = (a, b), (b, a)
    return lax.ppermute(state, "context", steps)


def chain_split(plan, state, hop):
    mirror = plan.groups - 1 - hop
    up = [(4 * hop + low, 4 * hop + 4 + low) for low in range(4)]
    down = [(4 * mirror + low, 4 * mirror - 4 + low) for low in range(4)]
    return lax.ppermute(state[0], "context", up), lax.ppermute(state[1], "context", down)


def plane_sums(plan, halves):
    _, chip, _ = device_place()
    replica = lax.axis_index("dp")
    ranks, copies, width = plan.ranks, plan.copies, plan.width
    totals = [half.reshape(copies, -1, 2, plan.height, width) for half in halves]

    def plane_part(target_replica, target_chip):
        parts = []
        for total in totals:
            some = lax.dynamic_index_in_dim(total, target_replica, 0, keepdims=False)
            parts.append(lax.dynamic_index_in_dim(some, target_chip, 1, keepdims=False))
        return jnp.concatenate(parts, axis=0)

    plane = plane_part(replica, chip)
    for turn in range(copies):
        for flip in range(2):
            if turn == 0 and flip == 0:
                continue
            steps = [
                (r * ranks + i, ((r + turn) % copies) * ranks + (i ^ (2 * flip)))
                for r in range(copies)
                for i in range(ranks)
            ]
            sent = plane_part((replica + turn) % copies, (chip + flip) % 2)
            plane = plane + lax.ppermute(sent, ("dp", "context"), steps)
    return plane


def group_sum(plan, plane):
    _, _, group = device_place()
    if plan.groups & (plan.groups - 1) == 0:
        turn = 1
        while turn < plan.groups:
            pairs = plane.reshape(-1, 2, *plane.shape[1:])
            mine = group // turn % 2
            steps = [(i, i ^ (4 * turn)) for i in range(plan.ranks)]
            sent = lax.dynamic_index_in_dim(pairs, 1 - mine, 1, keepdims=False)
            kept = lax.dynamic_index_in_dim(pairs, mine, 1, keepdims=False)
            plane = kept + lax.ppermute(sent, "context", steps)
            turn *= 2
        return plane[0]
    result = lax.dynamic_index_in_dim(plane, group, 0, keepdims=False)
    for turn in range(1, plan.groups):
        steps = [(i, (i + 4 * turn) % plan.ranks) for i in range(plan.ranks)]
        sent = lax.dynamic_index_in_dim(plane, (group + turn) % plan.groups, 0, keepdims=False)
        result = result + lax.ppermute(sent, "context", steps)
    return result


def select_group(plan, got):
    _, _, group = device_place()
    prefix = suffix = jnp.zeros_like(got[0])
    for hop, state in enumerate(got):
        prefix = jnp.where(group == hop + 1, state, prefix)
        suffix = jnp.where(group == plan.groups - 2 - hop, state, suffix)
    return jnp.stack([prefix, suffix])


def scan_alone(plan, group_state):
    before = jnp.zeros_like(group_state)
    for hop in range(plan.groups - 1):
        if plan.groups % 2:
            up, down = chain_split(plan, before + group_state, hop)
            before = before + jnp.stack([up, down])
    return before


def after(value, *others):
    return lax.optimization_barrier((value, *others))[0]


def per_device(queries, key_rows, value_rows, out_grad, maps):
    tokens = queries.shape[1]
    heads, width, _ = maps.shape
    plan = Plan(heads, width, tokens, lax.axis_size("context"), lax.axis_size("dp"))
    rows = [x.reshape(tokens, heads * width) for x in (queries, key_rows, value_rows, out_grad)]
    core, chip, group = device_place()
    side = jnp.arange(2).reshape(2, 1, 1, 1)
    chunks, hops, last = range(plan.chunks), plan.groups - 1, plan.chunks - 1

    kept, from_core, given = [], [], []
    total, from_chip = [], []
    for chunk in chunks:
        matrices = after(maps, given[-1]) if chunk else maps
        sent, kept_here, given_here = block_states(plan, chunk, rows, matrices)
        kept.append(kept_here)
        from_core.append(swap_core(plan, sent))
        given_here = given_here + from_core[chunk][1]
        given.append(given_here)
        total.append(kept_here[0] + from_core[chunk][0])
        from_chip.append(swap_chip(plan, given_here))
    ready = [given[-1]] * last + [sent]
    terms = [inner(plan, chunk, rows, after(maps, ready[chunk])) for chunk in chunks]
    if last:
        from_chip[0] = after(from_chip[0], *terms[last])
    group_state = [total[chunk] + from_chip[chunk] for chunk in chunks]

    def for_other_chip(chunk, before):
        return before + jnp.where(side == chip, total[chunk], 0.0)

    def for_other_core(chunk, turn, state):
        return state + jnp.where(side == core, kept[chunk][turn], 0.0)

    before, got, down = [None] * plan.chunks, [[] for _ in chunks], [None] * plan.chunks
    if plan.groups % 2:
        for chunk in chunks:
            before[chunk] = scan_alone(plan, group_state[chunk])
            down[chunk] = swap_chip(plan, for_other_chip(chunk, before[chunk]))
    else:
        ahead = behind = given[last]
        for stage in range(hops + last):
            for chunk in chunks:
                hop = stage - chunk
                if chunk == 0 and hop == hops:
                    before[0] = select_group(plan, got[0])
                    ahead = for_other_chip(0, before[0])
                    down[0] = swap_chip(plan, ahead)
                if not 0 <= hop < hops:
                    continue
                send = jnp.where(group == hop, group_state[chunk][0], group_state[chunk][1])
                if hop:
                    send = send + got[chunk][-1]
                if chunk:
                    behind = send = after(send, ahead)
                elif last:
                    ahead = send = after(send, *(terms[0] if hop == 1 else (behind,)))
                got[chunk].append(chain_swap(plan, send, hop))
        if last:
            got[last][-1] = after(got[last][-1], for_other_core(0, 1, down[0]))
        before[last] = select_group(plan, got[last])
        down[last] = swap_chip(plan, for_other_chip(last, before[last]))

    halves, done = [], ()
    for chunk in chunks:
        states = [before[chunk] + jnp.where(side != chip, from_chip[chunk], 0.0), down[chunk]]
        for turn in range(2):
            if turn and done:
                states[1] = after(states[1], states[2], *done)
            states.append(swap_core(plan, for_other_core(chunk, turn, states[turn])))
        if halves:
            states[3] = after(states[3], *halves)
        for_mate, own = maps_term(plan, states, from_core[chunk], *terms[chunk])
        halves.append(own + swap_core(plan, for_mate))
        matrices = after(maps, for_mate)
        done = output_rows(plan, chunk, rows, matrices, states, from_core[chunk], done)
    plane = after(plane_sums(plan, halves), *done)
    query_grad, key_grad, value_grad = done
    maps_grad = group_sum(plan, plane) * plan.norm
    return (query_grad[None], key_grad[None], value_grad[None], maps_grad)


def solution(mesh):
    in_specs = (
        P("dp", "context", None),
        P("dp", "context", None),
        P("dp", "context", None),
        P("dp", "context", None),
        P(),
    )
    out_specs = (
        P("dp", "context", None),
        P("dp", "context", None),
        P("dp", "context", None),
        P(("dp", "context"), None),
    )
    return jax.shard_map(
        per_device, mesh=mesh, in_specs=in_specs, out_specs=out_specs, check_vma=False
    )
```

```python
import functools
import math

import jax
import jax.numpy as jnp
from jax import lax
from jax.experimental import pallas as pl
from jax.experimental.pallas import tpu as pltpu
from jax.sharding import PartitionSpec as P

F32 = jnp.float32
BF16 = jnp.bfloat16
VMEM_LIMIT = 57 * 1024 * 1024
MIDDLE_LIMIT = 52 * 1024 * 1024
STATES_LIMIT = 53 * 1024 * 1024
SMALL_LIMIT = 16 * 1024 * 1024
LIGHT = 0.01


class Plan:
    def __init__(self, heads, width, tokens, ranks, copies):
        self.heads, self.width, self.tokens = heads, width, tokens
        self.ranks, self.copies = ranks, copies
        self.groups = ranks // 4
        per_copy = heads // copies if heads % copies == 0 else 0
        self.chunks = 2 if per_copy and per_copy % 2 == 0 and self.groups % 2 == 0 else 1
        self.in_chunk = heads // self.chunks
        self.quarter = self.in_chunk // 4
        self.run = per_copy // self.chunks if self.chunks > 1 else self.in_chunk
        self.stride = per_copy if self.chunks > 1 else 0
        self.height = heads * width // (copies * ranks)
        self.pieces = 2 if tokens % 32 == 0 else 1
        self.piece = tokens // self.pieces
        self.loads = 4 * self.pieces + 1
        self.factor = 1.0 / math.sqrt(width * tokens * ranks)
        self.norm = 1.0 / math.sqrt(copies * tokens * ranks)

    def head(self, chunk, place):
        return (place // self.run) * self.stride + chunk * self.run + place % self.run


def device_place():
    index = lax.axis_index("context")
    return index % 2, (index // 2) % 2, index // 4


def dot(left, right, left_dim=1, right_dim=0):
    return lax.dot_general(
        left, right, (((left_dim,), (right_dim,)), ((), ())), preferred_element_type=F32
    )


def call(body, operands, shapes, flops, scratch, copies, aliases=None, near=(), near_out=(), limit=VMEM_LIMIT, weight=1.0):
    moved = sum(x.size * x.dtype.itemsize for x in list(operands) + list(shapes))

    def specs(count, in_vmem):
        return [
            pl.BlockSpec(memory_space=pltpu.VMEM if n in in_vmem else pltpu.HBM)
            for n in range(count)
        ]

    return pl.pallas_call(
        body,
        out_shape=shapes,
        in_specs=specs(len(operands), near),
        out_specs=specs(len(shapes), near_out),
        scratch_shapes=list(scratch) + [pltpu.SemaphoreType.DMA((copies,))],
        input_output_aliases=aliases or {},
        compiler_params=pltpu.CompilerParams(vmem_limit_bytes=limit),
        cost_estimate=pl.CostEstimate(
            flops=int(flops * weight), bytes_accessed=int(moved * weight), transcendentals=0
        ),
    )(*operands)


class Copies:
    def __init__(self, sems):
        self.sems, self.used = sems, 0

    def start(self, source, target):
        copy = pltpu.make_async_copy(source, target, self.sems.at[self.used])
        self.used += 1
        copy.start()
        return copy


def wait(copies):
    for copy in copies:
        copy.wait()


def matmuls(plan, count):
    return 2 * count * plan.tokens * plan.width * plan.width


def load_chunk(plan, copies, chunk, offset, row_refs, maps_ref, row_bufs, maps_buf):
    width, started = plan.width, []
    for first in range(0, plan.in_chunk, plan.run):
        head = plan.head(chunk, first)
        source, target = pl.ds(head, plan.run), pl.ds(offset + first, plan.run)
        started.append(copies.start(maps_ref.at[source], maps_buf.at[target]))
        source = pl.ds(head * width, plan.run * width)
        target = pl.ds((offset + first) * width, plan.run * width)
        for ref, buf in zip(row_refs, row_bufs):
            for part in range(plan.pieces):
                rows = pl.ds(part * plan.piece, plan.piece)
                started.append(copies.start(ref.at[rows, source], buf.at[rows, target]))
    return started


def chunk_copies(plan):
    return plan.loads * (plan.in_chunk // plan.run)


def row_scratch(plan, count):
    rows = [pltpu.VMEM((plan.tokens, count * plan.width), BF16)] * 4
    return rows + [pltpu.VMEM((count, plan.width, plan.width), BF16)]


def head_of(buf, place, width):
    return buf[:, place * width : (place + 1) * width]


def quarter_of(plan, place):
    core, chip, _ = device_place()
    low = place // plan.quarter
    core_turn = 1 - core if low % 2 else core
    chip_turn = 1 - chip if low // 2 else chip
    return core_turn, chip_turn, place % plan.quarter


def states_kernel(plan, chunk, *refs):
    row_refs, maps_ref, sent_ref, kept_ref, given_ref = refs[:4], refs[4], refs[5], refs[6], refs[7]
    row_bufs, maps_buf, sems = refs[8:12], refs[12], refs[13]
    copies, width = Copies(sems), plan.width
    started = load_chunk(plan, copies, chunk, 0, row_refs, maps_ref, row_bufs, maps_buf)
    q_buf, k_buf, v_buf, g_buf = row_bufs
    size = plan.loads * max(1, 4 // plan.run)
    for first in range(0, plan.in_chunk, 4):
        places = range(first, first + 4)
        wait(started[:size])
        started = started[size:]
        feats_key = [dot(head_of(k_buf, n, width), maps_buf[n]).astype(BF16) for n in places]
        feats_query = [dot(head_of(q_buf, n, width), maps_buf[n]).astype(BF16) for n in places]
        key_states = [
            dot(feat, head_of(v_buf, n, width), 0, 0) for feat, n in zip(feats_key, places)
        ]
        query_states = [
            dot(feat, head_of(g_buf, n, width), 0, 0) for feat, n in zip(feats_query, places)
        ]
        for place, key_state, query_state in zip(places, key_states, query_states):
            core_turn, chip_turn, i = quarter_of(plan, place)

            @pl.when(core_turn == 1)
            def _():
                sent_ref[chip_turn, 0, i] = key_state
                sent_ref[chip_turn, 1, i] = query_state

            @pl.when(core_turn == 0)
            def _():
                kept_ref[chip_turn, 0, i] = key_state
                kept_ref[chip_turn, 1, i] = query_state
    given_ref[...] = kept_ref[1]


def block_states(plan, chunk, rows, maps):
    shape = (2, 2, plan.quarter, plan.width, plan.width)
    state = jax.ShapeDtypeStruct(shape, F32)
    return call(
        functools.partial(states_kernel, plan, chunk),
        (*rows, maps),
        [state, state, jax.ShapeDtypeStruct(shape[1:], F32)],
        matmuls(plan, 4 * plan.in_chunk),
        row_scratch(plan, plan.in_chunk),
        chunk_copies(plan),
        near_out=(0, 1, 2),
        limit=STATES_LIMIT,
    )


def causal_mask(tokens):
    row = lax.broadcasted_iota(jnp.int32, (tokens, tokens), 0)
    column = lax.broadcasted_iota(jnp.int32, (tokens, tokens), 1)
    return row >= column


def inner_kernel(plan, chunk, *refs):
    row_refs, maps_ref, base_ref, pair_ref = refs[:4], refs[4], refs[5], refs[6]
    row_bufs, maps_buf, base_buf, pair_buf, sems = refs[7:11], refs[11], refs[12], refs[13], refs[14]
    copies, width = Copies(sems), plan.width
    started = load_chunk(plan, copies, chunk, 0, row_refs, maps_ref, row_bufs, maps_buf)
    causal = causal_mask(plan.tokens)
    written = []
    size = plan.loads * max(1, 4 // plan.run)
    for first in range(0, plan.in_chunk, 4):
        places = range(first, first + 4)
        wait(started[:size])
        started = started[size:]
        queries, keys, values, grads = [
            [head_of(buf, n, width) for n in places] for buf in row_bufs
        ]
        scores = [
            jnp.where(causal, dot(grad, value, 1, 1), 0.0).astype(BF16)
            for grad, value in zip(grads, values)
        ]
        feats_query = [dot(x, maps_buf[n]).astype(BF16) for x, n in zip(queries, places)]
        feats_key = [dot(x, maps_buf[n]).astype(BF16) for x, n in zip(keys, places)]
        grads_a = [dot(s, feat).astype(BF16) for s, feat in zip(scores, feats_key)]
        grads_b = [dot(s, feat, 0, 0).astype(BF16) for s, feat in zip(scores, feats_query)]
        for n, place in enumerate(places):
            pair_buf[0, place] = dot(queries[n], grads[n], 0, 0).astype(BF16)
            pair_buf[1, place] = dot(keys[n], values[n], 0, 0).astype(BF16)
            base_buf[place] = dot(queries[n], grads_a[n], 0, 0) + dot(keys[n], grads_b[n], 0, 0)
        part = pl.ds(first, 4)
        written.append(copies.start(base_buf.at[part], base_ref.at[part]))
        written.append(copies.start(pair_buf.at[:, part], pair_ref.at[:, part]))
    wait(written)


def inner(plan, chunk, rows, maps):
    square = (plan.in_chunk, plan.width, plan.width)
    return call(
        functools.partial(inner_kernel, plan, chunk),
        (*rows, maps),
        [jax.ShapeDtypeStruct(square, F32), jax.ShapeDtypeStruct((2,) + square, BF16)],
        matmuls(plan, 9 * plan.in_chunk),
        row_scratch(plan, plan.in_chunk)
        + [pltpu.VMEM(square, F32), pltpu.VMEM((2,) + square, BF16)],
        chunk_copies(plan) + plan.in_chunk // 2,
    )


def finish_states(plan, state_refs, extra_buf, state_buf):
    core, _, _ = device_place()
    for core_turn in range(2):
        for chip_turn in range(2):
            for side in range(2):
                state = state_refs[2 * core_turn + chip_turn][side]
                if core_turn == 0:
                    wanted = core == 1 - side
                    state = state + jnp.where(wanted, extra_buf[chip_turn, side], 0.0)
                state_buf[core_turn, chip_turn, side] = state.astype(BF16)


def state_scratch(plan):
    shape = (2, 2, plan.quarter, plan.width, plan.width)
    return [pltpu.VMEM(shape, F32), pltpu.VMEM((2,) + shape, BF16)]


def term_kernel(plan, *refs):
    state_refs, extra_ref, base_ref, pair_ref = refs[:4], refs[4], refs[5], refs[6]
    out_refs = refs[7:-5]
    extra_buf, state_buf, base_buf, pair_buf, sems = refs[-5:]
    copies = Copies(sems)
    core, _, _ = device_place()
    extra_copy = copies.start(extra_ref, extra_buf)
    others = [copies.start(pair_ref, pair_buf), copies.start(base_ref, base_buf)]
    extra_copy.wait()
    finish_states(plan, state_refs, extra_buf, state_buf)
    wait(others)
    half = plan.width // 2
    for first in range(0, plan.in_chunk, 4):
        places = range(first, first + 4)
        where = [quarter_of(plan, place) for place in places]
        products = [
            dot(pair_buf[side, place], state_buf[c, y, side, i], 1, 1)
            for place, (c, y, i) in zip(places, where)
            for side in range(2)
        ]
        for n, place in enumerate(places):
            term = plan.factor * (base_buf[place] + products[2 * n] + products[2 * n + 1])
            if len(out_refs) == 1:
                out_refs[0][place] = term
            else:
                out_refs[0][place] = jnp.where(core == 0, term[half:], term[:half])
                out_refs[1][place] = jnp.where(core == 0, term[:half], term[half:])


def maps_term(plan, states, extra, base, pair):
    width = plan.width
    square = (plan.in_chunk, width, width)
    in_halves = 2 * plan.height == width and plan.height % 8 == 0
    shapes = [(plan.in_chunk, width // 2, width)] * 2 if in_halves else [square]
    outs = call(
        functools.partial(term_kernel, plan),
        (*states, extra, base, pair),
        [jax.ShapeDtypeStruct(shape, F32) for shape in shapes],
        matmuls(plan, 2 * plan.in_chunk),
        state_scratch(plan) + [pltpu.VMEM(square, F32), pltpu.VMEM((2,) + square, BF16)],
        3,
        near=range(4),
        near_out=range(2),
        limit=SMALL_LIMIT,
        weight=LIGHT,
    )
    if in_halves:
        return outs
    core, _, _ = device_place()
    parts = outs[0].reshape(-1, 2, plan.height, width)
    return [
        lax.dynamic_index_in_dim(parts, turn, 1, keepdims=False) for turn in (1 - core, core)
    ]


def rows_kernel(plan, chunk, *refs):
    state_refs, extra_ref, row_refs, maps_ref = refs[:4], refs[4], refs[5:9], refs[9]
    refs = refs[10 + (3 if chunk else 0) :]
    out_refs, row_bufs, maps_buf = refs[:3], refs[3:7], refs[7]
    extra_buf, state_buf, out_bufs, sems = refs[8], refs[9], refs[10:13], refs[13]
    copies, width = Copies(sems), plan.width
    extra_copy = copies.start(extra_ref, extra_buf)
    started = load_chunk(plan, copies, chunk, 0, row_refs, maps_ref, row_bufs, maps_buf)
    causal = causal_mask(plan.tokens)
    extra_copy.wait()
    finish_states(plan, state_refs, extra_buf, state_buf)
    written = []
    size = plan.loads * max(1, 4 // plan.run)
    for first in range(0, plan.in_chunk, 4):
        places = range(first, first + 4)
        wait(started[:size])
        started = started[size:]
        queries, keys, values, grads = [
            [head_of(buf, place, width) for place in places] for buf in row_bufs
        ]
        where = [quarter_of(plan, place) for place in places]
        prefixes = [state_buf[c, y, 0, i] for c, y, i in where]
        suffixes = [state_buf[c, y, 1, i] for c, y, i in where]
        matrices = [maps_buf[place] for place in places]
        scores_gv = [
            jnp.where(causal, dot(grad, value, 1, 1), 0.0).astype(BF16)
            for grad, value in zip(grads, values)
        ]
        feats_query = [dot(x, matrix).astype(BF16) for x, matrix in zip(queries, matrices)]
        feats_key = [dot(x, matrix).astype(BF16) for x, matrix in zip(keys, matrices)]
        scores_ab = [
            jnp.where(causal, dot(left, right, 1, 1), 0.0).astype(BF16)
            for left, right in zip(feats_query, feats_key)
        ]
        grads_a = [
            (plan.factor * (dot(score, feat) + dot(grad, prefix, 1, 1))).astype(BF16)
            for score, feat, grad, prefix in zip(scores_gv, feats_key, grads, prefixes)
        ]
        grads_b = [
            (plan.factor * (dot(score, feat, 0, 0) + dot(value, suffix, 1, 1))).astype(BF16)
            for score, feat, value, suffix in zip(scores_gv, feats_query, values, suffixes)
        ]
        for n, place in enumerate(places):
            at = slice(place * width, (place + 1) * width)
            out_bufs[0][:, at] = dot(grads_a[n], matrices[n], 1, 1).astype(BF16)
            out_bufs[1][:, at] = dot(grads_b[n], matrices[n], 1, 1).astype(BF16)
            value_grad = dot(scores_ab[n], grads[n], 0, 0) + dot(feats_key[n], suffixes[n])
            out_bufs[2][:, at] = (plan.factor * value_grad).astype(BF16)
        for part in range(first, first + 4, min(4, plan.run)):
            count = min(4, plan.run)
            source = pl.ds(part * width, count * width)
            target = pl.ds(plan.head(chunk, part) * width, count * width)
            for buf, ref in zip(out_bufs, out_refs):
                written.append(copies.start(buf.at[:, source], ref.at[:, target]))
    wait(written)


def output_rows(plan, chunk, rows, maps, states, extra, done):
    shape = jax.ShapeDtypeStruct((plan.tokens, plan.heads * plan.width), BF16)
    narrow = [pltpu.VMEM((plan.tokens, plan.in_chunk * plan.width), BF16)] * 3
    return call(
        functools.partial(rows_kernel, plan, chunk),
        (*states, extra, *rows, maps, *done),
        [shape] * 3,
        matmuls(plan, 12 * plan.in_chunk),
        row_scratch(plan, plan.in_chunk) + state_scratch(plan) + narrow,
        chunk_copies(plan) + 3 * plan.in_chunk + 1,
        {10: 0, 11: 1, 12: 2} if done else None,
        near=range(4),
        limit=MIDDLE_LIMIT,
        weight=LIGHT,
    )


def swap_core(plan, state):
    return lax.ppermute(state, "context", [(i, i ^ 1) for i in range(plan.ranks)])


def swap_chip(plan, state):
    return lax.ppermute(state, "context", [(i, i ^ 2) for i in range(plan.ranks)])


def chain_swap(plan, state, hop):
    mirror = plan.groups - 1 - hop
    steps = [(i, i ^ 1) for i in range(plan.ranks)]
    for low in range(4):
        for left in (hop, mirror - 1):
            a, b = 4 * left + low, 4 * left + 4 + low
            steps[a], steps[b] = (a, b), (b, a)
    return lax.ppermute(state, "context", steps)


def chain_split(plan, state, hop):
    mirror = plan.groups - 1 - hop
    up = [(4 * hop + low, 4 * hop + 4 + low) for low in range(4)]
    down = [(4 * mirror + low, 4 * mirror - 4 + low) for low in range(4)]
    return lax.ppermute(state[0], "context", up), lax.ppermute(state[1], "context", down)


def plane_sums(plan, halves):
    _, chip, _ = device_place()
    replica = lax.axis_index("dp")
    ranks, copies, width = plan.ranks, plan.copies, plan.width
    totals = [half.reshape(copies, -1, 2, plan.height, width) for half in halves]

    def plane_part(target_replica, target_chip):
        parts = []
        for total in totals:
            some = lax.dynamic_index_in_dim(total, target_replica, 0, keepdims=False)
            parts.append(lax.dynamic_index_in_dim(some, target_chip, 1, keepdims=False))
        return jnp.concatenate(parts, axis=0)

    plane = plane_part(replica, chip)
    for turn in range(copies):
        for flip in range(2):
            if turn == 0 and flip == 0:
                continue
            steps = [
                (r * ranks + i, ((r + turn) % copies) * ranks + (i ^ (2 * flip)))
                for r in range(copies)
                for i in range(ranks)
            ]
            sent = plane_part((replica + turn) % copies, (chip + flip) % 2)
            plane = plane + lax.ppermute(sent, ("dp", "context"), steps)
    return plane


def group_sum(plan, plane):
    _, _, group = device_place()
    result = lax.dynamic_index_in_dim(plane, group, 0, keepdims=False)
    in_pairs = plan.groups & (plan.groups - 1) == 0
    for turn in range(1, plan.groups):

        def partner(place):
            return place ^ turn if in_pairs else (place + turn) % plan.groups

        steps = [(i, 4 * partner(i // 4) + i % 4) for i in range(plan.ranks)]
        sent = lax.dynamic_index_in_dim(plane, partner(group), 0, keepdims=False)
        result = result + lax.ppermute(sent, "context", steps)
    return result


def select_group(plan, got):
    _, _, group = device_place()
    prefix = suffix = jnp.zeros_like(got[0])
    for hop, state in enumerate(got):
        prefix = jnp.where(group == hop + 1, state, prefix)
        suffix = jnp.where(group == plan.groups - 2 - hop, state, suffix)
    return jnp.stack([prefix, suffix])


def scan_alone(plan, group_state):
    before = jnp.zeros_like(group_state)
    for hop in range(plan.groups - 1):
        if plan.groups % 2:
            up, down = chain_split(plan, before + group_state, hop)
            before = before + jnp.stack([up, down])
    return before


def after(value, *others):
    return lax.optimization_barrier((value, *others))[0]


def per_device(queries, key_rows, value_rows, out_grad, maps):
    tokens = queries.shape[1]
    heads, width, _ = maps.shape
    plan = Plan(heads, width, tokens, lax.axis_size("context"), lax.axis_size("dp"))
    rows = [x.reshape(tokens, heads * width) for x in (queries, key_rows, value_rows, out_grad)]
    core, chip, group = device_place()
    side = jnp.arange(2).reshape(2, 1, 1, 1)
    chunks, hops, last = range(plan.chunks), plan.groups - 1, plan.chunks - 1

    kept, from_core, given = [], [], []
    total, from_chip = [], []
    for chunk in chunks:
        matrices = after(maps, given[-1]) if chunk else maps
        sent, kept_here, given_here = block_states(plan, chunk, rows, matrices)
        kept.append(kept_here)
        from_core.append(swap_core(plan, sent))
        given_here = given_here + from_core[chunk][1]
        given.append(given_here)
        total.append(kept_here[0] + from_core[chunk][0])
        from_chip.append(swap_chip(plan, given_here))
    ready = [given[-1]] * last + [sent]
    terms = [inner(plan, chunk, rows, after(maps, ready[chunk])) for chunk in chunks]
    if last:
        from_chip[0] = after(from_chip[0], *terms[last])
    group_state = [total[chunk] + from_chip[chunk] for chunk in chunks]

    def for_other_chip(chunk, before):
        return before + jnp.where(side == chip, total[chunk], 0.0)

    def for_other_core(chunk, turn, state):
        return state + jnp.where(side == core, kept[chunk][turn], 0.0)

    before, got, down = [None] * plan.chunks, [[] for _ in chunks], [None] * plan.chunks
    if plan.groups % 2:
        for chunk in chunks:
            before[chunk] = scan_alone(plan, group_state[chunk])
            down[chunk] = swap_chip(plan, for_other_chip(chunk, before[chunk]))
    else:
        ahead = behind = given[last]
        for stage in range(hops + last):
            for chunk in chunks:
                hop = stage - chunk
                if chunk == 0 and hop == hops:
                    before[0] = select_group(plan, got[0])
                    ahead = for_other_chip(0, before[0])
                    down[0] = swap_chip(plan, ahead)
                if not 0 <= hop < hops:
                    continue
                send = jnp.where(group == hop, group_state[chunk][0], group_state[chunk][1])
                if hop:
                    send = send + got[chunk][-1]
                if chunk:
                    behind = send = after(send, ahead)
                elif last:
                    ahead = send = after(send, *(terms[0] if hop == 1 else (behind,)))
                got[chunk].append(chain_swap(plan, send, hop))
        if last:
            got[last][-1] = after(got[last][-1], for_other_core(0, 1, down[0]))
        before[last] = select_group(plan, got[last])
        down[last] = swap_chip(plan, for_other_chip(last, before[last]))

    halves, done = [], ()
    for chunk in chunks:
        states = [before[chunk] + jnp.where(side != chip, from_chip[chunk], 0.0), down[chunk]]
        for turn in range(2):
            if turn and done:
                states[1] = after(states[1], states[2], *done)
            states.append(swap_core(plan, for_other_core(chunk, turn, states[turn])))
        if halves:
            states[3] = after(states[3], *halves)
        for_mate, own = maps_term(plan, states, from_core[chunk], *terms[chunk])
        halves.append(own + swap_core(plan, for_mate))
        matrices = after(maps, for_mate)
        done = output_rows(plan, chunk, rows, matrices, states, from_core[chunk], done)
    plane = after(plane_sums(plan, halves), *done)
    query_grad, key_grad, value_grad = done
    maps_grad = group_sum(plan, plane) * plan.norm
    return (query_grad[None], key_grad[None], value_grad[None], maps_grad)


def solution(mesh):
    in_specs = (
        P("dp", "context", None),
        P("dp", "context", None),
        P("dp", "context", None),
        P("dp", "context", None),
        P(),
    )
    out_specs = (
        P("dp", "context", None),
        P("dp", "context", None),
        P("dp", "context", None),
        P(("dp", "context"), None),
    )
    return jax.shard_map(
        per_device, mesh=mesh, in_specs=in_specs, out_specs=out_specs, check_vma=False
    )
```

```python
import functools
import math

import jax
import jax.numpy as jnp
from jax import lax
from jax.experimental import pallas as pl
from jax.experimental.pallas import tpu as pltpu
from jax.sharding import PartitionSpec as P

F32 = jnp.float32
BF16 = jnp.bfloat16
VMEM_LIMIT = 57 * 1024 * 1024
MIDDLE_LIMIT = 52 * 1024 * 1024
STATES_LIMIT = 53 * 1024 * 1024
SMALL_LIMIT = 16 * 1024 * 1024
LIGHT = 0.01


class Plan:
    def __init__(self, heads, width, tokens, ranks, copies):
        self.heads, self.width, self.tokens = heads, width, tokens
        self.ranks, self.copies = ranks, copies
        self.groups = ranks // 4
        per_copy = heads // copies if heads % copies == 0 else 0
        self.chunks = 2 if per_copy and per_copy % 2 == 0 and self.groups % 2 == 0 else 1
        self.in_chunk = heads // self.chunks
        self.quarter = self.in_chunk // 4
        self.run = per_copy // self.chunks if self.chunks > 1 else self.in_chunk
        self.stride = per_copy if self.chunks > 1 else 0
        self.height = heads * width // (copies * ranks)
        self.factor = 1.0 / math.sqrt(width * tokens * ranks)
        self.norm = 1.0 / math.sqrt(copies * tokens * ranks)

    def head(self, chunk, place):
        return (place // self.run) * self.stride + chunk * self.run + place % self.run


def device_place():
    index = lax.axis_index("context")
    return index % 2, (index // 2) % 2, index // 4


def dot(left, right, left_dim=1, right_dim=0):
    return lax.dot_general(
        left, right, (((left_dim,), (right_dim,)), ((), ())), preferred_element_type=F32
    )


def call(body, operands, shapes, flops, scratch, copies, aliases=None, near=(), near_out=(), limit=VMEM_LIMIT, weight=1.0):
    moved = sum(x.size * x.dtype.itemsize for x in list(operands) + list(shapes))

    def specs(count, in_vmem):
        return [
            pl.BlockSpec(memory_space=pltpu.VMEM if n in in_vmem else pltpu.HBM)
            for n in range(count)
        ]

    return pl.pallas_call(
        body,
        out_shape=shapes,
        in_specs=specs(len(operands), near),
        out_specs=specs(len(shapes), near_out),
        scratch_shapes=list(scratch) + [pltpu.SemaphoreType.DMA((copies,))],
        input_output_aliases=aliases or {},
        compiler_params=pltpu.CompilerParams(vmem_limit_bytes=limit),
        cost_estimate=pl.CostEstimate(
            flops=int(flops * weight), bytes_accessed=int(moved * weight), transcendentals=0
        ),
    )(*operands)


class Copies:
    def __init__(self, sems):
        self.sems, self.used = sems, 0

    def start(self, source, target):
        copy = pltpu.make_async_copy(source, target, self.sems.at[self.used])
        self.used += 1
        copy.start()
        return copy


def wait(copies):
    for copy in copies:
        copy.wait()


def matmuls(plan, count):
    return 2 * count * plan.tokens * plan.width * plan.width


def load_chunk(plan, copies, chunk, offset, row_refs, maps_ref, row_bufs, maps_buf):
    width, started = plan.width, []
    for first in range(0, plan.in_chunk, plan.run):
        head = plan.head(chunk, first)
        source, target = pl.ds(head, plan.run), pl.ds(offset + first, plan.run)
        started.append(copies.start(maps_ref.at[source], maps_buf.at[target]))
        source = pl.ds(head * width, plan.run * width)
        target = pl.ds((offset + first) * width, plan.run * width)
        for ref, buf in zip(row_refs, row_bufs):
            started.append(copies.start(ref.at[:, source], buf.at[:, target]))
    return started


def chunk_copies(plan):
    return 5 * (plan.in_chunk // plan.run)


def row_scratch(plan, count):
    rows = [pltpu.VMEM((plan.tokens, count * plan.width), BF16)] * 4
    return rows + [pltpu.VMEM((count, plan.width, plan.width), BF16)]


def head_of(buf, place, width):
    return buf[:, place * width : (place + 1) * width]


def quarter_of(plan, place):
    core, chip, _ = device_place()
    low = place // plan.quarter
    core_turn = 1 - core if low % 2 else core
    chip_turn = 1 - chip if low // 2 else chip
    return core_turn, chip_turn, place % plan.quarter


def states_kernel(plan, chunk, *refs):
    row_refs, maps_ref, sent_ref, kept_ref, given_ref = refs[:4], refs[4], refs[5], refs[6], refs[7]
    row_bufs, maps_buf, out_buf, sems = refs[8:12], refs[12], refs[13], refs[14]
    copies, width = Copies(sems), plan.width
    started = load_chunk(plan, copies, chunk, 0, row_refs, maps_ref, row_bufs, maps_buf)
    q_buf, k_buf, v_buf, g_buf = row_bufs
    size = 5 * max(1, 4 // plan.run)
    for first in range(0, plan.in_chunk, 4):
        places = range(first, first + 4)
        wait(started[:size])
        started = started[size:]
        feats_key = [dot(head_of(k_buf, n, width), maps_buf[n]).astype(BF16) for n in places]
        feats_query = [dot(head_of(q_buf, n, width), maps_buf[n]).astype(BF16) for n in places]
        key_states = [
            dot(feat, head_of(v_buf, n, width), 0, 0) for feat, n in zip(feats_key, places)
        ]
        query_states = [
            dot(feat, head_of(g_buf, n, width), 0, 0) for feat, n in zip(feats_query, places)
        ]
        for place, key_state, query_state in zip(places, key_states, query_states):
            core_turn, chip_turn, i = quarter_of(plan, place)
            out_buf[core_turn, chip_turn, 0, i] = key_state
            out_buf[core_turn, chip_turn, 1, i] = query_state
    sent_ref[...] = out_buf[1]
    kept_ref[...] = out_buf[0]
    given_ref[...] = out_buf[0, 1]


def block_states(plan, chunk, rows, maps):
    shape = (2, 2, plan.quarter, plan.width, plan.width)
    state = jax.ShapeDtypeStruct(shape, F32)
    return call(
        functools.partial(states_kernel, plan, chunk),
        (*rows, maps),
        [state, state, jax.ShapeDtypeStruct(shape[1:], F32)],
        matmuls(plan, 4 * plan.in_chunk),
        row_scratch(plan, plan.in_chunk) + [pltpu.VMEM((2,) + shape, F32)],
        chunk_copies(plan),
        near_out=(0, 1, 2),
        limit=STATES_LIMIT,
    )


def causal_mask(tokens):
    row = lax.broadcasted_iota(jnp.int32, (tokens, tokens), 0)
    column = lax.broadcasted_iota(jnp.int32, (tokens, tokens), 1)
    return row >= column


def inner_kernel(plan, chunk, *refs):
    row_refs, maps_ref, base_ref, pair_ref = refs[:4], refs[4], refs[5], refs[6]
    row_bufs, maps_buf, base_buf, pair_buf, sems = refs[7:11], refs[11], refs[12], refs[13], refs[14]
    copies, width = Copies(sems), plan.width
    started = load_chunk(plan, copies, chunk, 0, row_refs, maps_ref, row_bufs, maps_buf)
    causal = causal_mask(plan.tokens)
    written = []
    size = 5 * max(1, 4 // plan.run)
    for first in range(0, plan.in_chunk, 4):
        places = range(first, first + 4)
        wait(started[:size])
        started = started[size:]
        queries, keys, values, grads = [
            [head_of(buf, n, width) for n in places] for buf in row_bufs
        ]
        scores = [
            jnp.where(causal, dot(grad, value, 1, 1), 0.0).astype(BF16)
            for grad, value in zip(grads, values)
        ]
        feats_query = [dot(x, maps_buf[n]).astype(BF16) for x, n in zip(queries, places)]
        feats_key = [dot(x, maps_buf[n]).astype(BF16) for x, n in zip(keys, places)]
        grads_a = [dot(s, feat).astype(BF16) for s, feat in zip(scores, feats_key)]
        grads_b = [dot(s, feat, 0, 0).astype(BF16) for s, feat in zip(scores, feats_query)]
        for n, place in enumerate(places):
            pair_buf[0, place] = dot(queries[n], grads[n], 0, 0).astype(BF16)
            pair_buf[1, place] = dot(keys[n], values[n], 0, 0).astype(BF16)
            base_buf[place] = dot(queries[n], grads_a[n], 0, 0) + dot(keys[n], grads_b[n], 0, 0)
        part = pl.ds(first, 4)
        written.append(copies.start(base_buf.at[part], base_ref.at[part]))
        written.append(copies.start(pair_buf.at[:, part], pair_ref.at[:, part]))
    wait(written)


def inner(plan, chunk, rows, maps):
    square = (plan.in_chunk, plan.width, plan.width)
    return call(
        functools.partial(inner_kernel, plan, chunk),
        (*rows, maps),
        [jax.ShapeDtypeStruct(square, F32), jax.ShapeDtypeStruct((2,) + square, BF16)],
        matmuls(plan, 9 * plan.in_chunk),
        row_scratch(plan, plan.in_chunk)
        + [pltpu.VMEM(square, F32), pltpu.VMEM((2,) + square, BF16)],
        chunk_copies(plan) + plan.in_chunk // 2,
    )


def finish_states(plan, state_refs, extra_buf, state_buf):
    core, _, _ = device_place()
    for core_turn in range(2):
        for chip_turn in range(2):
            for side in range(2):
                state = state_refs[2 * core_turn + chip_turn][side]
                if core_turn == 0:
                    wanted = core == 1 - side
                    state = state + jnp.where(wanted, extra_buf[chip_turn, side], 0.0)
                state_buf[core_turn, chip_turn, side] = state.astype(BF16)


def state_scratch(plan):
    shape = (2, 2, plan.quarter, plan.width, plan.width)
    return [pltpu.VMEM(shape, F32), pltpu.VMEM((2,) + shape, BF16)]


def term_kernel(plan, *refs):
    state_refs, extra_ref, base_ref, pair_ref = refs[:4], refs[4], refs[5], refs[6]
    out_refs = refs[7:-5]
    extra_buf, state_buf, base_buf, pair_buf, sems = refs[-5:]
    copies = Copies(sems)
    core, _, _ = device_place()
    extra_copy = copies.start(extra_ref, extra_buf)
    others = [copies.start(pair_ref, pair_buf), copies.start(base_ref, base_buf)]
    extra_copy.wait()
    finish_states(plan, state_refs, extra_buf, state_buf)
    wait(others)
    half = plan.width // 2
    for first in range(0, plan.in_chunk, 4):
        places = range(first, first + 4)
        where = [quarter_of(plan, place) for place in places]
        products = [
            dot(pair_buf[side, place], state_buf[c, y, side, i], 1, 1)
            for place, (c, y, i) in zip(places, where)
            for side in range(2)
        ]
        for n, place in enumerate(places):
            term = plan.factor * (base_buf[place] + products[2 * n] + products[2 * n + 1])
            if len(out_refs) == 1:
                out_refs[0][place] = term
            else:
                out_refs[0][place] = jnp.where(core == 0, term[half:], term[:half])
                out_refs[1][place] = jnp.where(core == 0, term[:half], term[half:])


def maps_term(plan, states, extra, base, pair):
    width = plan.width
    square = (plan.in_chunk, width, width)
    in_halves = 2 * plan.height == width and plan.height % 8 == 0
    shapes = [(plan.in_chunk, width // 2, width)] * 2 if in_halves else [square]
    outs = call(
        functools.partial(term_kernel, plan),
        (*states, extra, base, pair),
        [jax.ShapeDtypeStruct(shape, F32) for shape in shapes],
        matmuls(plan, 2 * plan.in_chunk),
        state_scratch(plan) + [pltpu.VMEM(square, F32), pltpu.VMEM((2,) + square, BF16)],
        3,
        near=range(4),
        near_out=range(2),
        limit=SMALL_LIMIT,
        weight=LIGHT,
    )
    if in_halves:
        return outs
    core, _, _ = device_place()
    parts = outs[0].reshape(-1, 2, plan.height, width)
    return [
        lax.dynamic_index_in_dim(parts, turn, 1, keepdims=False) for turn in (1 - core, core)
    ]


def rows_kernel(plan, chunk, *refs):
    state_refs, extra_ref, row_refs, maps_ref = refs[:4], refs[4], refs[5:9], refs[9]
    refs = refs[10 + (3 if chunk else 0) :]
    out_refs, row_bufs, maps_buf = refs[:3], refs[3:7], refs[7]
    extra_buf, state_buf, out_bufs, sems = refs[8], refs[9], refs[10:13], refs[13]
    copies, width = Copies(sems), plan.width
    extra_copy = copies.start(extra_ref, extra_buf)
    started = load_chunk(plan, copies, chunk, 0, row_refs, maps_ref, row_bufs, maps_buf)
    causal = causal_mask(plan.tokens)
    extra_copy.wait()
    finish_states(plan, state_refs, extra_buf, state_buf)
    written = []
    size = 5 * max(1, 4 // plan.run)
    for first in range(0, plan.in_chunk, 4):
        places = range(first, first + 4)
        wait(started[:size])
        started = started[size:]
        queries, keys, values, grads = [
            [head_of(buf, place, width) for place in places] for buf in row_bufs
        ]
        where = [quarter_of(plan, place) for place in places]
        prefixes = [state_buf[c, y, 0, i] for c, y, i in where]
        suffixes = [state_buf[c, y, 1, i] for c, y, i in where]
        matrices = [maps_buf[place] for place in places]
        scores_gv = [
            jnp.where(causal, dot(grad, value, 1, 1), 0.0).astype(BF16)
            for grad, value in zip(grads, values)
        ]
        feats_query = [dot(x, matrix).astype(BF16) for x, matrix in zip(queries, matrices)]
        feats_key = [dot(x, matrix).astype(BF16) for x, matrix in zip(keys, matrices)]
        scores_ab = [
            jnp.where(causal, dot(left, right, 1, 1), 0.0).astype(BF16)
            for left, right in zip(feats_query, feats_key)
        ]
        grads_a = [
            (plan.factor * (dot(score, feat) + dot(grad, prefix, 1, 1))).astype(BF16)
            for score, feat, grad, prefix in zip(scores_gv, feats_key, grads, prefixes)
        ]
        grads_b = [
            (plan.factor * (dot(score, feat, 0, 0) + dot(value, suffix, 1, 1))).astype(BF16)
            for score, feat, value, suffix in zip(scores_gv, feats_query, values, suffixes)
        ]
        for n, place in enumerate(places):
            at = slice(place * width, (place + 1) * width)
            out_bufs[0][:, at] = dot(grads_a[n], matrices[n], 1, 1).astype(BF16)
            out_bufs[1][:, at] = dot(grads_b[n], matrices[n], 1, 1).astype(BF16)
            value_grad = dot(scores_ab[n], grads[n], 0, 0) + dot(feats_key[n], suffixes[n])
            out_bufs[2][:, at] = (plan.factor * value_grad).astype(BF16)
        for part in range(first, first + 4, min(4, plan.run)):
            count = min(4, plan.run)
            source = pl.ds(part * width, count * width)
            target = pl.ds(plan.head(chunk, part) * width, count * width)
            for buf, ref in zip(out_bufs, out_refs):
                written.append(copies.start(buf.at[:, source], ref.at[:, target]))
    wait(written)


def output_rows(plan, chunk, rows, maps, states, extra, done):
    shape = jax.ShapeDtypeStruct((plan.tokens, plan.heads * plan.width), BF16)
    narrow = [pltpu.VMEM((plan.tokens, plan.in_chunk * plan.width), BF16)] * 3
    return call(
        functools.partial(rows_kernel, plan, chunk),
        (*states, extra, *rows, maps, *done),
        [shape] * 3,
        matmuls(plan, 12 * plan.in_chunk),
        row_scratch(plan, plan.in_chunk) + state_scratch(plan) + narrow,
        chunk_copies(plan) + 3 * plan.in_chunk + 1,
        {10: 0, 11: 1, 12: 2} if done else None,
        near=range(4),
        limit=MIDDLE_LIMIT,
        weight=LIGHT,
    )


def swap_core(plan, state):
    return lax.ppermute(state, "context", [(i, i ^ 1) for i in range(plan.ranks)])


def swap_chip(plan, state):
    return lax.ppermute(state, "context", [(i, i ^ 2) for i in range(plan.ranks)])


def chain_swap(plan, state, hop):
    mirror = plan.groups - 1 - hop
    steps = [(i, i ^ 1) for i in range(plan.ranks)]
    for low in range(4):
        for left in (hop, mirror - 1):
            a, b = 4 * left + low, 4 * left + 4 + low
            steps[a], steps[b] = (a, b), (b, a)
    return lax.ppermute(state, "context", steps)


def chain_split(plan, state, hop):
    mirror = plan.groups - 1 - hop
    up = [(4 * hop + low, 4 * hop + 4 + low) for low in range(4)]
    down = [(4 * mirror + low, 4 * mirror - 4 + low) for low in range(4)]
    return lax.ppermute(state[0], "context", up), lax.ppermute(state[1], "context", down)


def plane_sums(plan, halves):
    _, chip, _ = device_place()
    replica = lax.axis_index("dp")
    ranks, copies, width = plan.ranks, plan.copies, plan.width
    totals = [half.reshape(copies, -1, 2, plan.height, width) for half in halves]

    def plane_part(target_replica, target_chip):
        parts = []
        for total in totals:
            some = lax.dynamic_index_in_dim(total, target_replica, 0, keepdims=False)
            parts.append(lax.dynamic_index_in_dim(some, target_chip, 1, keepdims=False))
        return jnp.concatenate(parts, axis=0)

    plane = plane_part(replica, chip)
    for turn in range(copies):
        for flip in range(2):
            if turn == 0 and flip == 0:
                continue
            steps = [
                (r * ranks + i, ((r + turn) % copies) * ranks + (i ^ (2 * flip)))
                for r in range(copies)
                for i in range(ranks)
            ]
            sent = plane_part((replica + turn) % copies, (chip + flip) % 2)
            plane = plane + lax.ppermute(sent, ("dp", "context"), steps)
    return plane


def group_sum(plan, plane):
    _, _, group = device_place()
    result = lax.dynamic_index_in_dim(plane, group, 0, keepdims=False)
    in_pairs = plan.groups & (plan.groups - 1) == 0
    for turn in range(1, plan.groups):

        def partner(place):
            return place ^ turn if in_pairs else (place + turn) % plan.groups

        steps = [(i, 4 * partner(i // 4) + i % 4) for i in range(plan.ranks)]
        sent = lax.dynamic_index_in_dim(plane, partner(group), 0, keepdims=False)
        result = result + lax.ppermute(sent, "context", steps)
    return result


def select_group(plan, got):
    _, _, group = device_place()
    prefix = suffix = jnp.zeros_like(got[0])
    for hop, state in enumerate(got):
        prefix = jnp.where(group == hop + 1, state, prefix)
        suffix = jnp.where(group == plan.groups - 2 - hop, state, suffix)
    return jnp.stack([prefix, suffix])


def scan_alone(plan, group_state):
    before = jnp.zeros_like(group_state)
    for hop in range(plan.groups - 1):
        if plan.groups % 2:
            up, down = chain_split(plan, before + group_state, hop)
            before = before + jnp.stack([up, down])
    return before


def after(value, *others):
    return lax.optimization_barrier((value, *others))[0]


def per_device(queries, key_rows, value_rows, out_grad, maps):
    tokens = queries.shape[1]
    heads, width, _ = maps.shape
    plan = Plan(heads, width, tokens, lax.axis_size("context"), lax.axis_size("dp"))
    rows = [x.reshape(tokens, heads * width) for x in (queries, key_rows, value_rows, out_grad)]
    core, chip, group = device_place()
    side = jnp.arange(2).reshape(2, 1, 1, 1)
    chunks, hops, last = range(plan.chunks), plan.groups - 1, plan.chunks - 1

    kept, from_core, given = [], [], []
    total, from_chip = [], []
    for chunk in chunks:
        matrices = after(maps, given[-1]) if chunk else maps
        sent, kept_here, given_here = block_states(plan, chunk, rows, matrices)
        kept.append(kept_here)
        from_core.append(swap_core(plan, sent))
        given_here = given_here + from_core[chunk][1]
        given.append(given_here)
        total.append(kept_here[0] + from_core[chunk][0])
        from_chip.append(swap_chip(plan, given_here))
    ready = [given[-1]] * last + [sent]
    terms = [inner(plan, chunk, rows, after(maps, ready[chunk])) for chunk in chunks]
    if last:
        from_chip[0] = after(from_chip[0], *terms[last])
    group_state = [total[chunk] + from_chip[chunk] for chunk in chunks]

    def for_other_chip(chunk, before):
        return before + jnp.where(side == chip, total[chunk], 0.0)

    def for_other_core(chunk, turn, state):
        return state + jnp.where(side == core, kept[chunk][turn], 0.0)

    before, got, down = [None] * plan.chunks, [[] for _ in chunks], [None] * plan.chunks
    if plan.groups % 2:
        for chunk in chunks:
            before[chunk] = scan_alone(plan, group_state[chunk])
            down[chunk] = swap_chip(plan, for_other_chip(chunk, before[chunk]))
    else:
        ahead = behind = given[last]
        for stage in range(hops + last):
            for chunk in chunks:
                hop = stage - chunk
                if chunk == 0 and hop == hops:
                    before[0] = select_group(plan, got[0])
                    ahead = for_other_chip(0, before[0])
                    down[0] = swap_chip(plan, ahead)
                if not 0 <= hop < hops:
                    continue
                send = jnp.where(group == hop, group_state[chunk][0], group_state[chunk][1])
                if hop:
                    send = send + got[chunk][-1]
                if chunk:
                    behind = send = after(send, ahead)
                elif last:
                    ahead = send = after(send, *(terms[0] if hop == 1 else (behind,)))
                got[chunk].append(chain_swap(plan, send, hop))
        if last:
            got[last][-1] = after(got[last][-1], for_other_core(0, 1, down[0]))
        before[last] = select_group(plan, got[last])
        down[last] = swap_chip(plan, for_other_chip(last, before[last]))

    halves, done = [], ()
    for chunk in chunks:
        states = [before[chunk] + jnp.where(side != chip, from_chip[chunk], 0.0), down[chunk]]
        for turn in range(2):
            if turn and done:
                states[1] = after(states[1], states[2], *done)
            states.append(swap_core(plan, for_other_core(chunk, turn, states[turn])))
        if halves:
            states[3] = after(states[3], *halves)
        for_mate, own = maps_term(plan, states, from_core[chunk], *terms[chunk])
        halves.append(own + swap_core(plan, for_mate))
        matrices = after(maps, for_mate)
        done = output_rows(plan, chunk, rows, matrices, states, from_core[chunk], done)
    plane = after(plane_sums(plan, halves), *done)
    query_grad, key_grad, value_grad = done
    maps_grad = group_sum(plan, plane) * plan.norm
    return (query_grad[None], key_grad[None], value_grad[None], maps_grad)


def solution(mesh):
    in_specs = (
        P("dp", "context", None),
        P("dp", "context", None),
        P("dp", "context", None),
        P("dp", "context", None),
        P(),
    )
    out_specs = (
        P("dp", "context", None),
        P("dp", "context", None),
        P("dp", "context", None),
        P(("dp", "context"), None),
    )
    return jax.shard_map(
        per_device, mesh=mesh, in_specs=in_specs, out_specs=out_specs, check_vma=False
    )
```
